32 devices in a mesh: seq: 8 (over z, x), dp: 2 (over core), tensor: 2 (over y).
Axes of the slice: x: 2, y: 2, z: 4, core: 2. Of those that a mesh axis runs over, the one named last changes fastest.
Arguments:
- head_inputs: bfloat16 [2, 2560, 4096], P('dp', 'tensor', 'seq'), may hold values from -6 to 6
- b_proj: bfloat16 [2, 4096, 128], P('dp', 'seq'), may hold values from -0.59765625 to 0.59765625
- c_proj: bfloat16 [2, 4096, 128], P('dp', 'seq'), may hold values from -0.59765625 to 0.59765625
- dt_raw: float32 [2, 40, 4096], P('dp', 'tensor', 'seq'), may hold values from -2 to 0
- a_log: float32 [40], P('tensor'), as said below
- d_skip: float32 [40], P('tensor'), may hold values from 0.5 to 1.5
- w_out: bfloat16 [2560, 2560], P('tensor', 'dp'), may hold values from -0.125 to 0.125
- out_grad: bfloat16 [2, 2560, 4096], P('dp', 'tensor', 'seq'), may hold values from -6 to 6
Outputs:
- mixed: bfloat16 [2, 2560, 4096], P('dp', 'tensor', 'seq')
- grad_inputs: bfloat16 [2, 2560, 4096], P('dp', 'tensor', 'seq')
- grad_b: bfloat16 [2, 4096, 128], P('dp', 'seq')
- grad_c: bfloat16 [2, 4096, 128], P('dp', 'seq')
- grad_dt: float32 [2, 40, 4096], P('dp', 'tensor', 'seq')
- grad_alog: float32 [40], P('tensor')
- grad_skip: float32 [40], P('tensor')
- grad_w: bfloat16 [2560, 2560], P('tensor', ('seq', 'dp'))
The draws below stay inside these ranges and needn't reach their ends.
Inputs may be any that keep to these rules, and one draw needn't show every extreme that they name: exp(a_log) lies between 0.1 / 4096 and 0.1.
All inputs are finite; a program needn't handle non-finite values.
Results may differ from the reference program's by a relative error of at most 0.0049.
Values may be sent and summed in bfloat16 or wider, within the bound.
No kernel may reach another device: no remote copies, remote signals or barrier semaphores. Data moves between devices by JAX's collectives and lax.ppermute only.
A program may use at most 192 MiB of HBM per device.

```python
import math
import jax
import jax.numpy as jnp
from jax import lax

HEADS = 40
HEAD_DIM = 64
STATE = 128
SPAN = 256
D_OUT = 2560
SEQ_LEN = 4096
ROLLOUTS = 2
HP = 2560
N_DP = 2
N_TENSOR = 2


def draw_a_log(key, part):
    spots = jax.random.uniform(key, (HEADS,), jnp.float32)
    lower = math.log(0.1 / SEQ_LEN)
    upper = math.log(0.1)
    return lower + (upper - lower) * spots


def raised(result, rng, source, target, parts, factor):
    def block_of(axis_at):
        return (jnp.arange(result.shape[axis_at]) // (result.shape[axis_at] // parts)).reshape((-1,) + (1,) * (result.ndim - 1 - axis_at))

    one_side = jax.random.permutation(rng, parts)[block_of(target)]
    second = (block_of(target) + parts // 2) % parts
    return jnp.where((block_of(source) == one_side) | (block_of(source) == second), factor * result, result)


def shard_levels(own_key, extent, pieces, low, high):
    def one(axis_at, blocks):
        draws = jax.random.uniform(jax.random.fold_in(jax.random.fold_in(own_key, 6), axis_at), (blocks,), jnp.float32, low / len(pieces), high / len(pieces))
        return jnp.repeat(jnp.exp(draws), extent[axis_at] // blocks).reshape((-1,) + (1,) * (len(extent) - axis_at - 1))

    loudness = one(*pieces[0])
    for cut in pieces[1:]:
        loudness = loudness * one(*cut)
    return loudness


def scatter_about(rng, dims, deviation, most, shards=(), kind=jnp.bfloat16):
    gain = shard_levels(rng, dims, shards, -0.22, 0.18) if shards else 1.0
    values = jax.random.normal(rng, dims, jnp.float32) * deviation * gain
    return jnp.minimum(jnp.maximum(values, -most), most).astype(kind)


def noise_with(rng, extent, deviation, reach, pieces, heavy, held_as=jnp.bfloat16):
    values = deviation * jax.random.normal(rng, extent, jnp.float32)
    if pieces:
        values = values * shard_levels(rng, extent, pieces, -0.22, 0.18)
    return jnp.clip(raised(values, jax.random.fold_in(rng, 3), *heavy), -reach, reach).astype(held_as)


def setup_inputs(seed: int = 0) -> dict:
    keys = jax.random.split(jax.random.key(seed), 9)
    return {
        "head_inputs": scatter_about(keys[0], (ROLLOUTS, HP, SEQ_LEN), 1.0, 6.0, ((0, 2), (1, 2), (2, 8))),
        "b_proj": scatter_about(keys[1], (ROLLOUTS, SEQ_LEN, STATE), 0.1, 0.59765625, ((0, 2), (1, 8))),
        "c_proj": scatter_about(keys[2], (ROLLOUTS, SEQ_LEN, STATE), 0.1, 0.59765625, ((0, 2), (1, 8))),
        "dt_raw": jnp.clip(-2.0 + 2.0 * jax.random.uniform(keys[3], (ROLLOUTS, HEADS, SEQ_LEN), jnp.float32) ** shard_levels(keys[3], (ROLLOUTS, HEADS, SEQ_LEN), ((0, 2), (1, 2), (2, 8)), -0.2, 0.2), -2.0, 0.0),
        "a_log": draw_a_log(jax.random.fold_in(keys[8], 71), 0),
        "d_skip": jnp.clip(0.5 + 1.0 * jax.random.uniform(keys[5], (HEADS,), jnp.float32) ** shard_levels(keys[5], (HEADS,), ((0, 2),), -0.2, 0.2), 0.5, 1.5),
        "w_out": scatter_about(keys[6], (HP, D_OUT), D_OUT ** -0.5, 0.125, ((0, 2), (1, 2))),
        "out_grad": noise_with(keys[7], (ROLLOUTS, D_OUT, SEQ_LEN), 1.0, 6.0, ((0, 2), (1, 2), (2, 8)), (2, 1, 8, 2.0)),
    }


HIGH = lax.Precision.HIGHEST

def span_pass(carried, x_block, b_block, c_block, step_block, decay_rate):
    log_decay = step_block * decay_rate[:, None]
    cumulative = jnp.cumsum(log_decay, axis=1)
    block = cumulative.shape[1]
    indices = jnp.arange(block)
    causal = (indices[:, None] >= indices[None, :])[None, :, :]
    spread = cumulative[:, :, None] - cumulative[:, None, :]
    weights = jnp.where(causal, jnp.exp(jnp.where(causal, spread, 0.0)), 0.0)
    affinity = jnp.dot(c_block, b_block.T, precision=HIGH)
    scores = affinity[None, :, :] * weights * step_block[:, None, :]
    block_out = jnp.einsum('hps,hts->hpt', x_block, scores, precision=HIGH)
    block_out = block_out + jnp.exp(cumulative)[:, None, :] * jnp.einsum('hpn,tn->hpt', carried, c_block, precision=HIGH)
    tail_weight = jnp.exp(cumulative[:, -1:] - cumulative) * step_block
    updated = jnp.exp(cumulative[:, -1])[:, None, None] * carried
    updated = updated + jnp.einsum('hps,sn->hpn', x_block * tail_weight[:, None, :], b_block, precision=HIGH)
    return (updated, block_out)

def sweep(streams, b_rows, c_rows, dt_rows, alog_part, skip_part, state_in):
    head_count, head_width, length = streams.shape
    blocks = length // SPAN
    step_size = jax.nn.softplus(dt_rows)
    decay_rate = -jnp.exp(alog_part)
    x_blocks = streams.reshape(head_count, head_width, blocks, SPAN).transpose(2, 0, 1, 3)
    b_blocks = b_rows.reshape(blocks, SPAN, b_rows.shape[1])
    c_blocks = c_rows.reshape(blocks, SPAN, c_rows.shape[1])
    s_blocks = step_size.reshape(head_count, blocks, SPAN).transpose(1, 0, 2)

    def advance(carried, inputs):
        return span_pass(carried, inputs[0], inputs[1], inputs[2], inputs[3], decay_rate)
    state_end, outputs = lax.scan(advance, state_in, (x_blocks, b_blocks, c_blocks, s_blocks))
    mixed_f = outputs.transpose(1, 2, 0, 3).reshape(head_count, head_width, length)
    return (mixed_f + skip_part[:, None, None] * streams, state_end)

def reference(head_inputs, b_proj, c_proj, dt_raw, a_log, d_skip, w_out, out_grad):
    group_size = HEADS // N_TENSOR
    mixed_all = []
    gin_all = []
    gb_all = []
    gc_all = []
    gdt_all = []
    alog_total = jnp.zeros((HEADS,), jnp.float32)
    skip_total = jnp.zeros((HEADS,), jnp.float32)
    w_total = jnp.zeros((HP, D_OUT), jnp.float32)
    for rollout in range(N_DP):
        cotan_half = jnp.dot(w_out, out_grad[rollout], preferred_element_type=jnp.float32).astype(jnp.bfloat16)
        y_cotan = lax.optimization_barrier(cotan_half).astype(jnp.float32)
        b_rows = b_proj[rollout].astype(jnp.float32)
        c_rows = c_proj[rollout].astype(jnp.float32)
        streams = head_inputs[rollout].astype(jnp.float32).reshape(N_TENSOR, group_size, HEAD_DIM, SEQ_LEN)
        cotans = y_cotan.reshape(N_TENSOR, group_size, HEAD_DIM, SEQ_LEN)
        dt_groups = dt_raw[rollout].reshape(N_TENSOR, group_size, SEQ_LEN)
        alog_groups = a_log.reshape(N_TENSOR, group_size)
        skip_groups = d_skip.reshape(N_TENSOR, group_size)

        def per_group(running, inputs):
            start_state = jnp.zeros((group_size, HEAD_DIM, STATE), jnp.float32)

            def forward(xa, ba, ca, da, aa, sa):
                return sweep(xa, ba, ca, da, aa, sa, start_state)[0]
            primal, pullback = jax.vjp(forward, inputs[0], b_rows, c_rows, inputs[2], inputs[3], inputs[4])
            grads = pullback(inputs[1])
            return ((running[0] + grads[1], running[1] + grads[2]), (primal, grads[0], grads[3], grads[4], grads[5]))
        zero_rows = jnp.zeros((SEQ_LEN, STATE), jnp.float32)
        sums, results = lax.scan(per_group, (zero_rows, zero_rows), (streams, cotans, dt_groups, alog_groups, skip_groups))
        mixed_half = results[0].reshape(HP, SEQ_LEN).astype(jnp.bfloat16)
        mixed_all.append(mixed_half)
        gin_all.append(results[1].reshape(HP, SEQ_LEN).astype(jnp.bfloat16))
        gb_all.append(sums[0].astype(jnp.bfloat16))
        gc_all.append(sums[1].astype(jnp.bfloat16))
        gdt_all.append(results[2].reshape(HEADS, SEQ_LEN))
        alog_total = alog_total + results[3].reshape(HEADS)
        skip_total = skip_total + results[4].reshape(HEADS)
        w_total = w_total + lax.dot_general(mixed_half, out_grad[rollout], (((1,), (1,)), ((), ())), preferred_element_type=jnp.float32)
    return (jnp.stack(mixed_all), jnp.stack(gin_all), jnp.stack(gb_all), jnp.stack(gc_all), jnp.stack(gdt_all), alog_total, skip_total, w_total.astype(jnp.bfloat16))
```

```python
import jax
import jax.numpy as jnp
from jax import lax
from jax.sharding import PartitionSpec as P

HEAD_DIM = 64
HIGHEST = lax.Precision.HIGHEST
HIGH = lax.Precision.HIGH
F32 = jnp.float32
BF16 = jnp.bfloat16


def swap(value, axis, size, bit):
    return lax.ppermute(value, axis, [(i, i ^ bit) for i in range(size)])


def shifted(value, axis, size, step):
    pairs = [(i, i + step) for i in range(size) if 0 <= i + step < size]
    return lax.ppermute(value, axis, pairs)


def butterfly(value, axis, size):
    bit = 1
    while bit < size:
        value = value + swap(value, axis, size, bit)
        bit *= 2
    return value


def pack(state, total):
    heads, rows, lanes = state.shape
    high = lax.reduce_precision(total, 8, 7)
    middle = lax.reduce_precision(total - high, 8, 7)
    low = total - high - middle
    terms = jnp.stack([high, middle, low]).astype(BF16)
    extra = jnp.pad(terms, ((0, rows - 3), (0, lanes - heads)))
    return jnp.concatenate([state.astype(BF16), extra[None]], axis=0)


def unpack(payload):
    heads = payload.shape[0] - 1
    terms = payload[heads, :3, :heads].astype(F32)
    return payload[:heads].astype(F32), terms[0] + terms[1] + terms[2]


def decay(total):
    return jnp.exp(total)[:, None, None]


def pair_scan(local, total, n_seq, reverse):
    heads, width, lanes = local.shape
    place = lax.axis_index("seq")
    upper = lax.rem(place, 2) == 1
    late = jnp.logical_not(upper) if reverse else upper
    halves = local.reshape(heads, 2, width // 2, lanes)
    mine = jnp.where(upper, halves[:, 1], halves[:, 0])
    theirs = jnp.where(upper, halves[:, 0], halves[:, 1])
    other, other_total = unpack(swap(pack(theirs, total), "seq", n_seq, 1))
    mine = mine.astype(BF16).astype(F32)
    first = jnp.where(late, other, mine)
    second = jnp.where(late, mine, other)
    first_total = jnp.where(late, other_total, total)
    second_total = jnp.where(late, total, other_total)
    span = decay(second_total) * first + second
    span_total = first_total + second_total
    before, before_total = jnp.zeros_like(span), jnp.zeros_like(span_total)
    step = 2
    while step < n_seq:
        moved = shifted(pack(span, span_total), "seq", n_seq, -step if reverse else step)
        earlier, earlier_total = unpack(moved)
        before = decay(before_total) * earlier + before
        span = decay(span_total) * earlier + span
        before_total = before_total + earlier_total
        span_total = span_total + earlier_total
        step *= 2
    for_first = before.astype(BF16)
    for_second = (decay(first_total) * before + first).astype(BF16)
    keep = jnp.where(late, for_second, for_first)
    give = jnp.where(late, for_first, for_second)
    got = swap(give, "seq", n_seq, 1)
    low = jnp.where(upper, got, keep)
    high = jnp.where(upper, keep, got)
    return jnp.concatenate([low[:, None], high[:, None]], axis=1).reshape(heads * width, lanes)


def per_device(mesh, head_inputs, b_proj, c_proj, dt_raw, a_log, d_skip, w_out, out_grad):
    n_seq, n_dp, n_tensor = mesh.shape["seq"], mesh.shape["dp"], mesh.shape["tensor"]
    x, b, c, dt, g = head_inputs[0], b_proj[0], c_proj[0], dt_raw[0], out_grad[0]
    heads, length = dt.shape
    channels = heads * HEAD_DIM
    features = g.shape[0]
    all_features = features * n_tensor
    out_columns = all_features // (n_seq * n_dp)
    my_dp, my_tensor, my_seq = (lax.axis_index(a) for a in ("dp", "tensor", "seq"))

    def rows(values):
        spread = jnp.broadcast_to(values[:, None, :], (heads, HEAD_DIM, values.shape[1]))
        return spread.reshape(channels, values.shape[1])

    def head_sum(values):
        return jnp.sum(values.reshape(heads, HEAD_DIM, values.shape[1]), axis=1)

    if n_tensor == 2:
        g_other = swap(g, "tensor", 2, 1)
        g_full = jnp.where(
            my_tensor == 0, jnp.concatenate([g, g_other]), jnp.concatenate([g_other, g])
        )
    else:
        g_full = lax.all_gather(g, "tensor", axis=0, tiled=True)
    w_other = swap(w_out, "dp", 2, 1)
    w_full = jnp.where(
        my_dp == 0,
        jnp.concatenate([w_out, w_other], axis=1),
        jnp.concatenate([w_other, w_out], axis=1),
    )

    step_size = jax.nn.softplus(dt)
    rate = -jnp.exp(a_log)[:, None]
    log_decay = step_size * rate
    token = jnp.arange(length)
    causal = token[:, None] <= token[None, :]
    cumulative = jnp.dot(log_decay, causal.astype(F32), precision=HIGHEST)
    total = cumulative[:, -1]
    grown = rows(jnp.exp(cumulative))
    shrunk = rows(step_size * jnp.exp(-cumulative))
    skip = rows(d_skip[:, None])
    end_decay = rows(jnp.exp(total)[:, None])

    xs = x.astype(F32) * shrunk
    b32, c32 = b.astype(F32), c.astype(F32)
    gathered = jnp.dot(xs, b32, precision=HIGH)
    local_state = (end_decay * gathered).reshape(heads, HEAD_DIM, -1)
    state_in = pair_scan(local_state, total, n_seq, False)
    affinity_t = lax.dot_general(b, c, (((1,), (1,)), ((), ())), preferred_element_type=F32)
    affinity_t = jnp.where(causal, affinity_t, 0.0)
    inner = jnp.dot(xs, affinity_t, precision=HIGH) + lax.dot_general(
        state_in, c, (((1,), (1,)), ((), ())), preferred_element_type=F32
    )
    mixed = (grown * inner + skip * x.astype(F32)).astype(BF16)

    blocks = g_full.reshape(n_seq, n_dp, out_columns, length)
    g_mine = jnp.where(my_dp == 0, blocks[:, 0], blocks[:, 1])
    g_theirs = jnp.where(my_dp == 0, blocks[:, 1], blocks[:, 0])
    g_pair = jnp.concatenate([g_mine, swap(g_theirs, "dp", 2, 1)], axis=2)
    mixed_pair = jnp.concatenate([mixed, swap(mixed, "dp", 2, 1)], axis=1)

    def halving(mixed_rows, bits):
        n_bits = n_seq.bit_length() - 1
        operand = g_pair.reshape((2,) * n_bits + (out_columns, 2 * length))
        held = None
        left = list(range(n_bits))
        for bit in bits:
            mine = jnp.bitwise_and(my_seq >> bit, 1) == 1
            axis = left.index(n_bits - 1 - bit)
            left.remove(n_bits - 1 - bit)
            source = operand if held is None else held
            zero = lax.index_in_dim(source, 0, axis, keepdims=False)
            one = lax.index_in_dim(source, 1, axis, keepdims=False)
            keep, send = jnp.where(mine, one, zero), jnp.where(mine, zero, one)
            if held is None:
                product = lambda part: lax.dot_general(
                    part, mixed_rows, (((part.ndim - 1,), (1,)), ((), ())), preferred_element_type=F32
                )
                keep, send = product(keep), product(send)
            got = swap(send.astype(BF16), "seq", n_seq, 1 << bit)
            held = keep + got.astype(F32)
        return held

    n_bits = n_seq.bit_length() - 1
    half = channels // 2
    order_a = list(range(n_bits))
    order_b = [1, 0] + order_a[2:]
    grad_w = jnp.concatenate(
        [halving(mixed_pair[:half], order_a), halving(mixed_pair[half:], order_b)], axis=1
    ).T.astype(BF16)

    y_cotan = jnp.dot(w_full, g_full, preferred_element_type=F32)
    y_cotan = lax.optimization_barrier(y_cotan.astype(BF16))
    gs = y_cotan.astype(F32) * grown
    local_cotan = jnp.dot(gs, c32, precision=HIGH).reshape(heads, HEAD_DIM, -1)
    cotan_in = pair_scan(local_cotan, total, n_seq, True)
    cotan_end = (end_decay * cotan_in.astype(F32)).astype(BF16)
    outer = lax.dot_general(
        gs, affinity_t, (((1,), (1,)), ((), ())), precision=HIGH
    ) + lax.dot_general(cotan_end, b, (((1,), (1,)), ((), ())), preferred_element_type=F32)
    grad_inputs = (shrunk * outer + skip * y_cotan.astype(F32)).astype(BF16)
    across = lax.dot_general(xs, gs, (((0,), (0,)), ((), ())), precision=HIGH)
    across = jnp.where(causal, across, 0.0)
    grad_b = jnp.dot(across, c32, precision=HIGH) + lax.dot_general(
        xs.astype(BF16), cotan_end, (((0,), (0,)), ((), ())), preferred_element_type=F32
    )
    grad_c = lax.dot_general(
        across, b32, (((0,), (0,)), ((), ())), precision=HIGH
    ) + lax.dot_general(gs.astype(BF16), state_in, (((0,), (0,)), ((), ())), preferred_element_type=F32)
    grad_bc = jnp.concatenate([grad_b, grad_c], axis=1)
    if n_tensor == 2:
        grad_bc = lax.reduce_precision(grad_bc, 8, 7)
        grad_bc = grad_bc + swap(grad_bc.astype(BF16), "tensor", 2, 1).astype(F32)
    else:
        grad_bc = lax.psum(grad_bc, "tensor")
    grad_bc = grad_bc.astype(BF16)

    from_y = head_sum(gs.astype(F32) * inner)
    from_x = head_sum(xs.astype(F32) * outer)
    ends = cotan_end.astype(F32) * (gathered + state_in.astype(F32))
    from_end = jnp.sum(head_sum(ends), axis=1, keepdims=True)
    flow = jnp.dot(from_y - from_x, causal.astype(F32).T, precision=HIGHEST) + from_end
    grad_dt = (from_x / step_size + flow * rate) * jax.nn.sigmoid(dt)
    alog_part = jnp.sum(flow * log_decay, axis=1)
    skip_part = jnp.sum(head_sum(y_cotan.astype(F32) * x.astype(F32)), axis=1)
    small = jnp.stack([alog_part, skip_part])
    small = butterfly(butterfly(small, "dp", n_dp), "seq", n_seq)
    n_state = b.shape[1]
    return (
        mixed[None],
        grad_inputs[None],
        grad_bc[None, :, :n_state],
        grad_bc[None, :, n_state:],
        grad_dt[None],
        small[0],
        small[1],
        grad_w,
    )


def solution(mesh):
    in_specs = (
        P("dp", "tensor", "seq"),
        P("dp", "seq", None),
        P("dp", "seq", None),
        P("dp", "tensor", "seq"),
        P("tensor"),
        P("tensor"),
        P("tensor", "dp"),
        P("dp", "tensor", "seq"),
    )
    out_specs = (
        P("dp", "tensor", "seq"),
        P("dp", "tensor", "seq"),
        P("dp", "seq", None),
        P("dp", "seq", None),
        P("dp", "tensor", "seq"),
        P("tensor"),
        P("tensor"),
        P("tensor", ("seq", "dp")),
    )

    def whole(*args):
        return per_device(mesh, *args)

    return jax.shard_map(
        whole, mesh=mesh, in_specs=in_specs, out_specs=out_specs, check_vma=False
    )
```

```python
import functools

import jax
import jax.numpy as jnp
from jax import lax
from jax.experimental import pallas as pl
from jax.experimental.pallas import tpu as pltpu
from jax.sharding import PartitionSpec as P

HEAD_DIM = 64
F32 = jnp.float32
BF16 = jnp.bfloat16
NN = (((1,), (0,)), ((), ()))
NT = (((1,), (1,)), ((), ()))
TN = (((0,), (0,)), ((), ()))
VMEM_BYTES = 32 * 1024 * 1024
COST_SCALE = 20


def dot(a, b, dims=NN):
    return lax.dot_general(a, b, dims, preferred_element_type=F32)


def split(values):
    high = values.astype(BF16)
    return high, (values - high.astype(F32)).astype(BF16)


def dot_split(a, b, dims=NN):
    return dot(a[0], b[0], dims) + dot(a[1], b[0], dims) + dot(a[0], b[1], dims)


def part(pair, index):
    return pair[0][index], pair[1][index]


def running_sum(values, reverse=False):
    length = values.shape[1]
    lane = lax.broadcasted_iota(jnp.int32, values.shape, 1)
    step = 1
    while step < length:
        if reverse:
            moved = jnp.where(lane < length - step, pltpu.roll(values, length - step, 1), 0.0)
        else:
            moved = jnp.where(lane >= step, pltpu.roll(values, step, 1), 0.0)
        values = values + moved
        step *= 2
    return values


def softplus(values):
    return jnp.maximum(values, 0.0) + jnp.log(1.0 + jnp.exp(-jnp.abs(values)))


def causal_affinity(b, c):
    affinity = dot(b, c, NT)
    source = lax.broadcasted_iota(jnp.int32, affinity.shape, 0)
    later = lax.broadcasted_iota(jnp.int32, affinity.shape, 1)
    return jnp.where(source <= later, affinity, 0.0)


def as_column(row):
    square = jnp.broadcast_to(row, (row.shape[1], row.shape[1]))
    along = lax.broadcasted_iota(jnp.int32, square.shape, 0)
    across = lax.broadcasted_iota(jnp.int32, square.shape, 1)
    return jnp.sum(jnp.where(along == across, square, 0.0), axis=1, keepdims=True)


def per_head(values, heads):
    return values.reshape(heads, HEAD_DIM, values.shape[1])


def call(kernel, grid, in_specs, out_specs, out_shape, scratch=(), flops=0, prefetch=0):
    return pl.pallas_call(
        kernel,
        out_shape=out_shape,
        grid_spec=pltpu.PrefetchScalarGridSpec(
            num_scalar_prefetch=prefetch,
            grid=grid,
            in_specs=in_specs,
            out_specs=out_specs,
            scratch_shapes=list(scratch),
        ),
        compiler_params=pltpu.CompilerParams(
            vmem_limit_bytes=VMEM_BYTES, dimension_semantics=("arbitrary",) * len(grid)
        ),
        cost_estimate=pl.CostEstimate(flops=flops * COST_SCALE, bytes_accessed=4_000_000 * COST_SCALE, transcendentals=0),
    )


def whole(*shape):
    return pl.BlockSpec(shape, lambda i, *_: (0,) * len(shape))


def by_row(*shape):
    return pl.BlockSpec(shape, lambda i, *_: (i,) + (0,) * (len(shape) - 1))


ANY = pl.BlockSpec(memory_space=pl.ANY)


def decay_kernel(x_ref, b_ref, dt_ref, alog_ref, skip_ref, grown_ref, shrunk_ref, skips_ref, total_ref, gathered_ref):
    heads, length = dt_ref.shape
    group = x_ref.shape[0] // HEAD_DIM

    @pl.when(pl.program_id(0) == 0)
    def _():
        step_size = softplus(dt_ref[...])
        cumulative = running_sum(step_size * -jnp.exp(as_column(alog_ref[...])))
        grown = jnp.exp(cumulative)
        shrunk = step_size * jnp.exp(-cumulative)
        skips = jnp.broadcast_to(as_column(skip_ref[...]), (heads, length))
        for h in range(heads):
            grown_ref[h] = grown[h : h + 1]
            shrunk_ref[h] = shrunk[h : h + 1]
            skips_ref[h] = skips[h : h + 1]
        total_ref[...] = jnp.broadcast_to(cumulative[:, length - 1 :], total_ref.shape)

    shrunk = shrunk_ref[pl.ds(pl.program_id(0) * group, group)]
    xs = (per_head(x_ref[...].astype(F32), group) * shrunk).reshape(x_ref.shape)
    high, low = split(xs)
    gathered_ref[...] = dot(high, b_ref[...]) + dot(low, b_ref[...])


def inner_kernel(x_ref, b_ref, c_ref, shrunk_ref, after_ref, inner_ref, high_ref, low_ref):
    group = x_ref.shape[0] // HEAD_DIM
    half = x_ref.shape[1] // 2

    @pl.when(pl.program_id(0) == 0)
    def _():
        high_ref[...], low_ref[...] = split(causal_affinity(b_ref[...], c_ref[...]))

    xs = split((per_head(x_ref[...].astype(F32), group) * shrunk_ref[...]).reshape(x_ref.shape))
    affinity = (high_ref, low_ref)
    early = (slice(None), slice(0, half))
    late = (slice(None), slice(half, None))
    corner = (slice(0, half), slice(0, half))
    inner_ref[:, :half] = dot_split(part(xs, early), part(affinity, corner))
    inner_ref[:, half:] = dot_split(xs, part(affinity, late))


def mixed_kernel(inner_ref, state_ref, c_ref, x_ref, grown_ref, skips_ref, after_ref, mixed_ref):
    group = x_ref.shape[0] // HEAD_DIM
    inner = per_head(inner_ref[...] + dot(state_ref[...], c_ref[...], NT), group)
    x = per_head(x_ref[...].astype(F32), group)
    mixed = grown_ref[...] * inner + skips_ref[...] * x
    mixed_ref[...] = mixed.reshape(x_ref.shape).astype(BF16)


def cotan_first_kernel(flag_ref, mine_ref, other_ref, g_ref, after_ref, out_ref):
    @pl.when(flag_ref[0] == 1)
    def _():
        out_ref[...] = dot(mine_ref[...], g_ref[...])

    @pl.when(flag_ref[0] == 0)
    def _():
        out_ref[...] = dot(other_ref[...], g_ref[...])


def cotan_kernel(flag_ref, mine_ref, other_ref, g_ref, first_ref, c_ref, grown_ref, after_ref, cotan_ref, local_ref, sum_ref):
    @pl.when(flag_ref[0] == 0)
    def _():
        sum_ref[...] = first_ref[...] + dot(mine_ref[...], g_ref[...])

    @pl.when(flag_ref[0] == 1)
    def _():
        sum_ref[...] = first_ref[...] + dot(other_ref[...], g_ref[...])

    cotan = sum_ref[...].astype(BF16)
    cotan_ref[...] = cotan
    group = cotan.shape[0] // HEAD_DIM
    gs = (per_head(cotan.astype(F32), group) * grown_ref[...]).reshape(cotan.shape)
    high, low = split(gs)
    local_ref[...] = dot(high, c_ref[...]) + dot(low, c_ref[...])


def terms_kernel(pick_ref, g0_ref, g1_ref, m0_ref, m1_ref, after_ref, out_ref):
    high, _, low, columns, length = g0_ref.shape
    if columns % 16 == 0:
        flat = lambda ref: ref[...].reshape(high * low * columns, length)
        product = dot(flat(g0_ref), m0_ref[...], NT) + dot(flat(g1_ref), m1_ref[...], NT)
        out_ref[...] = product.reshape(out_ref.shape).astype(out_ref.dtype)
    else:
        for i in range(high):
            for j in range(low):
                product = dot(g0_ref[i, 0, j], m0_ref[...], NT) + dot(g1_ref[i, 0, j], m1_ref[...], NT)
                out_ref[i * low + j] = product.astype(out_ref.dtype)


def back_kernel(x_ref, cotan_ref, inner_ref, state_ref, b_ref, c_ref, grown_ref, shrunk_ref, after_ref,
                outer_ref, from_y_ref, grad_b_ref, grad_c_ref, high_ref, low_ref, across_ref):
    step = pl.program_id(0)
    group = x_ref.shape[0] // HEAD_DIM
    half = x_ref.shape[1] // 2

    @pl.when(step == 0)
    def _():
        high_ref[...], low_ref[...] = split(causal_affinity(b_ref[...], c_ref[...]))
        across_ref[...] = jnp.zeros_like(across_ref)
        grad_c_ref[...] = jnp.zeros_like(grad_c_ref)

    x = per_head(x_ref[...].astype(F32), group)
    xs = split((x * shrunk_ref[...]).reshape(x_ref.shape))
    gs_full = (per_head(cotan_ref[...].astype(F32), group) * grown_ref[...]).reshape(x_ref.shape)
    gs = split(gs_full)
    affinity = (high_ref, low_ref)
    late = (slice(None), slice(half, None))
    early = (slice(None), slice(0, half))
    top = (slice(0, half), slice(None))
    corner = (slice(half, None), slice(half, None))
    outer_ref[:, :half] = dot_split(gs, part(affinity, top), NT)
    outer_ref[:, half:] = dot_split(part(gs, late), part(affinity, corner), NT)
    across_ref[:half] += dot_split(part(xs, early), gs, TN)
    across_ref[half:, half:] += dot_split(part(xs, late), part(gs, late), TN)
    state = state_ref[...]
    grad_c_ref[...] += dot(gs[0], state, TN) + dot(gs[1], state, TN)
    inner = inner_ref[...] + dot(state, c_ref[...], NT)
    from_y_ref[...] = jnp.sum(per_head(gs_full * inner, group), axis=1, keepdims=True)

    @pl.when(step == pl.num_programs(0) - 1)
    def _():
        across = across_ref[...]
        source = lax.broadcasted_iota(jnp.int32, across.shape, 0)
        later = lax.broadcasted_iota(jnp.int32, across.shape, 1)
        high, low = split(jnp.where(source <= later, across, 0.0))
        grad_b_ref[...] = dot(high, c_ref[...]) + dot(low, c_ref[...])
        grad_c_ref[...] += dot(high, b_ref[...], TN) + dot(low, b_ref[...], TN)


def last_kernel(x_ref, cotan_ref, outer_ref, ends_ref, gathered_ref, state_ref, shrunk_ref, skips_ref,
                b_ref, dt_ref, alog_ref, from_y_ref, grad_b_ref, grad_c_ref, after_a_ref, after_b_ref,
                grad_inputs_ref, grad_dt_ref, small_ref, both_ref,
                from_x_s, from_end_s, from_skip_s, rows_x, rows_y, rows_skip, rows_end):
    step = pl.program_id(0)
    group = x_ref.shape[0] // HEAD_DIM
    heads, length = dt_ref.shape
    n_state = b_ref.shape[1]
    ends = ends_ref[...]
    outer = per_head(outer_ref[...] + dot(ends, b_ref[...], NT), group)
    x = per_head(x_ref[...].astype(F32), group)
    cotan = per_head(cotan_ref[...].astype(F32), group)
    xs = x * shrunk_ref[...]
    grad_inputs = shrunk_ref[...] * outer + skips_ref[...] * cotan
    grad_inputs_ref[...] = grad_inputs.reshape(x_ref.shape).astype(BF16)
    here = pl.ds(step * group, group)
    from_x_s[here] = jnp.sum(xs * outer, axis=1, keepdims=True)
    from_skip_s[here] = jnp.sum(x * cotan, axis=1, keepdims=True)
    moved = ends.astype(F32) * (gathered_ref[...] + state_ref[...].astype(F32))
    from_end_s[here] = jnp.sum(per_head(moved, group), axis=1, keepdims=True)
    high, low = split(xs.reshape(x_ref.shape))

    @pl.when(step == 0)
    def _():
        both_ref[:, :n_state] = grad_b_ref[...]
        both_ref[:, n_state:] = grad_c_ref[...]

    both_ref[:, :n_state] += dot(high, ends, TN) + dot(low, ends, TN)

    @pl.when(step == pl.num_programs(0) - 1)
    def _():
        for h in range(heads):
            rows_x[h : h + 1] = from_x_s[h]
            rows_y[h : h + 1] = from_y_ref[h]
            rows_skip[h : h + 1] = from_skip_s[h]
            rows_end[h : h + 1] = from_end_s[h]
        from_x = rows_x[...]
        from_end = jnp.sum(rows_end[...], axis=1, keepdims=True)
        flow = running_sum(rows_y[...] - from_x, reverse=True) + from_end
        dt = dt_ref[...]
        step_size = softplus(dt)
        rate = -jnp.exp(as_column(alog_ref[...]))
        grad_dt_ref[...] = (from_x / step_size + flow * rate) / (1.0 + jnp.exp(-dt))
        alog = jnp.sum(flow * step_size * rate, axis=1, keepdims=True)
        skip = jnp.sum(rows_skip[...], axis=1, keepdims=True)
        small_ref[0] = jnp.broadcast_to(alog, small_ref.shape[1:])
        small_ref[1] = jnp.broadcast_to(skip, small_ref.shape[1:])


def swap(value, axis, size, bit):
    return lax.ppermute(value, axis, [(i, i ^ bit) for i in range(size)])


def shifted(value, axis, size, step):
    pairs = [(i, i + step) for i in range(size) if 0 <= i + step < size]
    return lax.ppermute(value, axis, pairs)


def butterfly(value, axis, size):
    bit = 1
    while bit < size:
        value = value + swap(value, axis, size, bit)
        bit *= 2
    return value


def pack(state, total):
    heads, rows, lanes = state.shape
    high = lax.reduce_precision(total, 8, 7)
    middle = lax.reduce_precision(total - high, 8, 7)
    low = total - high - middle
    terms = jnp.stack([high, middle, low]).astype(BF16)
    extra = jnp.pad(terms, ((0, rows - 3), (0, lanes - heads)))
    return jnp.concatenate([state.astype(BF16), extra[None]], axis=0)


def unpack(payload):
    heads = payload.shape[0] - 1
    terms = payload[heads, :3, :heads].astype(F32)
    return payload[:heads].astype(F32), terms[0] + terms[1] + terms[2]


def decay(total):
    return jnp.exp(total)[:, None, None]


def pair_scan(local, total, n_seq, reverse, beside):
    works = []

    def traveling(payload, got):
        if len(works) in beside:
            work = beside[len(works)](payload)
            got, work = lax.optimization_barrier((got, work))
            works.append(work)
        return got

    heads, width, lanes = local.shape
    place = lax.axis_index("seq")
    upper = lax.rem(place, 2) == 1
    late = jnp.logical_not(upper) if reverse else upper
    halves = local.reshape(heads, 2, width // 2, lanes)
    mine = jnp.where(upper, halves[:, 1], halves[:, 0])
    theirs = jnp.where(upper, halves[:, 0], halves[:, 1])
    payload = pack(theirs, total)
    other, other_total = unpack(traveling(payload, swap(payload, "seq", n_seq, 1)))
    first = jnp.where(late, other, mine)
    second = jnp.where(late, mine, other)
    first_total = jnp.where(late, other_total, total)
    second_total = jnp.where(late, total, other_total)
    span = decay(second_total) * first + second
    span_total = first_total + second_total
    before, before_total = jnp.zeros_like(span), jnp.zeros_like(span_total)
    step = 2
    while step < n_seq:
        payload = pack(span, span_total)
        moved = shifted(payload, "seq", n_seq, -step if reverse else step)
        earlier, earlier_total = unpack(traveling(payload, moved))
        before = decay(before_total) * earlier + before
        span = decay(span_total) * earlier + span
        before_total = before_total + earlier_total
        span_total = span_total + earlier_total
        step *= 2
    for_first = before
    for_second = decay(first_total) * before + first
    if reverse:
        for_first = decay(first_total) * for_first
        for_second = decay(second_total) * for_second
    keep = jnp.where(late, for_second, for_first).astype(BF16)
    give = jnp.where(late, for_first, for_second).astype(BF16)
    got = swap(give, "seq", n_seq, 1)
    low = jnp.where(upper, got, keep)
    high = jnp.where(upper, keep, got)
    result = jnp.concatenate([low[:, None], high[:, None]], axis=1).reshape(heads * width, lanes)
    return works, result, give


def per_device(mesh, head_inputs, b_proj, c_proj, dt_raw, a_log, d_skip, w_out, out_grad):
    n_seq, n_dp, n_tensor = mesh.shape["seq"], mesh.shape["dp"], mesh.shape["tensor"]
    x, b, c, dt, g = head_inputs[0], b_proj[0], c_proj[0], dt_raw[0], out_grad[0]
    heads, length = dt.shape
    channels = heads * HEAD_DIM
    n_state = b.shape[1]
    features = g.shape[0] * n_tensor
    out_columns = features // (n_seq * n_dp)
    my_dp, my_tensor, my_seq = (lax.axis_index(a) for a in ("dp", "tensor", "seq"))
    group = 4 if heads % 4 == 0 else 1
    block = group * HEAD_DIM
    grid = (heads // group,)
    alog2, skip2 = a_log[None], d_skip[None]

    if n_tensor == 2:
        g_first, half_index = g, my_tensor
        g_second = swap(g, "tensor", 2, 1)
    else:
        g_all = lax.all_gather(g, "tensor", axis=0, tiled=True)
        g_first, g_second, half_index = g_all[: features // 2], g_all[features // 2 :], 0

    long = jax.ShapeDtypeStruct((heads, 1, length), F32)
    grown, shrunk, skips, totals, gathered = call(
        decay_kernel,
        grid,
        [by_row(block, length), whole(length, n_state), whole(heads, length), whole(1, heads), whole(1, heads)],
        [whole(heads, 1, length)] * 3 + [whole(heads, 128), by_row(block, n_state)],
        [long] * 3
        + [jax.ShapeDtypeStruct((heads, 128), F32), jax.ShapeDtypeStruct((channels, n_state), F32)],
        flops=4 * channels * length * n_state,
    )(x, b, dt, alog2, skip2)
    total = totals[:, 0]
    local_state = decay(total) * gathered.reshape(heads, HEAD_DIM, n_state)

    inners = lambda after: call(
        inner_kernel,
        grid,
        [by_row(block, length), whole(length, n_state), whole(length, n_state), by_row(group, 1, length), ANY],
        by_row(block, length),
        jax.ShapeDtypeStruct((channels, length), F32),
        [pltpu.VMEM((length, length), BF16)] * 2,
        flops=5 * channels * length * length,
    )(x, b, c, shrunk, after)

    w_other = swap(w_out, "dp", 2, 1)
    flag = (my_dp == half_index).astype(jnp.int32).reshape(1)
    half_features = features // 2
    wide_group = heads // 2 if heads % 2 == 0 else 1
    wide_block = wide_group * HEAD_DIM
    wide_grid = (heads // wide_group,)

    def weights(wanted):
        return pl.BlockSpec(
            (wide_block, half_features), lambda i, flag: (jnp.where(flag[0] == wanted, i, 0), 0)
        )

    first = lambda after: call(
        cotan_first_kernel,
        wide_grid,
        [weights(1), weights(0), whole(half_features, length), ANY],
        by_row(wide_block, length),
        jax.ShapeDtypeStruct((channels, length), F32),
        flops=2 * channels * half_features * length,
        prefetch=1,
    )(flag, w_out, w_other, g_first, after)
    cotans = lambda g_second, first, after: call(
        cotan_kernel,
        wide_grid,
        [weights(0), weights(1)]
        + [whole(half_features, length), by_row(wide_block, length), whole(length, n_state), by_row(wide_group, 1, length), ANY],
        [by_row(wide_block, length), by_row(wide_block, n_state)],
        [jax.ShapeDtypeStruct((channels, length), BF16), jax.ShapeDtypeStruct((channels, n_state), F32)],
        [pltpu.VMEM((wide_block, length), F32)],
        flops=2 * channels * length * (half_features + 2 * n_state),
        prefetch=1,
    )(flag, w_out, w_other, g_second, first, c, grown, after)

    beside = {0: inners, 1: first}
    (inner, first_sum), state_in, give = pair_scan(local_state, total, n_seq, False, beside)
    if n_tensor == 2:
        g_second, give = lax.optimization_barrier((g_second, give))
    y_cotan, local_cotan = cotans(g_second, first_sum, give)

    def mix(after):
        return call(
            mixed_kernel,
            grid,
            [by_row(block, length), by_row(block, n_state), whole(length, n_state), by_row(block, length)]
            + [by_row(group, 1, length)] * 2
            + [ANY],
            by_row(block, length),
            jax.ShapeDtypeStruct((channels, length), BF16),
            flops=2 * channels * length * n_state,
        )(inner, state_in, c, x, grown, skips, after)

    firsts = g_first.reshape(n_seq // 2, n_dp, out_columns, length)
    seconds = g_second.reshape(n_seq // 2, n_dp, out_columns, length)

    def chosen(place):
        pick = lambda blocks: lax.dynamic_index_in_dim(blocks, place, 1, keepdims=False)
        return jnp.concatenate([pick(firsts), pick(seconds)])

    g_mine = chosen(my_dp)
    g_other = swap(chosen(1 - my_dp), "dp", 2, 1)
    n_bits = n_seq.bit_length() - 1
    half = channels // 2

    def my_bit(bit):
        value = jnp.bitwise_and(my_seq >> bit, 1)
        return value ^ half_index if bit == n_bits - 1 else value

    def terms(mixed, mixed_other, stream, bit, value, dtype, after):
        low = 1 << bit
        high = n_seq // (2 * low)
        rows = pl.BlockSpec((half, length), lambda i, pick: (stream, 0))
        columns = pl.BlockSpec(
            (high, 1, low, out_columns, length), lambda i, pick: (0, pick[0], 0, 0, 0)
        )
        split_blocks = lambda blocks: blocks.reshape(high, 2, low, out_columns, length)
        return call(
            terms_kernel,
            (1,),
            [columns, columns, rows, rows, ANY],
            whole(n_seq // 2, out_columns, half),
            jax.ShapeDtypeStruct((n_seq // 2, out_columns, half), dtype),
            flops=n_seq * out_columns * half * 2 * length,
            prefetch=1,
        )(
            value.astype(jnp.int32).reshape(1),
            split_blocks(g_mine), split_blocks(g_other), mixed, mixed_other, after,
        )

    orders = [list(range(n_bits)), [1, 0] + list(range(2, n_bits))]
    held = {}

    def traded(after):
        mixed = mix(after)
        held["mixed"] = mixed, swap(mixed, "dp", 2, 1)
        return mixed

    def sending(after):
        held["sends"] = [
            terms(*held["mixed"], s, orders[s][0], 1 - my_bit(orders[s][0]), BF16, after) for s in (0, 1)
        ]
        return held["sends"]

    def keeping(after):
        sends = held["sends"]
        held["gots"] = [swap(sends[s], "seq", n_seq, 1 << orders[s][0]) for s in (0, 1)]
        held["keeps"] = [
            terms(*held["mixed"], s, orders[s][0], my_bit(orders[s][0]), F32, after) for s in (0, 1)
        ]
        held["back"] = back(after)
        return held["keeps"], held["back"]

    long = jax.ShapeDtypeStruct((heads, 1, length), F32)
    wide = jax.ShapeDtypeStruct((length, n_state), F32)
    back = lambda after: call(
        back_kernel,
        grid,
        [by_row(block, length)] * 3
        + [by_row(block, n_state), whole(length, n_state), whole(length, n_state)]
        + [by_row(group, 1, length)] * 2
        + [ANY],
        [by_row(block, length), by_row(group, 1, length), whole(length, n_state), whole(length, n_state)],
        [jax.ShapeDtypeStruct((channels, length), F32), long, wide, wide],
        [pltpu.VMEM((length, length), BF16)] * 2 + [pltpu.VMEM((length, length), F32)],
        flops=10 * channels * length * length,
    )(x, y_cotan, inner, state_in, b, c, grown, shrunk, after)
    _, cotan_end, _ = pair_scan(
        local_cotan.reshape(heads, HEAD_DIM, n_state), total, n_seq, True,
        {0: traded, 1: sending, 2: keeping},
    )
    mixed = held["mixed"][0]
    outer, from_y, grad_b, grad_c = held["back"]

    def halve(sums, left):
        axis = sorted(left, reverse=True).index(left[0])
        pick = lambda value: lax.dynamic_index_in_dim(sums, value, axis, keepdims=False)
        return pick(my_bit(left[0])), pick(1 - my_bit(left[0])).astype(BF16)

    streams = []
    for s in (0, 1):
        sums = held["keeps"][s] + held["gots"][s].astype(F32)
        sums = sums.reshape((2,) * (n_bits - 1) + (out_columns, half))
        streams.append(halve(sums, orders[s][1:]))
    grad_inputs, grad_dt, small, both = call(
        last_kernel,
        grid,
        [by_row(block, length)] * 3
        + [by_row(block, n_state)] * 3
        + [by_row(group, 1, length)] * 2
        + [whole(length, n_state), whole(heads, length), whole(1, heads), whole(heads, 1, length)]
        + [whole(length, n_state)] * 2
        + [ANY] * 2,
        [
            by_row(block, length),
            whole(heads, length),
            whole(2, heads, 128),
            whole(length, 2 * n_state),
        ],
        [
            jax.ShapeDtypeStruct((channels, length), BF16),
            jax.ShapeDtypeStruct((heads, length), F32),
            jax.ShapeDtypeStruct((2, heads, 128), F32),
            jax.ShapeDtypeStruct((length, 2 * n_state), F32),
        ],
        [
            pltpu.VMEM((heads, 1, length), F32),
            pltpu.VMEM((heads, 1, n_state), F32),
            pltpu.VMEM((heads, 1, length), F32),
            pltpu.VMEM((heads, length), F32),
            pltpu.VMEM((heads, length), F32),
            pltpu.VMEM((heads, length), F32),
            pltpu.VMEM((heads, n_state), F32),
        ],
        flops=6 * channels * length * n_state,
    )(
        x, y_cotan, outer, cotan_end, gathered, state_in, shrunk, skips,
        b, dt, alog2, from_y, grad_b, grad_c, streams[0][1], streams[1][1],
    )
    if n_tensor == 2:
        both_other = swap(both, "tensor", 2, 1)
    small = butterfly(small, "dp", n_dp)
    for done in range(1, n_bits):
        pairs = []
        for s in (0, 1):
            keep, send = streams[s]
            pairs.append(keep + swap(send, "seq", n_seq, 1 << orders[s][done]).astype(F32))
        if done + 1 < n_bits:
            streams = [halve(pairs[s], orders[s][done + 1 :]) for s in (0, 1)]
            if done + 2 == n_bits:
                small, streams = lax.optimization_barrier((small, streams))
    small = butterfly(small, "seq", n_seq)
    if n_tensor == 2:
        both_other, small = lax.optimization_barrier((both_other, small))
        both = both + both_other
    else:
        both = lax.psum(both, "tensor")
    both = both.astype(BF16)
    grad_w = jnp.concatenate(pairs, axis=1).T.astype(BF16)
    return (
        mixed[None],
        grad_inputs[None],
        both[None, :, :n_state],
        both[None, :, n_state:],
        grad_dt[None],
        small[0, :, 0],
        small[1, :, 0],
        grad_w,
    )


def solution(mesh):
    in_specs = (
        P("dp", "tensor", "seq"),
        P("dp", "seq", None),
        P("dp", "seq", None),
        P("dp", "tensor", "seq"),
        P("tensor"),
        P("tensor"),
        P("tensor", "dp"),
        P("dp", "tensor", "seq"),
    )
    out_specs = (
        P("dp", "tensor", "seq"),
        P("dp", "tensor", "seq"),
        P("dp", "seq", None),
        P("dp", "seq", None),
        P("dp", "tensor", "seq"),
        P("tensor"),
        P("tensor"),
        P("tensor", ("seq", "dp")),
    )
    return jax.shard_map(
        functools.partial(per_device, mesh),
        mesh=mesh,
        in_specs=in_specs,
        out_specs=out_specs,
        check_vma=False,
    )
```

```python
import functools

import jax
import jax.numpy as jnp
from jax import lax
from jax.experimental import pallas as pl
from jax.experimental.pallas import tpu as pltpu
from jax.sharding import PartitionSpec as P

HEAD_DIM = 64
F32 = jnp.float32
BF16 = jnp.bfloat16
NN = (((1,), (0,)), ((), ()))
NT = (((1,), (1,)), ((), ()))
TN = (((0,), (0,)), ((), ()))
VMEM_BYTES = 32 * 1024 * 1024
COST_SCALE = 20
FIRST_VMEM_BYTES = 32 * 1024 * 1024


def dot(a, b, dims=NN):
    return lax.dot_general(a, b, dims, preferred_element_type=F32)


def split(values):
    high = values.astype(BF16)
    return high, (values - high.astype(F32)).astype(BF16)


def dot_split(a, b, dims=NN):
    return dot(a[0], b[0], dims) + dot(a[1], b[0], dims) + dot(a[0], b[1], dims)


def part(pair, index):
    return pair[0][index], pair[1][index]


def running_sum(values, reverse=False):
    length = values.shape[1]
    lane = lax.broadcasted_iota(jnp.int32, values.shape, 1)
    step = 1
    while step < length:
        if reverse:
            moved = jnp.where(lane < length - step, pltpu.roll(values, length - step, 1), 0.0)
        else:
            moved = jnp.where(lane >= step, pltpu.roll(values, step, 1), 0.0)
        values = values + moved
        step *= 2
    return values


def softplus(values):
    return jnp.maximum(values, 0.0) + jnp.log(1.0 + jnp.exp(-jnp.abs(values)))


def causal_affinity(b, c):
    affinity = dot(b, c, NT)
    source = lax.broadcasted_iota(jnp.int32, affinity.shape, 0)
    later = lax.broadcasted_iota(jnp.int32, affinity.shape, 1)
    return jnp.where(source <= later, affinity, 0.0)


def as_column(row):
    square = jnp.broadcast_to(row, (row.shape[1], row.shape[1]))
    along = lax.broadcasted_iota(jnp.int32, square.shape, 0)
    across = lax.broadcasted_iota(jnp.int32, square.shape, 1)
    return jnp.sum(jnp.where(along == across, square, 0.0), axis=1, keepdims=True)


def per_head(values, heads):
    return values.reshape(heads, HEAD_DIM, values.shape[1])


def call(kernel, grid, in_specs, out_specs, out_shape, scratch=(), flops=0, prefetch=0, vmem=VMEM_BYTES):
    return pl.pallas_call(
        kernel,
        out_shape=out_shape,
        grid_spec=pltpu.PrefetchScalarGridSpec(
            num_scalar_prefetch=prefetch,
            grid=grid,
            in_specs=in_specs,
            out_specs=out_specs,
            scratch_shapes=list(scratch),
        ),
        compiler_params=pltpu.CompilerParams(
            vmem_limit_bytes=vmem, dimension_semantics=("arbitrary",) * len(grid)
        ),
        cost_estimate=pl.CostEstimate(flops=flops * COST_SCALE, bytes_accessed=4_000_000 * COST_SCALE, transcendentals=0),
    )


def whole(*shape):
    return pl.BlockSpec(shape, lambda i, *_: (0,) * len(shape))


def by_row(*shape):
    return pl.BlockSpec(shape, lambda i, *_: (i,) + (0,) * (len(shape) - 1))


ANY = pl.BlockSpec(memory_space=pl.ANY)


def decay_kernel(x_ref, b_ref, dt_ref, alog_ref, skip_ref, grown_ref, shrunk_ref, skips_ref, total_ref, gathered_ref):
    heads, length = dt_ref.shape
    group = x_ref.shape[0] // HEAD_DIM

    @pl.when(pl.program_id(0) == 0)
    def _():
        step_size = softplus(dt_ref[...])
        cumulative = running_sum(step_size * -jnp.exp(as_column(alog_ref[...])))
        grown = jnp.exp(cumulative)
        shrunk = step_size * jnp.exp(-cumulative)
        skips = jnp.broadcast_to(as_column(skip_ref[...]), (heads, length))
        for h in range(heads):
            grown_ref[h] = grown[h : h + 1]
            shrunk_ref[h] = shrunk[h : h + 1]
            skips_ref[h] = skips[h : h + 1]
        total_ref[...] = jnp.broadcast_to(cumulative[:, length - 1 :], total_ref.shape)

    shrunk = shrunk_ref[pl.ds(pl.program_id(0) * group, group)]
    xs = (per_head(x_ref[...].astype(F32), group) * shrunk).reshape(x_ref.shape)
    high, low = split(xs)
    gathered_ref[...] = dot(high, b_ref[...]) + dot(low, b_ref[...])


def inner_kernel(x_ref, b_ref, c_ref, shrunk_ref, after_ref, inner_ref, high_ref, low_ref):
    group = x_ref.shape[0] // HEAD_DIM
    half = x_ref.shape[1] // 2

    @pl.when(pl.program_id(0) == 0)
    def _():
        high_ref[...], low_ref[...] = split(causal_affinity(b_ref[...], c_ref[...]))

    xs = split((per_head(x_ref[...].astype(F32), group) * shrunk_ref[...]).reshape(x_ref.shape))
    affinity = (high_ref, low_ref)
    early = (slice(None), slice(0, half))
    late = (slice(None), slice(half, None))
    corner = (slice(0, half), slice(0, half))
    inner_ref[:, :half] = dot_split(part(xs, early), part(affinity, corner))
    inner_ref[:, half:] = dot_split(xs, part(affinity, late))


def mixed_kernel(inner_ref, state_ref, c_ref, x_ref, grown_ref, skips_ref, after_ref, mixed_ref):
    group = x_ref.shape[0] // HEAD_DIM
    inner = per_head(inner_ref[...] + dot(state_ref[...], c_ref[...], NT), group)
    x = per_head(x_ref[...].astype(F32), group)
    mixed = grown_ref[...] * inner + skips_ref[...] * x
    mixed_ref[...] = mixed.reshape(x_ref.shape).astype(BF16)


def cotan_first_kernel(flag_ref, mine_ref, other_ref, g_ref, after_ref, out_ref):
    @pl.when(flag_ref[0] == 1)
    def _():
        out_ref[...] = dot(mine_ref[...], g_ref[...])

    @pl.when(flag_ref[0] == 0)
    def _():
        out_ref[...] = dot(other_ref[...], g_ref[...])


def cotan_kernel(flag_ref, mine_ref, other_ref, g_ref, first_ref, c_ref, grown_ref, after_ref, cotan_ref, local_ref, sum_ref):
    @pl.when(flag_ref[0] == 0)
    def _():
        sum_ref[...] = first_ref[...] + dot(mine_ref[...], g_ref[...])

    @pl.when(flag_ref[0] == 1)
    def _():
        sum_ref[...] = first_ref[...] + dot(other_ref[...], g_ref[...])

    cotan = sum_ref[...].astype(BF16)
    cotan_ref[...] = cotan
    group = cotan.shape[0] // HEAD_DIM
    gs = (per_head(cotan.astype(F32), group) * grown_ref[...]).reshape(cotan.shape)
    high, low = split(gs)
    local_ref[...] = dot(high, c_ref[...]) + dot(low, c_ref[...])


def terms_kernel(pick_ref, g0_ref, g1_ref, m0_ref, m1_ref, after_ref, out_ref):
    high, _, low, columns, length = g0_ref.shape
    if columns % 16 == 0:
        flat = lambda ref: ref[...].reshape(high * low * columns, length)
        product = dot(flat(g0_ref), m0_ref[...], NT) + dot(flat(g1_ref), m1_ref[...], NT)
        out_ref[...] = product.reshape(out_ref.shape).astype(out_ref.dtype)
    else:
        for i in range(high):
            for j in range(low):
                product = dot(g0_ref[i, 0, j], m0_ref[...], NT) + dot(g1_ref[i, 0, j], m1_ref[...], NT)
                out_ref[i * low + j] = product.astype(out_ref.dtype)


def back_kernel(x_ref, cotan_ref, inner_ref, state_ref, b_ref, c_ref, grown_ref, shrunk_ref, after_ref,
                outer_ref, from_y_ref, grad_b_ref, grad_c_ref, high_ref, low_ref, across_ref):
    step = pl.program_id(0)
    group = x_ref.shape[0] // HEAD_DIM
    half = x_ref.shape[1] // 2

    @pl.when(step == 0)
    def _():
        high_ref[...], low_ref[...] = split(causal_affinity(b_ref[...], c_ref[...]))
        across_ref[...] = jnp.zeros_like(across_ref)
        grad_c_ref[...] = jnp.zeros_like(grad_c_ref)

    x = per_head(x_ref[...].astype(F32), group)
    xs = split((x * shrunk_ref[...]).reshape(x_ref.shape))
    gs_full = (per_head(cotan_ref[...].astype(F32), group) * grown_ref[...]).reshape(x_ref.shape)
    gs = split(gs_full)
    affinity = (high_ref, low_ref)
    late = (slice(None), slice(half, None))
    early = (slice(None), slice(0, half))
    top = (slice(0, half), slice(None))
    corner = (slice(half, None), slice(half, None))
    outer_ref[:, :half] = dot_split(gs, part(affinity, top), NT)
    outer_ref[:, half:] = dot_split(part(gs, late), part(affinity, corner), NT)
    across_ref[:half] += dot_split(part(xs, early), gs, TN)
    across_ref[half:, half:] += dot_split(part(xs, late), part(gs, late), TN)
    state = state_ref[...]
    grad_c_ref[...] += dot(gs[0], state, TN) + dot(gs[1], state, TN)
    inner = inner_ref[...] + dot(state, c_ref[...], NT)
    from_y_ref[...] = jnp.sum(per_head(gs_full * inner, group), axis=1, keepdims=True)

    @pl.when(step == pl.num_programs(0) - 1)
    def _():
        across = across_ref[...]
        source = lax.broadcasted_iota(jnp.int32, across.shape, 0)
        later = lax.broadcasted_iota(jnp.int32, across.shape, 1)
        high, low = split(jnp.where(source <= later, across, 0.0))
        grad_b_ref[...] = dot(high, c_ref[...]) + dot(low, c_ref[...])
        grad_c_ref[...] += dot(high, b_ref[...], TN) + dot(low, b_ref[...], TN)


def last_kernel(x_ref, cotan_ref, outer_ref, ends_ref, gathered_ref, state_ref, shrunk_ref, skips_ref,
                b_ref, dt_ref, alog_ref, from_y_ref, grad_b_ref, grad_c_ref, after_a_ref, after_b_ref,
                grad_inputs_ref, grad_dt_ref, small_ref, both_ref,
                from_x_s, from_end_s, from_skip_s, rows_x, rows_y, rows_skip, rows_end):
    step = pl.program_id(0)
    group = x_ref.shape[0] // HEAD_DIM
    heads, length = dt_ref.shape
    n_state = b_ref.shape[1]
    ends = ends_ref[...]
    outer = per_head(outer_ref[...] + dot(ends, b_ref[...], NT), group)
    x = per_head(x_ref[...].astype(F32), group)
    cotan = per_head(cotan_ref[...].astype(F32), group)
    xs = x * shrunk_ref[...]
    grad_inputs = shrunk_ref[...] * outer + skips_ref[...] * cotan
    grad_inputs_ref[...] = grad_inputs.reshape(x_ref.shape).astype(BF16)
    here = pl.ds(step * group, group)
    from_x_s[here] = jnp.sum(xs * outer, axis=1, keepdims=True)
    from_skip_s[here] = jnp.sum(x * cotan, axis=1, keepdims=True)
    moved = ends.astype(F32) * (gathered_ref[...] + state_ref[...].astype(F32))
    from_end_s[here] = jnp.sum(per_head(moved, group), axis=1, keepdims=True)
    high, low = split(xs.reshape(x_ref.shape))

    @pl.when(step == 0)
    def _():
        both_ref[:, :n_state] = grad_b_ref[...]
        both_ref[:, n_state:] = grad_c_ref[...]

    both_ref[:, :n_state] += dot(high, ends, TN) + dot(low, ends, TN)

    @pl.when(step == pl.num_programs(0) - 1)
    def _():
        for h in range(heads):
            rows_x[h : h + 1] = from_x_s[h]
            rows_y[h : h + 1] = from_y_ref[h]
            rows_skip[h : h + 1] = from_skip_s[h]
            rows_end[h : h + 1] = from_end_s[h]
        from_x = rows_x[...]
        from_end = jnp.sum(rows_end[...], axis=1, keepdims=True)
        flow = running_sum(rows_y[...] - from_x, reverse=True) + from_end
        dt = dt_ref[...]
        step_size = softplus(dt)
        rate = -jnp.exp(as_column(alog_ref[...]))
        grad_dt_ref[...] = (from_x / step_size + flow * rate) / (1.0 + jnp.exp(-dt))
        alog = jnp.sum(flow * step_size * rate, axis=1, keepdims=True)
        skip = jnp.sum(rows_skip[...], axis=1, keepdims=True)
        small_ref[0] = jnp.broadcast_to(alog, small_ref.shape[1:])
        small_ref[1] = jnp.broadcast_to(skip, small_ref.shape[1:])


def swap(value, axis, size, bit):
    return lax.ppermute(value, axis, [(i, i ^ bit) for i in range(size)])


def shifted(value, axis, size, step):
    pairs = [(i, i + step) for i in range(size) if 0 <= i + step < size]
    return lax.ppermute(value, axis, pairs)


def pack(state, total):
    heads, rows, lanes = state.shape
    high = lax.reduce_precision(total, 8, 7)
    middle = lax.reduce_precision(total - high, 8, 7)
    low = total - high - middle
    terms = jnp.stack([high, middle, low]).astype(BF16)
    extra = jnp.pad(terms, ((0, rows - 3), (0, lanes - heads)))
    return jnp.concatenate([state.astype(BF16), extra[None]], axis=0)


def unpack(payload):
    heads = payload.shape[0] - 1
    terms = payload[heads, :3, :heads].astype(F32)
    return payload[:heads].astype(F32), terms[0] + terms[1] + terms[2]


def decay(total):
    return jnp.exp(total)[:, None, None]


def pair_scan(local, total, n_seq, reverse, beside):
    works = []

    def traveling(payload, got):
        if len(works) in beside:
            work = beside[len(works)](payload)
            got, work = lax.optimization_barrier((got, work))
            works.append(work)
        return got

    heads, width, lanes = local.shape
    place = lax.axis_index("seq")
    upper = lax.rem(place, 2) == 1
    late = jnp.logical_not(upper) if reverse else upper
    halves = local.reshape(heads, 2, width // 2, lanes)
    mine = jnp.where(upper, halves[:, 1], halves[:, 0])
    theirs = jnp.where(upper, halves[:, 0], halves[:, 1])
    payload = pack(theirs, total)
    other, other_total = unpack(traveling(payload, swap(payload, "seq", n_seq, 1)))
    first = jnp.where(late, other, mine)
    second = jnp.where(late, mine, other)
    first_total = jnp.where(late, other_total, total)
    second_total = jnp.where(late, total, other_total)
    span = decay(second_total) * first + second
    span_total = first_total + second_total
    before, before_total = jnp.zeros_like(span), jnp.zeros_like(span_total)
    step = 2
    while step < n_seq:
        payload = pack(span, span_total)
        moved = shifted(payload, "seq", n_seq, -step if reverse else step)
        earlier, earlier_total = unpack(traveling(payload, moved))
        before = decay(before_total) * earlier + before
        span = decay(span_total) * earlier + span
        before_total = before_total + earlier_total
        span_total = span_total + earlier_total
        step *= 2
    for_first = before
    for_second = decay(first_total) * before + first
    if reverse:
        for_first = decay(first_total) * for_first
        for_second = decay(second_total) * for_second
    keep = jnp.where(late, for_second, for_first).astype(BF16)
    give = jnp.where(late, for_first, for_second).astype(BF16)
    got = swap(give, "seq", n_seq, 1)
    low = jnp.where(upper, got, keep)
    high = jnp.where(upper, keep, got)
    result = jnp.concatenate([low[:, None], high[:, None]], axis=1).reshape(heads * width, lanes)
    return works, result, give


def per_device(mesh, head_inputs, b_proj, c_proj, dt_raw, a_log, d_skip, w_out, out_grad):
    n_seq, n_dp, n_tensor = mesh.shape["seq"], mesh.shape["dp"], mesh.shape["tensor"]
    x, b, c, dt, g = head_inputs[0], b_proj[0], c_proj[0], dt_raw[0], out_grad[0]
    heads, length = dt.shape
    channels = heads * HEAD_DIM
    n_state = b.shape[1]
    features = g.shape[0] * n_tensor
    out_columns = features // (n_seq * n_dp)
    my_dp, my_tensor, my_seq = (lax.axis_index(a) for a in ("dp", "tensor", "seq"))
    group = 4 if heads % 4 == 0 else 1
    block = group * HEAD_DIM
    grid = (heads // group,)
    alog2, skip2 = a_log[None], d_skip[None]

    if n_tensor == 2:
        g_first, half_index = g, my_tensor
        g_second = swap(g, "tensor", 2, 1)
    else:
        g_all = lax.all_gather(g, "tensor", axis=0, tiled=True)
        g_first, g_second, half_index = g_all[: features // 2], g_all[features // 2 :], 0

    long = jax.ShapeDtypeStruct((heads, 1, length), F32)
    grown, shrunk, skips, totals, gathered = call(
        decay_kernel,
        grid,
        [by_row(block, length), whole(length, n_state), whole(heads, length), whole(1, heads), whole(1, heads)],
        [whole(heads, 1, length)] * 3 + [whole(heads, 128), by_row(block, n_state)],
        [long] * 3
        + [jax.ShapeDtypeStruct((heads, 128), F32), jax.ShapeDtypeStruct((channels, n_state), F32)],
        flops=4 * channels * length * n_state,
        vmem=FIRST_VMEM_BYTES,
    )(x, b, dt, alog2, skip2)
    total = totals[:, 0]
    local_state = decay(total) * gathered.reshape(heads, HEAD_DIM, n_state)

    inners = lambda after: call(
        inner_kernel,
        grid,
        [by_row(block, length), whole(length, n_state), whole(length, n_state), by_row(group, 1, length), ANY],
        by_row(block, length),
        jax.ShapeDtypeStruct((channels, length), F32),
        [pltpu.VMEM((length, length), BF16)] * 2,
        flops=5 * channels * length * length,
    )(x, b, c, shrunk, after)

    w_other = swap(w_out, "dp", 2, 1)
    flag = (my_dp == half_index).astype(jnp.int32).reshape(1)
    half_features = features // 2
    wide_group = heads // 2 if heads % 2 == 0 else 1
    wide_block = wide_group * HEAD_DIM
    wide_grid = (heads // wide_group,)

    def weights(wanted):
        return pl.BlockSpec(
            (wide_block, half_features), lambda i, flag: (jnp.where(flag[0] == wanted, i, 0), 0)
        )

    first = lambda after: call(
        cotan_first_kernel,
        wide_grid,
        [weights(1), weights(0), whole(half_features, length), ANY],
        by_row(wide_block, length),
        jax.ShapeDtypeStruct((channels, length), F32),
        flops=2 * channels * half_features * length,
        prefetch=1,
    )(flag, w_out, w_other, g_first, after)
    cotans = lambda g_second, first, after: call(
        cotan_kernel,
        wide_grid,
        [weights(0), weights(1)]
        + [whole(half_features, length), by_row(wide_block, length), whole(length, n_state), by_row(wide_group, 1, length), ANY],
        [by_row(wide_block, length), by_row(wide_block, n_state)],
        [jax.ShapeDtypeStruct((channels, length), BF16), jax.ShapeDtypeStruct((channels, n_state), F32)],
        [pltpu.VMEM((wide_block, length), F32)],
        flops=2 * channels * length * (half_features + 2 * n_state),
        prefetch=1,
    )(flag, w_out, w_other, g_second, first, c, grown, after)

    beside = {0: inners, 1: first}
    (inner, first_sum), state_in, give = pair_scan(local_state, total, n_seq, False, beside)
    if n_tensor == 2:
        g_second, give = lax.optimization_barrier((g_second, give))
    y_cotan, local_cotan = cotans(g_second, first_sum, give)

    def mix(after):
        return call(
            mixed_kernel,
            grid,
            [by_row(block, length), by_row(block, n_state), whole(length, n_state), by_row(block, length)]
            + [by_row(group, 1, length)] * 2
            + [ANY],
            by_row(block, length),
            jax.ShapeDtypeStruct((channels, length), BF16),
            flops=2 * channels * length * n_state,
        )(inner, state_in, c, x, grown, skips, after)

    firsts = g_first.reshape(n_seq // 2, n_dp, out_columns, length)
    seconds = g_second.reshape(n_seq // 2, n_dp, out_columns, length)

    def chosen(place):
        pick = lambda blocks: lax.dynamic_index_in_dim(blocks, place, 1, keepdims=False)
        return jnp.concatenate([pick(firsts), pick(seconds)])

    g_mine = chosen(my_dp)
    g_other = swap(chosen(1 - my_dp), "dp", 2, 1)
    n_bits = n_seq.bit_length() - 1
    half = channels // 2

    def my_bit(bit):
        value = jnp.bitwise_and(my_seq >> bit, 1)
        return value ^ half_index if bit == n_bits - 1 else value

    def terms(mixed, mixed_other, stream, bit, value, dtype, after):
        low = 1 << bit
        high = n_seq // (2 * low)
        rows = pl.BlockSpec((half, length), lambda i, pick: (stream, 0))
        columns = pl.BlockSpec(
            (high, 1, low, out_columns, length), lambda i, pick: (0, pick[0], 0, 0, 0)
        )
        split_blocks = lambda blocks: blocks.reshape(high, 2, low, out_columns, length)
        return call(
            terms_kernel,
            (1,),
            [columns, columns, rows, rows, ANY],
            whole(n_seq // 2, out_columns, half),
            jax.ShapeDtypeStruct((n_seq // 2, out_columns, half), dtype),
            flops=n_seq * out_columns * half * 2 * length,
            prefetch=1,
        )(
            value.astype(jnp.int32).reshape(1),
            split_blocks(g_mine), split_blocks(g_other), mixed, mixed_other, after,
        )

    orders = [list(range(n_bits)), [1, 0] + list(range(2, n_bits))]
    held = {}

    def traded(after):
        mixed = mix(after)
        held["mixed"] = mixed, swap(mixed, "dp", 2, 1)
        return mixed

    def sending(after):
        held["sends"] = [
            terms(*held["mixed"], s, orders[s][0], 1 - my_bit(orders[s][0]), BF16, after) for s in (0, 1)
        ]
        return held["sends"]

    def keeping(after):
        sends = held["sends"]
        held["gots"] = [swap(sends[s], "seq", n_seq, 1 << orders[s][0]) for s in (0, 1)]
        held["keeps"] = [
            terms(*held["mixed"], s, orders[s][0], my_bit(orders[s][0]), F32, after) for s in (0, 1)
        ]
        held["back"] = back(after)
        return held["keeps"], held["back"], held["gots"]

    long = jax.ShapeDtypeStruct((heads, 1, length), F32)
    wide = jax.ShapeDtypeStruct((length, n_state), F32)
    back = lambda after: call(
        back_kernel,
        grid,
        [by_row(block, length)] * 3
        + [by_row(block, n_state), whole(length, n_state), whole(length, n_state)]
        + [by_row(group, 1, length)] * 2
        + [ANY],
        [by_row(block, length), by_row(group, 1, length), whole(length, n_state), whole(length, n_state)],
        [jax.ShapeDtypeStruct((channels, length), F32), long, wide, wide],
        [pltpu.VMEM((length, length), BF16)] * 2 + [pltpu.VMEM((length, length), F32)],
        flops=10 * channels * length * length,
    )(x, y_cotan, inner, state_in, b, c, grown, shrunk, after)
    works, cotan_end, _ = pair_scan(
        local_cotan.reshape(heads, HEAD_DIM, n_state), total, n_seq, True,
        {0: traded, 1: sending, 2: keeping},
    )
    mixed = held["mixed"][0]
    keeps, (outer, from_y, grad_b, grad_c), gots = works[2]

    def halve(sums, left):
        axis = sorted(left, reverse=True).index(left[0])
        pick = lambda value: lax.dynamic_index_in_dim(sums, value, axis, keepdims=False)
        return pick(my_bit(left[0])), pick(1 - my_bit(left[0])).astype(BF16)

    streams = []
    for s in (0, 1):
        sums = keeps[s] + gots[s].astype(F32)
        sums = sums.reshape((2,) * (n_bits - 1) + (out_columns, half))
        streams.append(halve(sums, orders[s][1:]))
    grad_inputs, grad_dt, small, both = call(
        last_kernel,
        grid,
        [by_row(block, length)] * 3
        + [by_row(block, n_state)] * 3
        + [by_row(group, 1, length)] * 2
        + [whole(length, n_state), whole(heads, length), whole(1, heads), whole(heads, 1, length)]
        + [whole(length, n_state)] * 2
        + [ANY] * 2,
        [
            by_row(block, length),
            whole(heads, length),
            whole(2, heads, 128),
            whole(length, 2 * n_state),
        ],
        [
            jax.ShapeDtypeStruct((channels, length), BF16),
            jax.ShapeDtypeStruct((heads, length), F32),
            jax.ShapeDtypeStruct((2, heads, 128), F32),
            jax.ShapeDtypeStruct((length, 2 * n_state), F32),
        ],
        [
            pltpu.VMEM((heads, 1, length), F32),
            pltpu.VMEM((heads, 1, n_state), F32),
            pltpu.VMEM((heads, 1, length), F32),
            pltpu.VMEM((heads, length), F32),
            pltpu.VMEM((heads, length), F32),
            pltpu.VMEM((heads, length), F32),
            pltpu.VMEM((heads, n_state), F32),
        ],
        flops=6 * channels * length * n_state,
    )(
        x, y_cotan, outer, cotan_end, gathered, state_in, shrunk, skips,
        b, dt, alog2, from_y, grad_b, grad_c, streams[0][1], streams[1][1],
    )
    if n_tensor == 2:
        both_other = swap(both, "tensor", 2, 1)
    small = small + swap(small, "dp", 2, 1)
    for done in range(1, n_bits):
        gots = [swap(streams[s][1], "seq", n_seq, 1 << orders[s][done]) for s in (0, 1)]
        if done == 1:
            gots, both, small = lax.optimization_barrier((gots, both, small))
        pairs = [streams[s][0] + gots[s].astype(F32) for s in (0, 1)]
        if done + 1 < n_bits:
            streams = [halve(pairs[s], orders[s][done + 1 :]) for s in (0, 1)]
            if done + 2 == n_bits:
                small, _ = lax.optimization_barrier((small, [stream[1] for stream in streams]))
    small = lax.all_to_all(jnp.broadcast_to(small, (n_seq,) + small.shape), "seq", 0, 0)
    small = jnp.sum(small[:, :, :, 0], axis=0)
    if n_tensor == 2:
        both_other, small = lax.optimization_barrier((both_other, small))
        both = both + both_other
    else:
        both = lax.psum(both, "tensor")
    both = both.astype(BF16)
    grad_w = jnp.concatenate(pairs, axis=1).T.astype(BF16)
    return (
        mixed[None],
        grad_inputs[None],
        both[None, :, :n_state],
        both[None, :, n_state:],
        grad_dt[None],
        small[0],
        small[1],
        grad_w,
    )


def solution(mesh):
    in_specs = (
        P("dp", "tensor", "seq"),
        P("dp", "seq", None),
        P("dp", "seq", None),
        P("dp", "tensor", "seq"),
        P("tensor"),
        P("tensor"),
        P("tensor", "dp"),
        P("dp", "tensor", "seq"),
    )
    out_specs = (
        P("dp", "tensor", "seq"),
        P("dp", "tensor", "seq"),
        P("dp", "seq", None),
        P("dp", "seq", None),
        P("dp", "tensor", "seq"),
        P("tensor"),
        P("tensor"),
        P("tensor", ("seq", "dp")),
    )
    return jax.shard_map(
        functools.partial(per_device, mesh),
        mesh=mesh,
        in_specs=in_specs,
        out_specs=out_specs,
        check_vma=False,
    )
```

```python
import functools

import jax
import jax.numpy as jnp
from jax import lax
from jax.experimental import pallas as pl
from jax.experimental.pallas import tpu as pltpu
from jax.sharding import PartitionSpec as P

HEAD_DIM = 64
F32 = jnp.float32
BF16 = jnp.bfloat16
NN = (((1,), (0,)), ((), ()))
NT = (((1,), (1,)), ((), ()))
TN = (((0,), (0,)), ((), ()))
VMEM_BYTES = 32 * 1024 * 1024
COST_SCALE = 20
FIRST_VMEM_BYTES = 58 * 1024 * 1024


def dot(a, b, dims=NN):
    return lax.dot_general(a, b, dims, preferred_element_type=F32)


def split(values):
    high = values.astype(BF16)
    return high, (values - high.astype(F32)).astype(BF16)


def dot_split(a, b, dims=NN):
    return dot(a[0], b[0], dims) + dot(a[1], b[0], dims) + dot(a[0], b[1], dims)


def part(pair, index):
    return pair[0][index], pair[1][index]


def running_sum(values, reverse=False):
    length = values.shape[1]
    lane = lax.broadcasted_iota(jnp.int32, values.shape, 1)
    step = 1
    while step < length:
        if reverse:
            moved = jnp.where(lane < length - step, pltpu.roll(values, length - step, 1), 0.0)
        else:
            moved = jnp.where(lane >= step, pltpu.roll(values, step, 1), 0.0)
        values = values + moved
        step *= 2
    return values


def softplus(values):
    return jnp.maximum(values, 0.0) + jnp.log(1.0 + jnp.exp(-jnp.abs(values)))


def causal_affinity(b, c):
    affinity = dot(b, c, NT)
    source = lax.broadcasted_iota(jnp.int32, affinity.shape, 0)
    later = lax.broadcasted_iota(jnp.int32, affinity.shape, 1)
    return jnp.where(source <= later, affinity, 0.0)


def as_column(row):
    square = jnp.broadcast_to(row, (row.shape[1], row.shape[1]))
    along = lax.broadcasted_iota(jnp.int32, square.shape, 0)
    across = lax.broadcasted_iota(jnp.int32, square.shape, 1)
    return jnp.sum(jnp.where(along == across, square, 0.0), axis=1, keepdims=True)


def per_head(values, heads):
    return values.reshape(heads, HEAD_DIM, values.shape[1])


def call(kernel, grid, in_specs, out_specs, out_shape, scratch=(), flops=0, prefetch=0, vmem=VMEM_BYTES):
    return pl.pallas_call(
        kernel,
        out_shape=out_shape,
        grid_spec=pltpu.PrefetchScalarGridSpec(
            num_scalar_prefetch=prefetch,
            grid=grid,
            in_specs=in_specs,
            out_specs=out_specs,
            scratch_shapes=list(scratch),
        ),
        compiler_params=pltpu.CompilerParams(
            vmem_limit_bytes=vmem, dimension_semantics=("arbitrary",) * len(grid)
        ),
        cost_estimate=pl.CostEstimate(flops=flops * COST_SCALE, bytes_accessed=4_000_000 * COST_SCALE, transcendentals=0),
    )


def whole(*shape):
    return pl.BlockSpec(shape, lambda i, *_: (0,) * len(shape))


def by_row(*shape):
    return pl.BlockSpec(shape, lambda i, *_: (i,) + (0,) * (len(shape) - 1))


ANY = pl.BlockSpec(memory_space=pl.ANY)


def decay_kernel(upper_ref, x_hbm, b_hbm, dt_hbm, alog_hbm, grown_ref, shrunk_ref, total_ref, gathered_ref,
                 payload_ref, mine_ref, x_ref, b_ref, dt_ref, alog_ref, rows_dt, sems):
    heads, length = rows_dt.shape
    group = 4 if heads % 4 == 0 else 1
    block = group * HEAD_DIM
    parts = heads // group
    pieces = [(dt_hbm, dt_ref), (alog_hbm, alog_ref), (b_hbm, b_ref)]
    for i in range(parts):
        here = pl.ds(i * block, block)
        pieces.append((x_hbm.at[here], x_ref.at[here]))
    copies = [pltpu.make_async_copy(src, dst, sems.at[i]) for i, (src, dst) in enumerate(pieces)]
    for copy in copies:
        copy.start()
    copies[0].wait()
    copies[1].wait()
    for h in range(heads):
        rows_dt[h : h + 1] = dt_ref[h]
    step_size = softplus(rows_dt[...])
    cumulative = running_sum(step_size * -jnp.exp(as_column(alog_ref[...])))
    grown = jnp.exp(cumulative)
    shrunk = step_size * jnp.exp(-cumulative)
    for h in range(heads):
        grown_ref[h] = grown[h : h + 1]
        shrunk_ref[h] = shrunk[h : h + 1]
    total = jnp.broadcast_to(cumulative[:, length - 1 :], total_ref.shape)
    total_ref[...] = total
    along = lax.broadcasted_iota(jnp.int32, total.shape, 0)
    across = lax.broadcasted_iota(jnp.int32, total.shape, 1)
    row = jnp.sum(jnp.where(along == across, total, 0.0), axis=0, keepdims=True)
    high, low = split(row)
    middle, low = split(row - high.astype(F32))
    rows = lax.broadcasted_iota(jnp.int32, payload_ref.shape[1:], 0)
    terms = jnp.where(rows == 0, high.astype(F32), jnp.where(rows == 1, middle.astype(F32), low.astype(F32)))
    payload_ref[heads] = jnp.where(rows < 3, terms, 0.0).astype(BF16)
    upper = upper_ref[0] == 1
    copies[2].wait()
    for i in range(parts):
        copies[3 + i].wait()
        x = per_head(x_ref[i * block : (i + 1) * block].astype(F32), group)
        high, low = split((x * shrunk_ref[i * group : (i + 1) * group]).reshape(block, length))
        gathered = dot(high, b_ref[...]) + dot(low, b_ref[...])
        gathered_ref[i * block : (i + 1) * block] = gathered
        for j in range(group):
            h = i * group + j
            local = gathered[j * HEAD_DIM : (j + 1) * HEAD_DIM] * jnp.exp(total[h : h + 1])
            first, second = local[: HEAD_DIM // 2], local[HEAD_DIM // 2 :]
            mine_ref[h] = jnp.where(upper, second, first)
            payload_ref[h] = jnp.where(upper, first, second).astype(BF16)


def inner_kernel(x_ref, b_ref, c_ref, shrunk_ref, skip_ref, after_ref, inner_ref, skips_ref, high_ref, low_ref):
    group = x_ref.shape[0] // HEAD_DIM
    half = x_ref.shape[1] // 2

    @pl.when(pl.program_id(0) == 0)
    def _():
        high_ref[...], low_ref[...] = split(causal_affinity(b_ref[...], c_ref[...]))
        skips = jnp.broadcast_to(as_column(skip_ref[...]), (skips_ref.shape[0], skips_ref.shape[2]))
        for h in range(skips_ref.shape[0]):
            skips_ref[h] = skips[h : h + 1]

    xs = split((per_head(x_ref[...].astype(F32), group) * shrunk_ref[...]).reshape(x_ref.shape))
    affinity = (high_ref, low_ref)
    early = (slice(None), slice(0, half))
    late = (slice(None), slice(half, None))
    corner = (slice(0, half), slice(0, half))
    inner_ref[:, :half] = dot_split(part(xs, early), part(affinity, corner))
    inner_ref[:, half:] = dot_split(xs, part(affinity, late))


def mixed_kernel(inner_ref, state_ref, c_ref, x_ref, grown_ref, skips_ref, after_ref, mixed_ref):
    group = x_ref.shape[0] // HEAD_DIM
    inner = per_head(inner_ref[...] + dot(state_ref[...], c_ref[...], NT), group)
    x = per_head(x_ref[...].astype(F32), group)
    mixed = grown_ref[...] * inner + skips_ref[...] * x
    mixed_ref[...] = mixed.reshape(x_ref.shape).astype(BF16)


def cotan_first_kernel(flag_ref, mine_ref, other_ref, g_ref, after_ref, out_ref):
    @pl.when(flag_ref[0] == 1)
    def _():
        out_ref[...] = dot(mine_ref[...], g_ref[...])

    @pl.when(flag_ref[0] == 0)
    def _():
        out_ref[...] = dot(other_ref[...], g_ref[...])


def cotan_kernel(flag_ref, mine_ref, other_ref, g_ref, first_ref, c_ref, grown_ref, after_ref, cotan_ref, local_ref, sum_ref):
    @pl.when(flag_ref[0] == 0)
    def _():
        sum_ref[...] = first_ref[...] + dot(mine_ref[...], g_ref[...])

    @pl.when(flag_ref[0] == 1)
    def _():
        sum_ref[...] = first_ref[...] + dot(other_ref[...], g_ref[...])

    cotan = sum_ref[...].astype(BF16)
    cotan_ref[...] = cotan
    group = cotan.shape[0] // HEAD_DIM
    gs = (per_head(cotan.astype(F32), group) * grown_ref[...]).reshape(cotan.shape)
    high, low = split(gs)
    local_ref[...] = dot(high, c_ref[...]) + dot(low, c_ref[...])


def terms_kernel(pick_ref, g0_ref, g1_ref, m0_ref, m1_ref, after_ref, out_ref):
    high, _, low, columns, length = g0_ref.shape
    if columns % 16 == 0:
        flat = lambda ref: ref[...].reshape(high * low * columns, length)
        product = dot(flat(g0_ref), m0_ref[...], NT) + dot(flat(g1_ref), m1_ref[...], NT)
        out_ref[...] = product.reshape(out_ref.shape).astype(out_ref.dtype)
    else:
        for i in range(high):
            for j in range(low):
                product = dot(g0_ref[i, 0, j], m0_ref[...], NT) + dot(g1_ref[i, 0, j], m1_ref[...], NT)
                out_ref[i * low + j] = product.astype(out_ref.dtype)


def back_kernel(x_ref, cotan_ref, inner_ref, state_ref, b_ref, c_ref, grown_ref, shrunk_ref, after_ref,
                outer_ref, from_y_ref, grad_b_ref, grad_c_ref, high_ref, low_ref, across_ref):
    step = pl.program_id(0)
    group = x_ref.shape[0] // HEAD_DIM
    half = x_ref.shape[1] // 2

    @pl.when(step == 0)
    def _():
        high_ref[...], low_ref[...] = split(causal_affinity(b_ref[...], c_ref[...]))
        across_ref[...] = jnp.zeros_like(across_ref)
        grad_c_ref[...] = jnp.zeros_like(grad_c_ref)

    x = per_head(x_ref[...].astype(F32), group)
    xs = split((x * shrunk_ref[...]).reshape(x_ref.shape))
    gs_full = (per_head(cotan_ref[...].astype(F32), group) * grown_ref[...]).reshape(x_ref.shape)
    gs = split(gs_full)
    affinity = (high_ref, low_ref)
    late = (slice(None), slice(half, None))
    early = (slice(None), slice(0, half))
    top = (slice(0, half), slice(None))
    corner = (slice(half, None), slice(half, None))
    outer_ref[:, :half] = dot_split(gs, part(affinity, top), NT)
    outer_ref[:, half:] = dot_split(part(gs, late), part(affinity, corner), NT)
    across_ref[:half] += dot_split(part(xs, early), gs, TN)
    across_ref[half:, half:] += dot_split(part(xs, late), part(gs, late), TN)
    state = state_ref[...]
    grad_c_ref[...] += dot(gs[0], state, TN) + dot(gs[1], state, TN)
    inner = inner_ref[...] + dot(state, c_ref[...], NT)
    from_y_ref[...] = jnp.sum(per_head(gs_full * inner, group), axis=1, keepdims=True)

    @pl.when(step == pl.num_programs(0) - 1)
    def _():
        across = across_ref[...]
        source = lax.broadcasted_iota(jnp.int32, across.shape, 0)
        later = lax.broadcasted_iota(jnp.int32, across.shape, 1)
        high, low = split(jnp.where(source <= later, across, 0.0))
        grad_b_ref[...] = dot(high, c_ref[...]) + dot(low, c_ref[...])
        grad_c_ref[...] += dot(high, b_ref[...], TN) + dot(low, b_ref[...], TN)


def last_kernel(x_ref, cotan_ref, outer_ref, ends_ref, gathered_ref, state_ref, shrunk_ref, skips_ref,
                b_ref, dt_ref, alog_ref, from_y_ref, grad_b_ref, grad_c_ref, after_a_ref, after_b_ref,
                grad_inputs_ref, grad_dt_ref, small_ref, both_ref,
                from_x_s, from_end_s, from_skip_s, rows_x, rows_y, rows_skip, rows_end, rows_dt):
    step = pl.program_id(0)
    group = x_ref.shape[0] // HEAD_DIM
    heads, length = rows_x.shape
    n_state = b_ref.shape[1]
    ends = ends_ref[...]
    outer = per_head(outer_ref[...] + dot(ends, b_ref[...], NT), group)
    x = per_head(x_ref[...].astype(F32), group)
    cotan = per_head(cotan_ref[...].astype(F32), group)
    xs = x * shrunk_ref[...]
    grad_inputs = shrunk_ref[...] * outer + skips_ref[...] * cotan
    grad_inputs_ref[...] = grad_inputs.reshape(x_ref.shape).astype(BF16)
    here = pl.ds(step * group, group)
    from_x_s[here] = jnp.sum(xs * outer, axis=1, keepdims=True)
    from_skip_s[here] = jnp.sum(x * cotan, axis=1, keepdims=True)
    moved = ends.astype(F32) * (gathered_ref[...] + state_ref[...].astype(F32))
    from_end_s[here] = jnp.sum(per_head(moved, group), axis=1, keepdims=True)
    high, low = split(xs.reshape(x_ref.shape))

    @pl.when(step == 0)
    def _():
        both_ref[:, :n_state] = grad_b_ref[...]
        both_ref[:, n_state:] = grad_c_ref[...]

    both_ref[:, :n_state] += dot(high, ends, TN) + dot(low, ends, TN)

    @pl.when(step == pl.num_programs(0) - 1)
    def _():
        for h in range(heads):
            rows_x[h : h + 1] = from_x_s[h]
            rows_y[h : h + 1] = from_y_ref[h]
            rows_skip[h : h + 1] = from_skip_s[h]
            rows_end[h : h + 1] = from_end_s[h]
            rows_dt[h : h + 1] = dt_ref[h]
        from_x = rows_x[...]
        from_end = jnp.sum(rows_end[...], axis=1, keepdims=True)
        flow = running_sum(rows_y[...] - from_x, reverse=True) + from_end
        dt = rows_dt[...]
        step_size = softplus(dt)
        rate = -jnp.exp(as_column(alog_ref[...]))
        grad_dt = (from_x / step_size + flow * rate) / (1.0 + jnp.exp(-dt))
        for h in range(heads):
            grad_dt_ref[h] = grad_dt[h : h + 1]
        alog = jnp.sum(flow * step_size * rate, axis=1, keepdims=True)
        skip = jnp.sum(rows_skip[...], axis=1, keepdims=True)
        small_ref[0] = jnp.broadcast_to(alog, small_ref.shape[1:])
        small_ref[1] = jnp.broadcast_to(skip, small_ref.shape[1:])


def swap(value, axis, size, bit):
    return lax.ppermute(value, axis, [(i, i ^ bit) for i in range(size)])


def shifted(value, axis, size, step):
    pairs = [(i, i + step) for i in range(size) if 0 <= i + step < size]
    return lax.ppermute(value, axis, pairs)


def pack(state, total):
    heads, rows, lanes = state.shape
    high = lax.reduce_precision(total, 8, 7)
    middle = lax.reduce_precision(total - high, 8, 7)
    low = total - high - middle
    terms = jnp.stack([high, middle, low]).astype(BF16)
    extra = jnp.pad(terms, ((0, rows - 3), (0, lanes - heads)))
    return jnp.concatenate([state.astype(BF16), extra[None]], axis=0)


def unpack(payload):
    heads = payload.shape[0] - 1
    terms = payload[heads, :3, :heads].astype(F32)
    return payload[:heads].astype(F32), terms[0] + terms[1] + terms[2]


def decay(total):
    return jnp.exp(total)[:, None, None]


def halves_of(local, total):
    heads, width, lanes = local.shape
    upper = lax.rem(lax.axis_index("seq"), 2) == 1
    halves = local.reshape(heads, 2, width // 2, lanes)
    mine = jnp.where(upper, halves[:, 1], halves[:, 0])
    theirs = jnp.where(upper, halves[:, 0], halves[:, 1])
    return pack(theirs, total), mine


def pair_scan(payload, mine, total, n_seq, reverse, beside):
    heads, half_width, lanes = mine.shape
    upper = lax.rem(lax.axis_index("seq"), 2) == 1
    late = jnp.logical_not(upper) if reverse else upper
    works, taken = [], []

    def traveling(payload, got):
        if len(taken) in beside:
            work = beside[len(taken)](payload)
            got, work = lax.optimization_barrier((got, work))
            works.append(work)
        taken.append(payload)
        return got

    other, other_total = unpack(traveling(payload, swap(payload, "seq", n_seq, 1)))
    first = jnp.where(late, other, mine)
    second = jnp.where(late, mine, other)
    first_total = jnp.where(late, other_total, total)
    second_total = jnp.where(late, total, other_total)
    span = decay(second_total) * first + second
    span_total = first_total + second_total
    before, before_total = jnp.zeros_like(span), jnp.zeros_like(span_total)
    step = 2
    while step < n_seq:
        payload = pack(span, span_total)
        moved = shifted(payload, "seq", n_seq, -step if reverse else step)
        earlier, earlier_total = unpack(traveling(payload, moved))
        before = decay(before_total) * earlier + before
        span = decay(span_total) * earlier + span
        before_total = before_total + earlier_total
        span_total = span_total + earlier_total
        step *= 2
    for_first = before
    for_second = decay(first_total) * before + first
    if reverse:
        for_first = decay(first_total) * for_first
        for_second = decay(second_total) * for_second
    keep = jnp.where(late, for_second, for_first).astype(BF16)
    give = jnp.where(late, for_first, for_second).astype(BF16)
    got = swap(give, "seq", n_seq, 1)
    low = jnp.where(upper, got, keep)
    high = jnp.where(upper, keep, got)
    result = jnp.concatenate([low[:, None], high[:, None]], axis=1).reshape(heads * 2 * half_width, lanes)
    return works, result, give


def per_device(mesh, head_inputs, b_proj, c_proj, dt_raw, a_log, d_skip, w_out, out_grad):
    n_seq, n_dp, n_tensor = mesh.shape["seq"], mesh.shape["dp"], mesh.shape["tensor"]
    x, b, c, dt, g = head_inputs[0], b_proj[0], c_proj[0], dt_raw[0], out_grad[0]
    heads, length = dt.shape
    channels = heads * HEAD_DIM
    n_state = b.shape[1]
    features = g.shape[0] * n_tensor
    out_columns = features // (n_seq * n_dp)
    my_dp, my_tensor, my_seq = (lax.axis_index(a) for a in ("dp", "tensor", "seq"))
    group = 4 if heads % 4 == 0 else 1
    block = group * HEAD_DIM
    grid = (heads // group,)
    alog2, skip2, dt3 = a_log[None], d_skip[None], dt[:, None]

    if n_tensor == 2:
        g_first, half_index = g, my_tensor
        g_second = swap(g, "tensor", 2, 1)
    else:
        g_all = lax.all_gather(g, "tensor", axis=0, tiled=True)
        g_first, g_second, half_index = g_all[: features // 2], g_all[features // 2 :], 0

    long = jax.ShapeDtypeStruct((heads, 1, length), F32)
    upper = lax.rem(my_seq, 2).astype(jnp.int32).reshape(1)
    half_state = (HEAD_DIM // 2, n_state)
    grown, shrunk, totals, gathered, payload, mine = call(
        decay_kernel,
        (1,),
        [ANY] * 4,
        [whole(heads, 1, length)] * 2
        + [whole(heads, 128), whole(channels, n_state), whole(heads + 1, *half_state), whole(heads, *half_state)],
        [long] * 2
        + [jax.ShapeDtypeStruct((heads, 128), F32), jax.ShapeDtypeStruct((channels, n_state), F32)]
        + [jax.ShapeDtypeStruct((heads + 1, *half_state), BF16), jax.ShapeDtypeStruct((heads, *half_state), F32)],
        [
            pltpu.VMEM((channels, length), BF16),
            pltpu.VMEM((length, n_state), BF16),
            pltpu.VMEM((heads, 1, length), F32),
            pltpu.VMEM((1, heads), F32),
            pltpu.VMEM((heads, length), F32),
            pltpu.SemaphoreType.DMA((3 + heads // group,)),
        ],
        flops=4 * channels * length * n_state,
        vmem=FIRST_VMEM_BYTES,
        prefetch=1,
    )(upper, x, b, dt3, alog2)
    total = totals[:, 0]

    inners = lambda after: call(
        inner_kernel,
        grid,
        [by_row(block, length), whole(length, n_state), whole(length, n_state), by_row(group, 1, length), whole(1, heads), ANY],
        [by_row(block, length), whole(heads, 1, length)],
        [jax.ShapeDtypeStruct((channels, length), F32), long],
        [pltpu.VMEM((length, length), BF16)] * 2,
        flops=5 * channels * length * length,
    )(x, b, c, shrunk, skip2, after)

    w_other = swap(w_out, "dp", 2, 1)
    flag = (my_dp == half_index).astype(jnp.int32).reshape(1)
    half_features = features // 2
    wide_group = heads // 2 if heads % 2 == 0 else 1
    wide_block = wide_group * HEAD_DIM
    wide_grid = (heads // wide_group,)

    def weights(wanted):
        return pl.BlockSpec(
            (wide_block, half_features), lambda i, flag: (jnp.where(flag[0] == wanted, i, 0), 0)
        )

    first = lambda after: call(
        cotan_first_kernel,
        wide_grid,
        [weights(1), weights(0), whole(half_features, length), ANY],
        by_row(wide_block, length),
        jax.ShapeDtypeStruct((channels, length), F32),
        flops=2 * channels * half_features * length,
        prefetch=1,
    )(flag, w_out, w_other, g_first, after)
    cotans = lambda g_second, first, after: call(
        cotan_kernel,
        wide_grid,
        [weights(0), weights(1)]
        + [whole(half_features, length), by_row(wide_block, length), whole(length, n_state), by_row(wide_group, 1, length), ANY],
        [by_row(wide_block, length), by_row(wide_block, n_state)],
        [jax.ShapeDtypeStruct((channels, length), BF16), jax.ShapeDtypeStruct((channels, n_state), F32)],
        [pltpu.VMEM((wide_block, length), F32)],
        flops=2 * channels * length * (half_features + 2 * n_state),
        prefetch=1,
    )(flag, w_out, w_other, g_second, first, c, grown, after)

    beside = {1: first}
    (first_sum,), state_in, give = pair_scan(payload, mine, total, n_seq, False, beside)

    inner, skips = inners(give)

    def mix(after):
        return call(
            mixed_kernel,
            grid,
            [by_row(block, length), by_row(block, n_state), whole(length, n_state), by_row(block, length)]
            + [by_row(group, 1, length)] * 2
            + [ANY],
            by_row(block, length),
            jax.ShapeDtypeStruct((channels, length), BF16),
            flops=2 * channels * length * n_state,
        )(inner, state_in, c, x, grown, skips, after)

    n_bits = n_seq.bit_length() - 1
    half = channels // 2

    def my_bit(bit):
        value = jnp.bitwise_and(my_seq >> bit, 1)
        return value ^ half_index if bit == n_bits - 1 else value

    def terms(mixed, mixed_other, stream, bit, value, dtype, after):
        low = 1 << bit
        high = n_seq // (2 * low)
        rows = pl.BlockSpec((half, length), lambda i, pick: (stream, 0))
        columns = pl.BlockSpec(
            (high, 1, low, out_columns, length), lambda i, pick: (0, pick[0], 0, 0, 0)
        )
        split_blocks = lambda blocks: blocks.reshape(high, 2, low, out_columns, length)
        return call(
            terms_kernel,
            (1,),
            [columns, columns, rows, rows, ANY],
            whole(n_seq // 2, out_columns, half),
            jax.ShapeDtypeStruct((n_seq // 2, out_columns, half), dtype),
            flops=n_seq * out_columns * half * 2 * length,
            prefetch=1,
        )(
            value.astype(jnp.int32).reshape(1),
            split_blocks(g_mine), split_blocks(g_other), mixed, mixed_other, after,
        )

    orders = [list(range(n_bits)), [1, 0] + list(range(2, n_bits))]
    held = {}

    mixed = mix(give)
    held["mixed"] = mixed, swap(mixed, "dp", 2, 1)
    if n_tensor == 2:
        g_second, _ = lax.optimization_barrier((g_second, mixed))
    firsts = g_first.reshape(n_seq // 2, n_dp, out_columns, length)
    seconds = g_second.reshape(n_seq // 2, n_dp, out_columns, length)

    def chosen(place):
        pick = lambda blocks: lax.dynamic_index_in_dim(blocks, place, 1, keepdims=False)
        return jnp.concatenate([pick(firsts), pick(seconds)])

    g_mine = chosen(my_dp)
    g_other = swap(chosen(1 - my_dp), "dp", 2, 1)
    y_cotan, local_cotan = cotans(g_second, first_sum, mixed)

    def sending(after):
        held["sends"] = [
            terms(*held["mixed"], s, orders[s][0], 1 - my_bit(orders[s][0]), BF16, after) for s in (0, 1)
        ]
        return held["sends"]

    def keeping(after):
        sends = held["sends"]
        held["gots"] = [swap(sends[s], "seq", n_seq, 1 << orders[s][0]) for s in (0, 1)]
        held["keeps"] = [
            terms(*held["mixed"], s, orders[s][0], my_bit(orders[s][0]), F32, after) for s in (0, 1)
        ]
        held["back"] = back(after)
        return held["keeps"], held["back"], held["gots"]

    long = jax.ShapeDtypeStruct((heads, 1, length), F32)
    wide = jax.ShapeDtypeStruct((length, n_state), F32)
    back = lambda after: call(
        back_kernel,
        grid,
        [by_row(block, length)] * 3
        + [by_row(block, n_state), whole(length, n_state), whole(length, n_state)]
        + [by_row(group, 1, length)] * 2
        + [ANY],
        [by_row(block, length), by_row(group, 1, length), whole(length, n_state), whole(length, n_state)],
        [jax.ShapeDtypeStruct((channels, length), F32), long, wide, wide],
        [pltpu.VMEM((length, length), BF16)] * 2 + [pltpu.VMEM((length, length), F32)],
        flops=10 * channels * length * length,
    )(x, y_cotan, inner, state_in, b, c, grown, shrunk, after)
    works, cotan_end, _ = pair_scan(
        *halves_of(local_cotan.reshape(heads, HEAD_DIM, n_state), total), total, n_seq, True,
        {1: sending, 2: keeping},
    )
    keeps, (outer, from_y, grad_b, grad_c), gots = works[-1]

    def halve(sums, left):
        axis = sorted(left, reverse=True).index(left[0])
        pick = lambda value: lax.dynamic_index_in_dim(sums, value, axis, keepdims=False)
        return pick(my_bit(left[0])), pick(1 - my_bit(left[0])).astype(BF16)

    streams = []
    for s in (0, 1):
        sums = keeps[s] + gots[s].astype(F32)
        sums = sums.reshape((2,) * (n_bits - 1) + (out_columns, half))
        streams.append(halve(sums, orders[s][1:]))
    grad_inputs, grad_dt, small, both = call(
        last_kernel,
        grid,
        [by_row(block, length)] * 3
        + [by_row(block, n_state)] * 3
        + [by_row(group, 1, length)] * 2
        + [whole(length, n_state), whole(heads, 1, length), whole(1, heads), whole(heads, 1, length)]
        + [whole(length, n_state)] * 2
        + [ANY] * 2,
        [
            by_row(block, length),
            whole(heads, 1, length),
            whole(2, heads, 128),
            whole(length, 2 * n_state),
        ],
        [
            jax.ShapeDtypeStruct((channels, length), BF16),
            long,
            jax.ShapeDtypeStruct((2, heads, 128), F32),
            jax.ShapeDtypeStruct((length, 2 * n_state), F32),
        ],
        [
            pltpu.VMEM((heads, 1, length), F32),
            pltpu.VMEM((heads, 1, n_state), F32),
            pltpu.VMEM((heads, 1, length), F32),
            pltpu.VMEM((heads, length), F32),
            pltpu.VMEM((heads, length), F32),
            pltpu.VMEM((heads, length), F32),
            pltpu.VMEM((heads, n_state), F32),
            pltpu.VMEM((heads, length), F32),
        ],
        flops=6 * channels * length * n_state,
    )(
        x, y_cotan, outer, cotan_end, gathered, state_in, shrunk, skips,
        b, dt3, alog2, from_y, grad_b, grad_c, streams[0][1], streams[1][1],
    )
    if n_tensor == 2:
        both_other = swap(both, "tensor", 2, 1)
    small = small + swap(small, "dp", 2, 1)
    for done in range(1, n_bits):
        gots = [swap(streams[s][1], "seq", n_seq, 1 << orders[s][done]) for s in (0, 1)]
        if done == 1:
            gots, both, small = lax.optimization_barrier((gots, both, small))
        if done + 1 == n_bits:
            small = lax.all_to_all(jnp.broadcast_to(small, (n_seq,) + small.shape), "seq", 0, 0)
            both = (both + both_other if n_tensor == 2 else lax.psum(both, "tensor")).astype(BF16)
            gots, both = lax.optimization_barrier((gots, both))
        pairs = [streams[s][0] + gots[s].astype(F32) for s in (0, 1)]
        if done + 1 < n_bits:
            streams = [halve(pairs[s], orders[s][done + 1 :]) for s in (0, 1)]
            if done + 2 == n_bits:
                small, _ = lax.optimization_barrier((small, [stream[1] for stream in streams]))
    small = jnp.sum(small[:, :, :, 0], axis=0)
    grad_w = jnp.concatenate(pairs, axis=1).T.astype(BF16)
    return (
        mixed[None],
        grad_inputs[None],
        both[None, :, :n_state],
        both[None, :, n_state:],
        grad_dt[:, 0][None],
        small[0],
        small[1],
        grad_w,
    )


def solution(mesh):
    in_specs = (
        P("dp", "tensor", "seq"),
        P("dp", "seq", None),
        P("dp", "seq", None),
        P("dp", "tensor", "seq"),
        P("tensor"),
        P("tensor"),
        P("tensor", "dp"),
        P("dp", "tensor", "seq"),
    )
    out_specs = (
        P("dp", "tensor", "seq"),
        P("dp", "tensor", "seq"),
        P("dp", "seq", None),
        P("dp", "seq", None),
        P("dp", "tensor", "seq"),
        P("tensor"),
        P("tensor"),
        P("tensor", ("seq", "dp")),
    )
    return jax.shard_map(
        functools.partial(per_device, mesh),
        mesh=mesh,
        in_specs=in_specs,
        out_specs=out_specs,
        check_vma=False,
    )
```

```python
import functools

import jax
import jax.numpy as jnp
from jax import lax
from jax.experimental import pallas as pl
from jax.experimental.pallas import tpu as pltpu
from jax.sharding import PartitionSpec as P

HEAD_DIM = 64
F32 = jnp.float32
BF16 = jnp.bfloat16
NN = (((1,), (0,)), ((), ()))
NT = (((1,), (1,)), ((), ()))
TN = (((0,), (0,)), ((), ()))
VMEM_BYTES = 32 * 1024 * 1024
COST_SCALE = 20
FIRST_VMEM_BYTES = 58 * 1024 * 1024


def dot(a, b, dims=NN):
    return lax.dot_general(a, b, dims, preferred_element_type=F32)


def split(values):
    high = values.astype(BF16)
    return high, (values - high.astype(F32)).astype(BF16)


def dot_split(a, b, dims=NN):
    return dot(a[0], b[0], dims) + dot(a[1], b[0], dims) + dot(a[0], b[1], dims)


def part(pair, index):
    return pair[0][index], pair[1][index]


def running_sum(values, reverse=False):
    length = values.shape[1]
    lane = lax.broadcasted_iota(jnp.int32, values.shape, 1)
    step = 1
    while step < length:
        if reverse:
            moved = jnp.where(lane < length - step, pltpu.roll(values, length - step, 1), 0.0)
        else:
            moved = jnp.where(lane >= step, pltpu.roll(values, step, 1), 0.0)
        values = values + moved
        step *= 2
    return values


def softplus(values):
    return jnp.maximum(values, 0.0) + jnp.log(1.0 + jnp.exp(-jnp.abs(values)))


def causal_affinity(b, c):
    affinity = dot(b, c, NT)
    source = lax.broadcasted_iota(jnp.int32, affinity.shape, 0)
    later = lax.broadcasted_iota(jnp.int32, affinity.shape, 1)
    return jnp.where(source <= later, affinity, 0.0)


def as_column(row):
    square = jnp.broadcast_to(row, (row.shape[1], row.shape[1]))
    along = lax.broadcasted_iota(jnp.int32, square.shape, 0)
    across = lax.broadcasted_iota(jnp.int32, square.shape, 1)
    return jnp.sum(jnp.where(along == across, square, 0.0), axis=1, keepdims=True)


def per_head(values, heads):
    return values.reshape(heads, HEAD_DIM, values.shape[1])


def call(kernel, grid, in_specs, out_specs, out_shape, scratch=(), flops=0, prefetch=0, vmem=VMEM_BYTES):
    return pl.pallas_call(
        kernel,
        out_shape=out_shape,
        grid_spec=pltpu.PrefetchScalarGridSpec(
            num_scalar_prefetch=prefetch,
            grid=grid,
            in_specs=in_specs,
            out_specs=out_specs,
            scratch_shapes=list(scratch),
        ),
        compiler_params=pltpu.CompilerParams(
            vmem_limit_bytes=vmem, dimension_semantics=("arbitrary",) * len(grid)
        ),
        cost_estimate=pl.CostEstimate(flops=flops * COST_SCALE, bytes_accessed=4_000_000 * COST_SCALE, transcendentals=0),
    )


def whole(*shape):
    return pl.BlockSpec(shape, lambda i, *_: (0,) * len(shape))


def by_row(*shape):
    return pl.BlockSpec(shape, lambda i, *_: (i,) + (0,) * (len(shape) - 1))


ANY = pl.BlockSpec(memory_space=pl.ANY)


def decay_kernel(upper_ref, x_hbm, b_hbm, dt_hbm, alog_hbm, grown_ref, shrunk_ref, total_ref, gathered_ref,
                 payload_ref, mine_ref, x_ref, b_ref, dt_ref, alog_ref, rows_dt, sems):
    heads, length = rows_dt.shape
    group = 4 if heads % 4 == 0 else 1
    block = group * HEAD_DIM
    parts = heads // group
    pieces = [(dt_hbm, dt_ref), (alog_hbm, alog_ref), (b_hbm, b_ref)]
    for i in range(parts):
        here = pl.ds(i * block, block)
        pieces.append((x_hbm.at[here], x_ref.at[here]))
    copies = [pltpu.make_async_copy(src, dst, sems.at[i]) for i, (src, dst) in enumerate(pieces)]
    for copy in copies:
        copy.start()
    copies[0].wait()
    copies[1].wait()
    for h in range(heads):
        rows_dt[h : h + 1] = dt_ref[h]
    step_size = softplus(rows_dt[...])
    cumulative = running_sum(step_size * -jnp.exp(as_column(alog_ref[...])))
    grown = jnp.exp(cumulative)
    shrunk = step_size * jnp.exp(-cumulative)
    for h in range(heads):
        grown_ref[h] = grown[h : h + 1]
        shrunk_ref[h] = shrunk[h : h + 1]
    total = jnp.broadcast_to(cumulative[:, length - 1 :], total_ref.shape)
    total_ref[...] = total
    along = lax.broadcasted_iota(jnp.int32, total.shape, 0)
    across = lax.broadcasted_iota(jnp.int32, total.shape, 1)
    row = jnp.sum(jnp.where(along == across, total, 0.0), axis=0, keepdims=True)
    high, low = split(row)
    middle, low = split(row - high.astype(F32))
    rows = lax.broadcasted_iota(jnp.int32, payload_ref.shape[1:], 0)
    terms = jnp.where(rows == 0, high.astype(F32), jnp.where(rows == 1, middle.astype(F32), low.astype(F32)))
    payload_ref[heads] = jnp.where(rows < 3, terms, 0.0).astype(BF16)
    upper = upper_ref[0] == 1
    copies[2].wait()
    for i in range(parts):
        copies[3 + i].wait()
        x = per_head(x_ref[i * block : (i + 1) * block].astype(F32), group)
        high, low = split((x * shrunk_ref[i * group : (i + 1) * group]).reshape(block, length))
        gathered = dot(high, b_ref[...]) + dot(low, b_ref[...])
        gathered_ref[i * block : (i + 1) * block] = gathered
        for j in range(group):
            h = i * group + j
            local = gathered[j * HEAD_DIM : (j + 1) * HEAD_DIM] * jnp.exp(total[h : h + 1])
            first, second = local[: HEAD_DIM // 2], local[HEAD_DIM // 2 :]
            mine_ref[h] = jnp.where(upper, second, first)
            payload_ref[h] = jnp.where(upper, first, second).astype(BF16)


def inner_kernel(x_ref, b_ref, c_ref, shrunk_ref, skip_ref, after_ref, inner_ref, skips_ref, high_ref, low_ref):
    group = x_ref.shape[0] // HEAD_DIM
    half = x_ref.shape[1] // 2

    @pl.when(pl.program_id(0) == 0)
    def _():
        high_ref[...], low_ref[...] = split(causal_affinity(b_ref[...], c_ref[...]))
        skips = jnp.broadcast_to(as_column(skip_ref[...]), (skips_ref.shape[0], skips_ref.shape[2]))
        for h in range(skips_ref.shape[0]):
            skips_ref[h] = skips[h : h + 1]

    xs = split((per_head(x_ref[...].astype(F32), group) * shrunk_ref[...]).reshape(x_ref.shape))
    affinity = (high_ref, low_ref)
    early = (slice(None), slice(0, half))
    late = (slice(None), slice(half, None))
    corner = (slice(0, half), slice(0, half))
    inner_ref[:, :half] = dot_split(part(xs, early), part(affinity, corner))
    inner_ref[:, half:] = dot_split(xs, part(affinity, late))


def mixed_kernel(inner_ref, state_ref, c_ref, x_ref, grown_ref, skips_ref, after_ref, mixed_ref):
    group = x_ref.shape[0] // HEAD_DIM
    inner = per_head(inner_ref[...] + dot(state_ref[...], c_ref[...], NT), group)
    x = per_head(x_ref[...].astype(F32), group)
    mixed = grown_ref[...] * inner + skips_ref[...] * x
    mixed_ref[...] = mixed.reshape(x_ref.shape).astype(BF16)


def cotan_first_kernel(flag_ref, mine_ref, other_ref, g_ref, after_ref, out_ref):
    @pl.when(flag_ref[0] == 1)
    def _():
        out_ref[...] = dot(mine_ref[...], g_ref[...])

    @pl.when(flag_ref[0] == 0)
    def _():
        out_ref[...] = dot(other_ref[...], g_ref[...])


def cotan_kernel(flag_ref, mine_ref, other_ref, g_ref, first_ref, c_ref, grown_ref, after_ref, cotan_ref, local_ref, sum_ref):
    @pl.when(flag_ref[0] == 0)
    def _():
        sum_ref[...] = first_ref[...] + dot(mine_ref[...], g_ref[...])

    @pl.when(flag_ref[0] == 1)
    def _():
        sum_ref[...] = first_ref[...] + dot(other_ref[...], g_ref[...])

    cotan = sum_ref[...].astype(BF16)
    cotan_ref[...] = cotan
    group = cotan.shape[0] // HEAD_DIM
    gs = (per_head(cotan.astype(F32), group) * grown_ref[...]).reshape(cotan.shape)
    high, low = split(gs)
    local_ref[...] = dot(high, c_ref[...]) + dot(low, c_ref[...])


def terms_kernel(pick_ref, g0_ref, g1_ref, m0_ref, m1_ref, after_ref, out_ref):
    high, _, low, columns, length = g0_ref.shape
    if columns % 16 == 0:
        flat = lambda ref: ref[...].reshape(high * low * columns, length)
        product = dot(flat(g0_ref), m0_ref[...], NT) + dot(flat(g1_ref), m1_ref[...], NT)
        out_ref[...] = product.reshape(out_ref.shape).astype(out_ref.dtype)
    else:
        for i in range(high):
            for j in range(low):
                product = dot(g0_ref[i, 0, j], m0_ref[...], NT) + dot(g1_ref[i, 0, j], m1_ref[...], NT)
                out_ref[i * low + j] = product.astype(out_ref.dtype)


def back_kernel(x_ref, cotan_ref, inner_ref, state_ref, b_ref, c_ref, grown_ref, shrunk_ref, after_ref,
                outer_ref, from_y_ref, grad_b_ref, grad_c_ref, high_ref, low_ref, across_ref):
    step = pl.program_id(0)
    group = x_ref.shape[0] // HEAD_DIM
    half = x_ref.shape[1] // 2

    @pl.when(step == 0)
    def _():
        high_ref[...], low_ref[...] = split(causal_affinity(b_ref[...], c_ref[...]))
        across_ref[...] = jnp.zeros_like(across_ref)
        grad_c_ref[...] = jnp.zeros_like(grad_c_ref)

    x = per_head(x_ref[...].astype(F32), group)
    xs = split((x * shrunk_ref[...]).reshape(x_ref.shape))
    gs_full = (per_head(cotan_ref[...].astype(F32), group) * grown_ref[...]).reshape(x_ref.shape)
    gs = split(gs_full)
    affinity = (high_ref, low_ref)
    late = (slice(None), slice(half, None))
    early = (slice(None), slice(0, half))
    top = (slice(0, half), slice(None))
    corner = (slice(half, None), slice(half, None))
    outer_ref[:, :half] = dot_split(gs, part(affinity, top), NT)
    outer_ref[:, half:] = dot_split(part(gs, late), part(affinity, corner), NT)
    across_ref[:half] += dot_split(part(xs, early), gs, TN)
    across_ref[half:, half:] += dot_split(part(xs, late), part(gs, late), TN)
    state = state_ref[...]
    grad_c_ref[...] += dot(gs[0], state, TN) + dot(gs[1], state, TN)
    inner = inner_ref[...] + dot(state, c_ref[...], NT)
    from_y_ref[...] = jnp.sum(per_head(gs_full * inner, group), axis=1, keepdims=True)

    @pl.when(step == pl.num_programs(0) - 1)
    def _():
        across = across_ref[...]
        source = lax.broadcasted_iota(jnp.int32, across.shape, 0)
        later = lax.broadcasted_iota(jnp.int32, across.shape, 1)
        high, low = split(jnp.where(source <= later, across, 0.0))
        grad_b_ref[...] = dot(high, c_ref[...]) + dot(low, c_ref[...])
        grad_c_ref[...] += dot(high, b_ref[...], TN) + dot(low, b_ref[...], TN)


def last_kernel(x_ref, cotan_ref, outer_ref, ends_ref, gathered_ref, state_ref, shrunk_ref, skips_ref,
                b_ref, dt_ref, alog_ref, from_y_ref, grad_b_ref, grad_c_ref, after_a_ref, after_b_ref,
                grad_inputs_ref, grad_dt_ref, small_ref, both_ref,
                from_x_s, from_end_s, from_skip_s, rows_x, rows_y, rows_skip, rows_end, rows_dt):
    step = pl.program_id(0)
    group = x_ref.shape[0] // HEAD_DIM
    heads, length = rows_x.shape
    n_state = b_ref.shape[1]
    ends = ends_ref[...]
    outer = per_head(outer_ref[...] + dot(ends, b_ref[...], NT), group)
    x = per_head(x_ref[...].astype(F32), group)
    cotan = per_head(cotan_ref[...].astype(F32), group)
    xs = x * shrunk_ref[...]
    grad_inputs = shrunk_ref[...] * outer + skips_ref[...] * cotan
    grad_inputs_ref[...] = grad_inputs.reshape(x_ref.shape).astype(BF16)
    here = pl.ds(step * group, group)
    from_x_s[here] = jnp.sum(xs * outer, axis=1, keepdims=True)
    from_skip_s[here] = jnp.sum(x * cotan, axis=1, keepdims=True)
    moved = ends.astype(F32) * (gathered_ref[...] + state_ref[...].astype(F32))
    from_end_s[here] = jnp.sum(per_head(moved, group), axis=1, keepdims=True)
    high, low = split(xs.reshape(x_ref.shape))

    @pl.when(step == 0)
    def _():
        both_ref[:, :n_state] = grad_b_ref[...]
        both_ref[:, n_state:] = grad_c_ref[...]

    both_ref[:, :n_state] += dot(high, ends, TN) + dot(low, ends, TN)

    @pl.when(step == pl.num_programs(0) - 1)
    def _():
        for h in range(heads):
            rows_x[h : h + 1] = from_x_s[h]
            rows_y[h : h + 1] = from_y_ref[h]
            rows_skip[h : h + 1] = from_skip_s[h]
            rows_end[h : h + 1] = from_end_s[h]
            rows_dt[h : h + 1] = dt_ref[h]
        from_x = rows_x[...]
        from_end = jnp.sum(rows_end[...], axis=1, keepdims=True)
        flow = running_sum(rows_y[...] - from_x, reverse=True) + from_end
        dt = rows_dt[...]
        step_size = softplus(dt)
        rate = -jnp.exp(as_column(alog_ref[...]))
        grad_dt = (from_x / step_size + flow * rate) / (1.0 + jnp.exp(-dt))
        for h in range(heads):
            grad_dt_ref[h] = grad_dt[h : h + 1]
        alog = jnp.sum(flow * step_size * rate, axis=1, keepdims=True)
        skip = jnp.sum(rows_skip[...], axis=1, keepdims=True)
        small_ref[0] = jnp.broadcast_to(alog, small_ref.shape[1:])
        small_ref[1] = jnp.broadcast_to(skip, small_ref.shape[1:])


def swap(value, axis, size, bit):
    return lax.ppermute(value, axis, [(i, i ^ bit) for i in range(size)])


def shifted(value, axis, size, step):
    pairs = [(i, i + step) for i in range(size) if 0 <= i + step < size]
    return lax.ppermute(value, axis, pairs)


def pack(state, total):
    heads, rows, lanes = state.shape
    high = lax.reduce_precision(total, 8, 7)
    middle = lax.reduce_precision(total - high, 8, 7)
    low = total - high - middle
    terms = jnp.stack([high, middle, low]).astype(BF16)
    extra = jnp.pad(terms, ((0, rows - 3), (0, lanes - heads)))
    return jnp.concatenate([state.astype(BF16), extra[None]], axis=0)


def unpack(payload):
    heads = payload.shape[0] - 1
    terms = payload[heads, :3, :heads].astype(F32)
    return payload[:heads].astype(F32), terms[0] + terms[1] + terms[2]


def decay(total):
    return jnp.exp(total)[:, None, None]


def halves_of(local, total):
    heads, width, lanes = local.shape
    upper = lax.rem(lax.axis_index("seq"), 2) == 1
    halves = local.reshape(heads, 2, width // 2, lanes)
    mine = jnp.where(upper, halves[:, 1], halves[:, 0])
    theirs = jnp.where(upper, halves[:, 0], halves[:, 1])
    return pack(theirs, total), mine


def pair_scan(payload, mine, total, n_seq, reverse, beside):
    heads, half_width, lanes = mine.shape
    upper = lax.rem(lax.axis_index("seq"), 2) == 1
    late = jnp.logical_not(upper) if reverse else upper
    works, taken = [], []

    def traveling(payload, got):
        if len(taken) in beside:
            work = beside[len(taken)](payload)
            got, work = lax.optimization_barrier((got, work))
            works.append(work)
        taken.append(payload)
        return got

    other, other_total = unpack(traveling(payload, swap(payload, "seq", n_seq, 1)))
    first = jnp.where(late, other, mine)
    second = jnp.where(late, mine, other)
    first_total = jnp.where(late, other_total, total)
    second_total = jnp.where(late, total, other_total)
    span = decay(second_total) * first + second
    span_total = first_total + second_total
    before, before_total = jnp.zeros_like(span), jnp.zeros_like(span_total)
    step = 2
    while step < n_seq:
        payload = pack(span, span_total)
        moved = shifted(payload, "seq", n_seq, -step if reverse else step)
        earlier, earlier_total = unpack(traveling(payload, moved))
        before = decay(before_total) * earlier + before
        span = decay(span_total) * earlier + span
        before_total = before_total + earlier_total
        span_total = span_total + earlier_total
        step *= 2
    for_first = before
    for_second = decay(first_total) * before + first
    if reverse:
        for_first = decay(first_total) * for_first
        for_second = decay(second_total) * for_second
    keep = jnp.where(late, for_second, for_first).astype(BF16)
    give = jnp.where(late, for_first, for_second).astype(BF16)
    got = swap(give, "seq", n_seq, 1)
    low = jnp.where(upper, got, keep)
    high = jnp.where(upper, keep, got)
    result = jnp.concatenate([low[:, None], high[:, None]], axis=1).reshape(heads * 2 * half_width, lanes)
    return works, result, give


def per_device(mesh, head_inputs, b_proj, c_proj, dt_raw, a_log, d_skip, w_out, out_grad):
    n_seq, n_dp, n_tensor = mesh.shape["seq"], mesh.shape["dp"], mesh.shape["tensor"]
    x, b, c, dt, g = head_inputs[0], b_proj[0], c_proj[0], dt_raw[0], out_grad[0]
    heads, length = dt.shape
    channels = heads * HEAD_DIM
    n_state = b.shape[1]
    features = g.shape[0] * n_tensor
    out_columns = features // (n_seq * n_dp)
    my_dp, my_tensor, my_seq = (lax.axis_index(a) for a in ("dp", "tensor", "seq"))
    group = 4 if heads % 4 == 0 else 1
    block = group * HEAD_DIM
    grid = (heads // group,)
    alog2, skip2, dt3 = a_log[None], d_skip[None], dt[:, None]

    if n_tensor == 2:
        g_first, half_index = g, my_tensor
        g_second = swap(g, "tensor", 2, 1)
    else:
        g_all = lax.all_gather(g, "tensor", axis=0, tiled=True)
        g_first, g_second, half_index = g_all[: features // 2], g_all[features // 2 :], 0

    long = jax.ShapeDtypeStruct((heads, 1, length), F32)
    upper = lax.rem(my_seq, 2).astype(jnp.int32).reshape(1)
    half_state = (HEAD_DIM // 2, n_state)
    grown, shrunk, totals, gathered, payload, mine = call(
        decay_kernel,
        (1,),
        [ANY] * 4,
        [whole(heads, 1, length)] * 2
        + [whole(heads, 128), whole(channels, n_state), whole(heads + 1, *half_state), whole(heads, *half_state)],
        [long] * 2
        + [jax.ShapeDtypeStruct((heads, 128), F32), jax.ShapeDtypeStruct((channels, n_state), F32)]
        + [jax.ShapeDtypeStruct((heads + 1, *half_state), BF16), jax.ShapeDtypeStruct((heads, *half_state), F32)],
        [
            pltpu.VMEM((channels, length), BF16),
            pltpu.VMEM((length, n_state), BF16),
            pltpu.VMEM((heads, 1, length), F32),
            pltpu.VMEM((1, heads), F32),
            pltpu.VMEM((heads, length), F32),
            pltpu.SemaphoreType.DMA((3 + heads // group,)),
        ],
        flops=4 * channels * length * n_state,
        vmem=FIRST_VMEM_BYTES,
        prefetch=1,
    )(upper, x, b, dt3, alog2)
    total = totals[:, 0]

    inners = lambda after: call(
        inner_kernel,
        grid,
        [by_row(block, length), whole(length, n_state), whole(length, n_state), by_row(group, 1, length), whole(1, heads), ANY],
        [by_row(block, length), whole(heads, 1, length)],
        [jax.ShapeDtypeStruct((channels, length), F32), long],
        [pltpu.VMEM((length, length), BF16)] * 2,
        flops=5 * channels * length * length,
    )(x, b, c, shrunk, skip2, after)

    w_other = swap(w_out, "dp", 2, 1)
    flag = (my_dp == half_index).astype(jnp.int32).reshape(1)
    half_features = features // 2
    wide_group = heads // 2 if heads % 2 == 0 else 1
    wide_block = wide_group * HEAD_DIM
    wide_grid = (heads // wide_group,)

    def weights(wanted):
        return pl.BlockSpec(
            (wide_block, half_features), lambda i, flag: (jnp.where(flag[0] == wanted, i, 0), 0)
        )

    first = lambda after: call(
        cotan_first_kernel,
        wide_grid,
        [weights(1), weights(0), whole(half_features, length), ANY],
        by_row(wide_block, length),
        jax.ShapeDtypeStruct((channels, length), F32),
        flops=2 * channels * half_features * length,
        prefetch=1,
    )(flag, w_out, w_other, g_first, after)
    cotans = lambda g_second, first, after: call(
        cotan_kernel,
        wide_grid,
        [weights(0), weights(1)]
        + [whole(half_features, length), by_row(wide_block, length), whole(length, n_state), by_row(wide_group, 1, length), ANY],
        [by_row(wide_block, length), by_row(wide_block, n_state)],
        [jax.ShapeDtypeStruct((channels, length), BF16), jax.ShapeDtypeStruct((channels, n_state), F32)],
        [pltpu.VMEM((wide_block, length), F32)],
        flops=2 * channels * length * (half_features + 2 * n_state),
        prefetch=1,
    )(flag, w_out, w_other, g_second, first, c, grown, after)

    beside = {1: first}
    (first_sum,), state_in, give = pair_scan(payload, mine, total, n_seq, False, beside)

    inner, skips = inners(give)

    def mix(after):
        return call(
            mixed_kernel,
            grid,
            [by_row(block, length), by_row(block, n_state), whole(length, n_state), by_row(block, length)]
            + [by_row(group, 1, length)] * 2
            + [ANY],
            by_row(block, length),
            jax.ShapeDtypeStruct((channels, length), BF16),
            flops=2 * channels * length * n_state,
        )(inner, state_in, c, x, grown, skips, after)

    n_bits = n_seq.bit_length() - 1
    unit = channels // 5 if channels % 640 == 0 else channels // 2
    sizes = (3 * unit, 2 * unit) if channels % 640 == 0 else (unit, unit)

    def my_bit(bit):
        value = jnp.bitwise_and(my_seq >> bit, 1)
        return value ^ half_index if bit == n_bits - 1 else value

    def terms(mixed, mixed_other, stream, bit, value, dtype, after):
        low = 1 << bit
        high = n_seq // (2 * low)
        offset = sizes[0] // unit if stream else 0
        rows = pl.BlockSpec((unit, length), lambda i, pick: (offset + i, 0))
        columns = pl.BlockSpec(
            (high, 1, low, out_columns, length), lambda i, pick: (0, pick[0], 0, 0, 0)
        )
        split_blocks = lambda blocks: blocks.reshape(high, 2, low, out_columns, length)
        return call(
            terms_kernel,
            (sizes[stream] // unit,),
            [columns, columns, rows, rows, ANY],
            pl.BlockSpec((n_seq // 2, out_columns, unit), lambda i, pick: (0, 0, i)),
            jax.ShapeDtypeStruct((n_seq // 2, out_columns, sizes[stream]), dtype),
            flops=n_seq * out_columns * sizes[stream] * 2 * length,
            prefetch=1,
        )(
            value.astype(jnp.int32).reshape(1),
            split_blocks(g_mine), split_blocks(g_other), mixed, mixed_other, after,
        )

    orders = [list(range(n_bits)), [1, 0] + list(range(2, n_bits))]
    held = {}

    mixed = mix(give)
    held["mixed"] = mixed, swap(mixed, "dp", 2, 1)
    if n_tensor == 2:
        g_second, _ = lax.optimization_barrier((g_second, mixed))
    firsts = g_first.reshape(n_seq // 2, n_dp, out_columns, length)
    seconds = g_second.reshape(n_seq // 2, n_dp, out_columns, length)

    def chosen(place):
        pick = lambda blocks: lax.dynamic_index_in_dim(blocks, place, 1, keepdims=False)
        return jnp.concatenate([pick(firsts), pick(seconds)])

    g_mine = chosen(my_dp)
    g_other = swap(chosen(1 - my_dp), "dp", 2, 1)
    y_cotan, local_cotan = cotans(g_second, first_sum, mixed)

    def keeping(s, after):
        return terms(*held["mixed"], s, orders[s][0], my_bit(orders[s][0]), F32, after)

    def sending(s, after):
        send = terms(*held["mixed"], s, orders[s][0], 1 - my_bit(orders[s][0]), BF16, after)
        held[s] = swap(send, "seq", n_seq, 1 << orders[s][0])
        return send

    def sending_a(after):
        held["send"] = sending(0, after)
        return held["send"], keeping(0, held["send"])

    def sending_b(after):
        return sending(1, after)

    def behind(after):
        return [keeping(s, after) for s in (1,)], back(after), (held[0], held[1])

    long = jax.ShapeDtypeStruct((heads, 1, length), F32)
    wide = jax.ShapeDtypeStruct((length, n_state), F32)
    back = lambda after: call(
        back_kernel,
        grid,
        [by_row(block, length)] * 3
        + [by_row(block, n_state), whole(length, n_state), whole(length, n_state)]
        + [by_row(group, 1, length)] * 2
        + [ANY],
        [by_row(block, length), by_row(group, 1, length), whole(length, n_state), whole(length, n_state)],
        [jax.ShapeDtypeStruct((channels, length), F32), long, wide, wide],
        [pltpu.VMEM((length, length), BF16)] * 2 + [pltpu.VMEM((length, length), F32)],
        flops=10 * channels * length * length,
    )(x, y_cotan, inner, state_in, b, c, grown, shrunk, after)
    works, cotan_end, _ = pair_scan(
        *halves_of(local_cotan.reshape(heads, HEAD_DIM, n_state), total), total, n_seq, True,
        {0: sending_a, 1: sending_b, 2: behind},
    )
    (_, keep_a), _, ((keep_b,), (outer, from_y, grad_b, grad_c), gots) = works
    keeps = keep_a, keep_b

    def halve(sums, left):
        axis = sorted(left, reverse=True).index(left[0])
        pick = lambda value: lax.dynamic_index_in_dim(sums, value, axis, keepdims=False)
        return pick(my_bit(left[0])), pick(1 - my_bit(left[0])).astype(BF16)

    streams = []
    for s in (0, 1):
        sums = keeps[s] + gots[s].astype(F32)
        sums = sums.reshape((2,) * (n_bits - 1) + (out_columns, sizes[s]))
        streams.append(halve(sums, orders[s][1:]))
    grad_inputs, grad_dt, small, both = call(
        last_kernel,
        grid,
        [by_row(block, length)] * 3
        + [by_row(block, n_state)] * 3
        + [by_row(group, 1, length)] * 2
        + [whole(length, n_state), whole(heads, 1, length), whole(1, heads), whole(heads, 1, length)]
        + [whole(length, n_state)] * 2
        + [ANY] * 2,
        [
            by_row(block, length),
            whole(heads, 1, length),
            whole(2, heads, 128),
            whole(length, 2 * n_state),
        ],
        [
            jax.ShapeDtypeStruct((channels, length), BF16),
            long,
            jax.ShapeDtypeStruct((2, heads, 128), F32),
            jax.ShapeDtypeStruct((length, 2 * n_state), F32),
        ],
        [
            pltpu.VMEM((heads, 1, length), F32),
            pltpu.VMEM((heads, 1, n_state), F32),
            pltpu.VMEM((heads, 1, length), F32),
            pltpu.VMEM((heads, length), F32),
            pltpu.VMEM((heads, length), F32),
            pltpu.VMEM((heads, length), F32),
            pltpu.VMEM((heads, n_state), F32),
            pltpu.VMEM((heads, length), F32),
        ],
        flops=6 * channels * length * n_state,
    )(
        x, y_cotan, outer, cotan_end, gathered, state_in, shrunk, skips,
        b, dt3, alog2, from_y, grad_b, grad_c, streams[0][1], streams[1][1],
    )
    if n_tensor == 2:
        both_other = swap(both, "tensor", 2, 1)
    small = small + swap(small, "dp", 2, 1)
    for done in range(1, n_bits):
        gots = [swap(streams[s][1], "seq", n_seq, 1 << orders[s][done]) for s in (0, 1)]
        if done == 1:
            gots, both, small = lax.optimization_barrier((gots, both, small))
        if done + 1 == n_bits:
            small = lax.all_to_all(jnp.broadcast_to(small, (n_seq,) + small.shape), "seq", 0, 0)
            both = (both + both_other if n_tensor == 2 else lax.psum(both, "tensor")).astype(BF16)
            grad_b, grad_c = both[:, :n_state], both[:, n_state:]
            gots, grad_b, grad_c = lax.optimization_barrier((gots, grad_b, grad_c))
        pairs = [streams[s][0] + gots[s].astype(F32) for s in (0, 1)]
        if done + 1 < n_bits:
            streams = [halve(pairs[s], orders[s][done + 1 :]) for s in (0, 1)]
            if done + 2 == n_bits:
                small, _ = lax.optimization_barrier((small, [stream[1] for stream in streams]))
    small = jnp.sum(small[:, :, :, 0], axis=0)
    grad_w = jnp.concatenate(pairs, axis=1).T.astype(BF16)
    return (
        mixed[None],
        grad_inputs[None],
        grad_b[None],
        grad_c[None],
        grad_dt[:, 0][None],
        small[0],
        small[1],
        grad_w,
    )


def solution(mesh):
    in_specs = (
        P("dp", "tensor", "seq"),
        P("dp", "seq", None),
        P("dp", "seq", None),
        P("dp", "tensor", "seq"),
        P("tensor"),
        P("tensor"),
        P("tensor", "dp"),
        P("dp", "tensor", "seq"),
    )
    out_specs = (
        P("dp", "tensor", "seq"),
        P("dp", "tensor", "seq"),
        P("dp", "seq", None),
        P("dp", "seq", None),
        P("dp", "tensor", "seq"),
        P("tensor"),
        P("tensor"),
        P("tensor", ("seq", "dp")),
    )
    return jax.shard_map(
        functools.partial(per_device, mesh),
        mesh=mesh,
        in_specs=in_specs,
        out_specs=out_specs,
        check_vma=False,
    )
```

```python
import functools

import jax
import jax.numpy as jnp
from jax import lax
from jax.experimental import pallas as pl
from jax.experimental.pallas import tpu as pltpu
from jax.sharding import PartitionSpec as P

HEAD_DIM = 64
F32 = jnp.float32
BF16 = jnp.bfloat16
NN = (((1,), (0,)), ((), ()))
NT = (((1,), (1,)), ((), ()))
TN = (((0,), (0,)), ((), ()))
VMEM_BYTES = 16 * 1024 * 1024
COST_SCALE = 20
FIRST_VMEM_BYTES = 58 * 1024 * 1024


def dot(a, b, dims=NN):
    return lax.dot_general(a, b, dims, preferred_element_type=F32)


def split(values):
    high = values.astype(BF16)
    return high, (values - high.astype(F32)).astype(BF16)


def dot_split(a, b, dims=NN):
    return dot(a[0], b[0], dims) + dot(a[1], b[0], dims) + dot(a[0], b[1], dims)


def part(pair, index):
    return pair[0][index], pair[1][index]


def running_sum(values, reverse=False):
    length = values.shape[1]
    lane = lax.broadcasted_iota(jnp.int32, values.shape, 1)
    step = 1
    while step < length:
        if reverse:
            moved = jnp.where(lane < length - step, pltpu.roll(values, length - step, 1), 0.0)
        else:
            moved = jnp.where(lane >= step, pltpu.roll(values, step, 1), 0.0)
        values = values + moved
        step *= 2
    return values


def softplus(values):
    return jnp.maximum(values, 0.0) + jnp.log(1.0 + jnp.exp(-jnp.abs(values)))


def causal_affinity(b, c):
    affinity = dot(b, c, NT)
    source = lax.broadcasted_iota(jnp.int32, affinity.shape, 0)
    later = lax.broadcasted_iota(jnp.int32, affinity.shape, 1)
    return jnp.where(source <= later, affinity, 0.0)


def as_column(row):
    square = jnp.broadcast_to(row, (row.shape[1], row.shape[1]))
    along = lax.broadcasted_iota(jnp.int32, square.shape, 0)
    across = lax.broadcasted_iota(jnp.int32, square.shape, 1)
    return jnp.sum(jnp.where(along == across, square, 0.0), axis=1, keepdims=True)


def per_head(values, heads):
    return values.reshape(heads, HEAD_DIM, values.shape[1])


def call(kernel, grid, in_specs, out_specs, out_shape, scratch=(), flops=0, prefetch=0, vmem=VMEM_BYTES):
    return pl.pallas_call(
        kernel,
        out_shape=out_shape,
        grid_spec=pltpu.PrefetchScalarGridSpec(
            num_scalar_prefetch=prefetch,
            grid=grid,
            in_specs=in_specs,
            out_specs=out_specs,
            scratch_shapes=list(scratch),
        ),
        compiler_params=pltpu.CompilerParams(
            vmem_limit_bytes=vmem, dimension_semantics=("arbitrary",) * len(grid)
        ),
        cost_estimate=pl.CostEstimate(flops=flops * COST_SCALE, bytes_accessed=4_000_000 * COST_SCALE, transcendentals=0),
    )


def whole(*shape):
    return pl.BlockSpec(shape, lambda i, *_: (0,) * len(shape))


def by_row(*shape):
    return pl.BlockSpec(shape, lambda i, *_: (i,) + (0,) * (len(shape) - 1))


ANY = pl.BlockSpec(memory_space=pl.ANY)


def decay_kernel(upper_ref, x_hbm, b_hbm, dt_hbm, alog_hbm, grown_ref, shrunk_ref, total_ref, gathered_ref,
                 payload_ref, mine_ref, x_ref, b_ref, dt_ref, alog_ref, rows_dt, sems):
    heads, length = rows_dt.shape
    group = 4 if heads % 4 == 0 else 1
    block = group * HEAD_DIM
    parts = heads // group
    pieces = [(dt_hbm, dt_ref), (alog_hbm, alog_ref), (b_hbm, b_ref)]
    for i in range(parts):
        here = pl.ds(i * block, block)
        pieces.append((x_hbm.at[here], x_ref.at[here]))
    copies = [pltpu.make_async_copy(src, dst, sems.at[i]) for i, (src, dst) in enumerate(pieces)]
    for copy in copies:
        copy.start()
    copies[0].wait()
    copies[1].wait()
    for h in range(heads):
        rows_dt[h : h + 1] = dt_ref[h]
    step_size = softplus(rows_dt[...])
    cumulative = running_sum(step_size * -jnp.exp(as_column(alog_ref[...])))
    grown = jnp.exp(cumulative)
    shrunk = step_size * jnp.exp(-cumulative)
    for h in range(heads):
        grown_ref[h] = grown[h : h + 1]
        shrunk_ref[h] = shrunk[h : h + 1]
    total = jnp.broadcast_to(cumulative[:, length - 1 :], total_ref.shape)
    total_ref[...] = total
    along = lax.broadcasted_iota(jnp.int32, total.shape, 0)
    across = lax.broadcasted_iota(jnp.int32, total.shape, 1)
    row = jnp.sum(jnp.where(along == across, total, 0.0), axis=0, keepdims=True)
    high, low = split(row)
    middle, low = split(row - high.astype(F32))
    rows = lax.broadcasted_iota(jnp.int32, payload_ref.shape[1:], 0)
    terms = jnp.where(rows == 0, high.astype(F32), jnp.where(rows == 1, middle.astype(F32), low.astype(F32)))
    payload_ref[heads] = jnp.where(rows < 3, terms, 0.0).astype(BF16)
    upper = upper_ref[0] == 1
    copies[2].wait()
    for i in range(parts):
        copies[3 + i].wait()
        x = per_head(x_ref[i * block : (i + 1) * block].astype(F32), group)
        high, low = split((x * shrunk_ref[i * group : (i + 1) * group]).reshape(block, length))
        gathered = dot(high, b_ref[...]) + dot(low, b_ref[...])
        gathered_ref[i * block : (i + 1) * block] = gathered
        for j in range(group):
            h = i * group + j
            local = gathered[j * HEAD_DIM : (j + 1) * HEAD_DIM] * jnp.exp(total[h : h + 1])
            first, second = local[: HEAD_DIM // 2], local[HEAD_DIM // 2 :]
            mine_ref[h] = jnp.where(upper, second, first)
            payload_ref[h] = jnp.where(upper, first, second).astype(BF16)


def inner_kernel(x_ref, b_ref, c_ref, shrunk_ref, skip_ref, after_ref, inner_ref, skips_ref, high_ref, low_ref):
    group = x_ref.shape[0] // HEAD_DIM
    half = x_ref.shape[1] // 2

    @pl.when(pl.program_id(0) == 0)
    def _():
        high_ref[...], low_ref[...] = split(causal_affinity(b_ref[...], c_ref[...]))
        skips = jnp.broadcast_to(as_column(skip_ref[...]), (skips_ref.shape[0], skips_ref.shape[2]))
        for h in range(skips_ref.shape[0]):
            skips_ref[h] = skips[h : h + 1]

    xs = split((per_head(x_ref[...].astype(F32), group) * shrunk_ref[...]).reshape(x_ref.shape))
    affinity = (high_ref, low_ref)
    early = (slice(None), slice(0, half))
    late = (slice(None), slice(half, None))
    corner = (slice(0, half), slice(0, half))
    inner_ref[:, :half] = dot_split(part(xs, early), part(affinity, corner))
    inner_ref[:, half:] = dot_split(xs, part(affinity, late))


def mixed_kernel(inner_ref, state_ref, c_ref, x_ref, grown_ref, skips_ref, after_ref, mixed_ref):
    group = x_ref.shape[0] // HEAD_DIM
    inner = per_head(inner_ref[...] + dot(state_ref[...], c_ref[...], NT), group)
    x = per_head(x_ref[...].astype(F32), group)
    mixed = grown_ref[...] * inner + skips_ref[...] * x
    mixed_ref[...] = mixed.reshape(x_ref.shape).astype(BF16)


def cotan_first_kernel(flag_ref, mine_ref, other_ref, g_ref, after_ref, out_ref, later_ref):
    @pl.when(flag_ref[0] == 1)
    def _():
        out_ref[...] = dot(mine_ref[...], g_ref[...])
        later_ref[...] = other_ref[...]

    @pl.when(flag_ref[0] == 0)
    def _():
        out_ref[...] = dot(other_ref[...], g_ref[...])
        later_ref[...] = mine_ref[...]


def cotan_kernel(weights_ref, g_ref, first_ref, c_ref, grown_ref, after_ref, cotan_ref, local_ref, sum_ref):
    sum_ref[...] = first_ref[...] + dot(weights_ref[...], g_ref[...])
    cotan = sum_ref[...].astype(BF16)
    cotan_ref[...] = cotan
    group = cotan.shape[0] // HEAD_DIM
    gs = (per_head(cotan.astype(F32), group) * grown_ref[...]).reshape(cotan.shape)
    high, low = split(gs)
    local_ref[...] = dot(high, c_ref[...]) + dot(low, c_ref[...])


def terms_kernel(pick_ref, g0_ref, g1_ref, m0_ref, m1_ref, after_ref, out_ref):
    high, _, low, columns, length = g0_ref.shape
    if columns % 16 == 0:
        flat = lambda ref: ref[...].reshape(high * low * columns, length)
        product = dot(flat(g0_ref), m0_ref[...], NT) + dot(flat(g1_ref), m1_ref[...], NT)
        out_ref[...] = product.reshape(out_ref.shape).astype(out_ref.dtype)
    else:
        for i in range(high):
            for j in range(low):
                product = dot(g0_ref[i, 0, j], m0_ref[...], NT) + dot(g1_ref[i, 0, j], m1_ref[...], NT)
                out_ref[i * low + j] = product.astype(out_ref.dtype)


def back_kernel(x_ref, cotan_ref, inner_ref, state_ref, b_ref, c_ref, grown_ref, shrunk_ref, after_ref,
                outer_ref, from_y_ref, grad_b_ref, grad_c_ref, high_ref, low_ref, across_ref):
    step = pl.program_id(0)
    group = x_ref.shape[0] // HEAD_DIM
    half = x_ref.shape[1] // 2

    @pl.when(step == 0)
    def _():
        high_ref[...], low_ref[...] = split(causal_affinity(b_ref[...], c_ref[...]))
        across_ref[...] = jnp.zeros_like(across_ref)
        grad_c_ref[...] = jnp.zeros_like(grad_c_ref)

    x = per_head(x_ref[...].astype(F32), group)
    xs = split((x * shrunk_ref[...]).reshape(x_ref.shape))
    gs_full = (per_head(cotan_ref[...].astype(F32), group) * grown_ref[...]).reshape(x_ref.shape)
    gs = split(gs_full)
    affinity = (high_ref, low_ref)
    late = (slice(None), slice(half, None))
    early = (slice(None), slice(0, half))
    top = (slice(0, half), slice(None))
    corner = (slice(half, None), slice(half, None))
    outer_ref[:, :half] = dot_split(gs, part(affinity, top), NT)
    outer_ref[:, half:] = dot_split(part(gs, late), part(affinity, corner), NT)
    across_ref[:half] += dot_split(part(xs, early), gs, TN)
    across_ref[half:, half:] += dot_split(part(xs, late), part(gs, late), TN)
    state = state_ref[...]
    grad_c_ref[...] += dot(gs[0], state, TN) + dot(gs[1], state, TN)
    inner = inner_ref[...] + dot(state, c_ref[...], NT)
    from_y_ref[...] = jnp.sum(per_head(gs_full * inner, group), axis=1, keepdims=True)

    @pl.when(step == pl.num_programs(0) - 1)
    def _():
        across = across_ref[...]
        source = lax.broadcasted_iota(jnp.int32, across.shape, 0)
        later = lax.broadcasted_iota(jnp.int32, across.shape, 1)
        high, low = split(jnp.where(source <= later, across, 0.0))
        grad_b_ref[...] = dot(high, c_ref[...]) + dot(low, c_ref[...])
        grad_c_ref[...] += dot(high, b_ref[...], TN) + dot(low, b_ref[...], TN)


def last_kernel(x_ref, cotan_ref, outer_ref, ends_ref, gathered_ref, state_ref, shrunk_ref, skips_ref,
                b_ref, dt_ref, alog_ref, from_y_ref, grad_b_ref, grad_c_ref, after_a_ref, after_b_ref,
                grad_inputs_ref, grad_dt_ref, small_ref, both_ref,
                from_x_s, from_end_s, from_skip_s, rows_x, rows_y, rows_skip, rows_end, rows_dt):
    step = pl.program_id(0)
    group = x_ref.shape[0] // HEAD_DIM
    heads, length = rows_x.shape
    n_state = b_ref.shape[1]
    ends = ends_ref[...]
    outer = per_head(outer_ref[...] + dot(ends, b_ref[...], NT), group)
    x = per_head(x_ref[...].astype(F32), group)
    cotan = per_head(cotan_ref[...].astype(F32), group)
    xs = x * shrunk_ref[...]
    grad_inputs = shrunk_ref[...] * outer + skips_ref[...] * cotan
    grad_inputs_ref[...] = grad_inputs.reshape(x_ref.shape).astype(BF16)
    here = pl.ds(step * group, group)
    from_x_s[here] = jnp.sum(xs * outer, axis=1, keepdims=True)
    from_skip_s[here] = jnp.sum(x * cotan, axis=1, keepdims=True)
    moved = ends.astype(F32) * (gathered_ref[...] + state_ref[...].astype(F32))
    from_end_s[here] = jnp.sum(per_head(moved, group), axis=1, keepdims=True)
    high, low = split(xs.reshape(x_ref.shape))

    @pl.when(step == 0)
    def _():
        both_ref[:, :n_state] = grad_b_ref[...]
        both_ref[:, n_state:] = grad_c_ref[...]

    both_ref[:, :n_state] += dot(high, ends, TN) + dot(low, ends, TN)

    @pl.when(step == pl.num_programs(0) - 1)
    def _():
        for h in range(heads):
            rows_x[h : h + 1] = from_x_s[h]
            rows_y[h : h + 1] = from_y_ref[h]
            rows_skip[h : h + 1] = from_skip_s[h]
            rows_end[h : h + 1] = from_end_s[h]
            rows_dt[h : h + 1] = dt_ref[h]
        from_x = rows_x[...]
        from_end = jnp.sum(rows_end[...], axis=1, keepdims=True)
        flow = running_sum(rows_y[...] - from_x, reverse=True) + from_end
        dt = rows_dt[...]
        step_size = softplus(dt)
        rate = -jnp.exp(as_column(alog_ref[...]))
        grad_dt = (from_x / step_size + flow * rate) / (1.0 + jnp.exp(-dt))
        for h in range(heads):
            grad_dt_ref[h] = grad_dt[h : h + 1]
        alog = jnp.sum(flow * step_size * rate, axis=1, keepdims=True)
        skip = jnp.sum(rows_skip[...], axis=1, keepdims=True)
        small_ref[0] = jnp.broadcast_to(alog, small_ref.shape[1:])
        small_ref[1] = jnp.broadcast_to(skip, small_ref.shape[1:])


def swap(value, axis, size, bit):
    return lax.ppermute(value, axis, [(i, i ^ bit) for i in range(size)])


def shifted(value, axis, size, step):
    pairs = [(i, i + step) for i in range(size) if 0 <= i + step < size]
    return lax.ppermute(value, axis, pairs)


def pack(state, total):
    heads, rows, lanes = state.shape
    high = lax.reduce_precision(total, 8, 7)
    middle = lax.reduce_precision(total - high, 8, 7)
    low = total - high - middle
    terms = jnp.stack([high, middle, low]).astype(BF16)
    extra = jnp.pad(terms, ((0, rows - 3), (0, lanes - heads)))
    return jnp.concatenate([state.astype(BF16), extra[None]], axis=0)


def unpack(payload):
    heads = payload.shape[0] - 1
    terms = payload[heads, :3, :heads].astype(F32)
    return payload[:heads].astype(F32), terms[0] + terms[1] + terms[2]


def decay(total):
    return jnp.exp(total)[:, None, None]


def halves_of(local, total):
    heads, width, lanes = local.shape
    upper = lax.rem(lax.axis_index("seq"), 2) == 1
    halves = local.reshape(heads, 2, width // 2, lanes)
    mine = jnp.where(upper, halves[:, 1], halves[:, 0])
    theirs = jnp.where(upper, halves[:, 0], halves[:, 1])
    return pack(theirs, total), mine


def pair_scan(payload, mine, total, n_seq, reverse, beside):
    heads, half_width, lanes = mine.shape
    upper = lax.rem(lax.axis_index("seq"), 2) == 1
    late = jnp.logical_not(upper) if reverse else upper
    works, taken = [], []

    def traveling(payload, got):
        if len(taken) in beside:
            work = beside[len(taken)](payload)
            got, work = lax.optimization_barrier((got, work))
            works.append(work)
        taken.append(payload)
        return got

    other, other_total = unpack(traveling(payload, swap(payload, "seq", n_seq, 1)))
    first = jnp.where(late, other, mine)
    second = jnp.where(late, mine, other)
    first_total = jnp.where(late, other_total, total)
    second_total = jnp.where(late, total, other_total)
    span = decay(second_total) * first + second
    span_total = first_total + second_total
    before, before_total = jnp.zeros_like(span), jnp.zeros_like(span_total)
    step = 2
    while step < n_seq:
        payload = pack(span, span_total)
        moved = shifted(payload, "seq", n_seq, -step if reverse else step)
        earlier, earlier_total = unpack(traveling(payload, moved))
        before = decay(before_total) * earlier + before
        span = decay(span_total) * earlier + span
        before_total = before_total + earlier_total
        span_total = span_total + earlier_total
        step *= 2
    for_first = before
    for_second = decay(first_total) * before + first
    if reverse:
        for_first = decay(first_total) * for_first
        for_second = decay(second_total) * for_second
    keep = jnp.where(late, for_second, for_first).astype(BF16)
    give = jnp.where(late, for_first, for_second).astype(BF16)
    got = swap(give, "seq", n_seq, 1)
    low = jnp.where(upper, got, keep)
    high = jnp.where(upper, keep, got)
    result = jnp.concatenate([low[:, None], high[:, None]], axis=1).reshape(heads * 2 * half_width, lanes)
    return works, result, give


def per_device(mesh, head_inputs, b_proj, c_proj, dt_raw, a_log, d_skip, w_out, out_grad):
    n_seq, n_dp, n_tensor = mesh.shape["seq"], mesh.shape["dp"], mesh.shape["tensor"]
    x, b, c, dt, g = head_inputs[0], b_proj[0], c_proj[0], dt_raw[0], out_grad[0]
    heads, length = dt.shape
    channels = heads * HEAD_DIM
    n_state = b.shape[1]
    features = g.shape[0] * n_tensor
    out_columns = features // (n_seq * n_dp)
    my_dp, my_tensor, my_seq = (lax.axis_index(a) for a in ("dp", "tensor", "seq"))
    group = 4 if heads % 4 == 0 else 1
    block = group * HEAD_DIM
    grid = (heads // group,)
    alog2, skip2, dt3 = a_log[None], d_skip[None], dt[:, None]

    if n_tensor == 2:
        g_first, half_index = g, my_tensor
        g_second = swap(g, "tensor", 2, 1)
    else:
        g_all = lax.all_gather(g, "tensor", axis=0, tiled=True)
        g_first, g_second, half_index = g_all[: features // 2], g_all[features // 2 :], 0

    long = jax.ShapeDtypeStruct((heads, 1, length), F32)
    upper = lax.rem(my_seq, 2).astype(jnp.int32).reshape(1)
    half_state = (HEAD_DIM // 2, n_state)
    grown, shrunk, totals, gathered, payload, mine = call(
        decay_kernel,
        (1,),
        [ANY] * 4,
        [whole(heads, 1, length)] * 2
        + [whole(heads, 128), whole(channels, n_state), whole(heads + 1, *half_state), whole(heads, *half_state)],
        [long] * 2
        + [jax.ShapeDtypeStruct((heads, 128), F32), jax.ShapeDtypeStruct((channels, n_state), F32)]
        + [jax.ShapeDtypeStruct((heads + 1, *half_state), BF16), jax.ShapeDtypeStruct((heads, *half_state), F32)],
        [
            pltpu.VMEM((channels, length), BF16),
            pltpu.VMEM((length, n_state), BF16),
            pltpu.VMEM((heads, 1, length), F32),
            pltpu.VMEM((1, heads), F32),
            pltpu.VMEM((heads, length), F32),
            pltpu.SemaphoreType.DMA((3 + heads // group,)),
        ],
        flops=4 * channels * length * n_state,
        vmem=FIRST_VMEM_BYTES,
        prefetch=1,
    )(upper, x, b, dt3, alog2)
    total = totals[:, 0]

    inners = lambda after: call(
        inner_kernel,
        grid,
        [by_row(block, length), whole(length, n_state), whole(length, n_state), by_row(group, 1, length), whole(1, heads), ANY],
        [by_row(block, length), whole(heads, 1, length)],
        [jax.ShapeDtypeStruct((channels, length), F32), long],
        [pltpu.VMEM((length, length), BF16)] * 2,
        flops=5 * channels * length * length,
    )(x, b, c, shrunk, skip2, after)

    w_other = swap(w_out, "dp", 2, 1)
    flag = (my_dp == half_index).astype(jnp.int32).reshape(1)
    half_features = features // 2
    wide_group = heads // 2 if heads % 2 == 0 else 1
    wide_block = wide_group * HEAD_DIM
    wide_grid = (heads // wide_group,)

    first = lambda after: call(
        cotan_first_kernel,
        wide_grid,
        [by_row(wide_block, half_features)] * 2 + [whole(half_features, length), ANY],
        [by_row(wide_block, length), by_row(wide_block, half_features)],
        [jax.ShapeDtypeStruct((channels, length), F32), jax.ShapeDtypeStruct((channels, half_features), BF16)],
        flops=2 * channels * half_features * length,
        prefetch=1,
    )(flag, w_out, w_other, g_first, after)
    cotans = lambda g_second, first, later, after: call(
        cotan_kernel,
        wide_grid,
        [by_row(wide_block, half_features)]
        + [whole(half_features, length), by_row(wide_block, length), whole(length, n_state), by_row(wide_group, 1, length), ANY],
        [by_row(wide_block, length), by_row(wide_block, n_state)],
        [jax.ShapeDtypeStruct((channels, length), BF16), jax.ShapeDtypeStruct((channels, n_state), F32)],
        [pltpu.VMEM((wide_block, length), F32)],
        flops=2 * channels * length * (half_features + 2 * n_state),
    )(later, g_second, first, c, grown, after)

    beside = {1: first}
    ((first_sum, later),), state_in, give = pair_scan(payload, mine, total, n_seq, False, beside)

    inner, skips = inners(give)

    def mix(after):
        return call(
            mixed_kernel,
            grid,
            [by_row(block, length), by_row(block, n_state), whole(length, n_state), by_row(block, length)]
            + [by_row(group, 1, length)] * 2
            + [ANY],
            by_row(block, length),
            jax.ShapeDtypeStruct((channels, length), BF16),
            flops=2 * channels * length * n_state,
        )(inner, state_in, c, x, grown, skips, after)

    n_bits = n_seq.bit_length() - 1
    unit = channels // 5 if channels % 640 == 0 else channels // 2
    sizes = (3 * unit, 2 * unit) if channels % 640 == 0 else (unit, unit)

    def my_bit(bit):
        value = jnp.bitwise_and(my_seq >> bit, 1)
        return value ^ half_index if bit == n_bits - 1 else value

    def terms(mixed, mixed_other, stream, bit, value, dtype, after):
        low = 1 << bit
        high = n_seq // (2 * low)
        offset = sizes[0] // unit if stream else 0
        rows = pl.BlockSpec((unit, length), lambda i, pick: (offset + i, 0))
        columns = pl.BlockSpec(
            (high, 1, low, out_columns, length), lambda i, pick: (0, pick[0], 0, 0, 0)
        )
        split_blocks = lambda blocks: blocks.reshape(high, 2, low, out_columns, length)
        return call(
            terms_kernel,
            (sizes[stream] // unit,),
            [columns, columns, rows, rows, ANY],
            pl.BlockSpec((n_seq // 2, out_columns, unit), lambda i, pick: (0, 0, i)),
            jax.ShapeDtypeStruct((n_seq // 2, out_columns, sizes[stream]), dtype),
            flops=n_seq * out_columns * sizes[stream] * 2 * length,
            prefetch=1,
        )(
            value.astype(jnp.int32).reshape(1),
            split_blocks(g_mine), split_blocks(g_other), mixed, mixed_other, after,
        )

    orders = [list(range(n_bits)), [1, 0] + list(range(2, n_bits))]
    held = {}

    mixed = mix(give)
    held["mixed"] = mixed, swap(mixed, "dp", 2, 1)
    if n_tensor == 2:
        g_second, _ = lax.optimization_barrier((g_second, mixed))
    firsts = g_first.reshape(n_seq // 2, n_dp, out_columns, length)
    seconds = g_second.reshape(n_seq // 2, n_dp, out_columns, length)

    def chosen(place):
        pick = lambda blocks: lax.dynamic_index_in_dim(blocks, place, 1, keepdims=False)
        return jnp.concatenate([pick(firsts), pick(seconds)])

    g_mine = chosen(my_dp)
    g_other = swap(chosen(1 - my_dp), "dp", 2, 1)
    y_cotan, local_cotan = cotans(g_second, first_sum, later, mixed)

    def keeping(s, after):
        return terms(*held["mixed"], s, orders[s][0], my_bit(orders[s][0]), F32, after)

    def sending(s, after):
        send = terms(*held["mixed"], s, orders[s][0], 1 - my_bit(orders[s][0]), BF16, after)
        held[s] = swap(send, "seq", n_seq, 1 << orders[s][0])
        return send

    def sending_a(after):
        held["send"] = sending(0, after)
        return held["send"], keeping(0, held["send"])

    def sending_b(after):
        return sending(1, after)

    def behind(after):
        return [keeping(s, after) for s in (1,)], back(after), (held[0], held[1])

    long = jax.ShapeDtypeStruct((heads, 1, length), F32)
    wide = jax.ShapeDtypeStruct((length, n_state), F32)
    back = lambda after: call(
        back_kernel,
        grid,
        [by_row(block, length)] * 3
        + [by_row(block, n_state), whole(length, n_state), whole(length, n_state)]
        + [by_row(group, 1, length)] * 2
        + [ANY],
        [by_row(block, length), by_row(group, 1, length), whole(length, n_state), whole(length, n_state)],
        [jax.ShapeDtypeStruct((channels, length), F32), long, wide, wide],
        [pltpu.VMEM((length, length), BF16)] * 2 + [pltpu.VMEM((length, length), F32)],
        flops=10 * channels * length * length,
    )(x, y_cotan, inner, state_in, b, c, grown, shrunk, after)
    works, cotan_end, _ = pair_scan(
        *halves_of(local_cotan.reshape(heads, HEAD_DIM, n_state), total), total, n_seq, True,
        {0: sending_a, 1: sending_b, 2: behind},
    )
    (_, keep_a), _, ((keep_b,), (outer, from_y, grad_b, grad_c), gots) = works
    keeps = keep_a, keep_b

    def halve(sums, left):
        axis = sorted(left, reverse=True).index(left[0])
        pick = lambda value: lax.dynamic_index_in_dim(sums, value, axis, keepdims=False)
        return pick(my_bit(left[0])), pick(1 - my_bit(left[0])).astype(BF16)

    streams = []
    for s in (0, 1):
        sums = keeps[s] + gots[s].astype(F32)
        sums = sums.reshape((2,) * (n_bits - 1) + (out_columns, sizes[s]))
        streams.append(halve(sums, orders[s][1:]))
    grad_inputs, grad_dt, small, both = call(
        last_kernel,
        grid,
        [by_row(block, length)] * 3
        + [by_row(block, n_state)] * 3
        + [by_row(group, 1, length)] * 2
        + [whole(length, n_state), whole(heads, 1, length), whole(1, heads), whole(heads, 1, length)]
        + [whole(length, n_state)] * 2
        + [ANY] * 2,
        [
            by_row(block, length),
            whole(heads, 1, length),
            whole(2, heads, 128),
            whole(length, 2 * n_state),
        ],
        [
            jax.ShapeDtypeStruct((channels, length), BF16),
            long,
            jax.ShapeDtypeStruct((2, heads, 128), F32),
            jax.ShapeDtypeStruct((length, 2 * n_state), F32),
        ],
        [
            pltpu.VMEM((heads, 1, length), F32),
            pltpu.VMEM((heads, 1, n_state), F32),
            pltpu.VMEM((heads, 1, length), F32),
            pltpu.VMEM((heads, length), F32),
            pltpu.VMEM((heads, length), F32),
            pltpu.VMEM((heads, length), F32),
            pltpu.VMEM((heads, n_state), F32),
            pltpu.VMEM((heads, length), F32),
        ],
        flops=6 * channels * length * n_state,
    )(
        x, y_cotan, outer, cotan_end, gathered, state_in, shrunk, skips,
        b, dt3, alog2, from_y, grad_b, grad_c, streams[0][1], streams[1][1],
    )
    if n_tensor == 2:
        both_other = swap(both, "tensor", 2, 1)
    small = small + swap(small, "dp", 2, 1)
    for done in range(1, n_bits):
        gots = [swap(streams[s][1], "seq", n_seq, 1 << orders[s][done]) for s in (0, 1)]
        if done == 1:
            gots, both, small = lax.optimization_barrier((gots, both, small))
        if done + 1 == n_bits:
            small = lax.all_to_all(jnp.broadcast_to(small, (n_seq,) + small.shape), "seq", 0, 0)
            both = (both + both_other if n_tensor == 2 else lax.psum(both, "tensor")).astype(BF16)
            grad_b, grad_c = both[:, :n_state], both[:, n_state:]
            gots, grad_b, grad_c = lax.optimization_barrier((gots, grad_b, grad_c))
        pairs = [streams[s][0] + gots[s].astype(F32) for s in (0, 1)]
        if done + 1 < n_bits:
            streams = [halve(pairs[s], orders[s][done + 1 :]) for s in (0, 1)]
            if done + 2 == n_bits:
                small, _ = lax.optimization_barrier((small, [stream[1] for stream in streams]))
    small = jnp.sum(small[:, :, :, 0], axis=0)
    grad_w = jnp.concatenate(pairs, axis=1).T.astype(BF16)
    return (
        mixed[None],
        grad_inputs[None],
        grad_b[None],
        grad_c[None],
        grad_dt[:, 0][None],
        small[0],
        small[1],
        grad_w,
    )


def solution(mesh):
    in_specs = (
        P("dp", "tensor", "seq"),
        P("dp", "seq", None),
        P("dp", "seq", None),
        P("dp", "tensor", "seq"),
        P("tensor"),
        P("tensor"),
        P("tensor", "dp"),
        P("dp", "tensor", "seq"),
    )
    out_specs = (
        P("dp", "tensor", "seq"),
        P("dp", "tensor", "seq"),
        P("dp", "seq", None),
        P("dp", "seq", None),
        P("dp", "tensor", "seq"),
        P("tensor"),
        P("tensor"),
        P("tensor", ("seq", "dp")),
    )
    return jax.shard_map(
        functools.partial(per_device, mesh),
        mesh=mesh,
        in_specs=in_specs,
        out_specs=out_specs,
        check_vma=False,
    )
```

```python
import functools

import jax
import jax.numpy as jnp
from jax import lax
from jax.experimental import pallas as pl
from jax.experimental.pallas import tpu as pltpu
from jax.sharding import PartitionSpec as P

HEAD_DIM = 64
F32 = jnp.float32
BF16 = jnp.bfloat16
NN = (((1,), (0,)), ((), ()))
NT = (((1,), (1,)), ((), ()))
TN = (((0,), (0,)), ((), ()))
VMEM_BYTES = 16 * 1024 * 1024
COST_SCALE = 20
FIRST_VMEM_BYTES = 58 * 1024 * 1024


def dot(a, b, dims=NN):
    return lax.dot_general(a, b, dims, preferred_element_type=F32)


def split(values):
    high = values.astype(BF16)
    return high, (values - high.astype(F32)).astype(BF16)


def dot_split(a, b, dims=NN):
    return dot(a[0], b[0], dims) + dot(a[1], b[0], dims) + dot(a[0], b[1], dims)


def part(pair, index):
    return pair[0][index], pair[1][index]


def running_sum(values, reverse=False):
    length = values.shape[1]
    lane = lax.broadcasted_iota(jnp.int32, values.shape, 1)
    step = 1
    while step < length:
        if reverse:
            moved = jnp.where(lane < length - step, pltpu.roll(values, length - step, 1), 0.0)
        else:
            moved = jnp.where(lane >= step, pltpu.roll(values, step, 1), 0.0)
        values = values + moved
        step *= 2
    return values


def softplus(values):
    return jnp.maximum(values, 0.0) + jnp.log(1.0 + jnp.exp(-jnp.abs(values)))


def causal_affinity(b, c):
    affinity = dot(b, c, NT)
    source = lax.broadcasted_iota(jnp.int32, affinity.shape, 0)
    later = lax.broadcasted_iota(jnp.int32, affinity.shape, 1)
    return jnp.where(source <= later, affinity, 0.0)


def as_column(row):
    square = jnp.broadcast_to(row, (row.shape[1], row.shape[1]))
    along = lax.broadcasted_iota(jnp.int32, square.shape, 0)
    across = lax.broadcasted_iota(jnp.int32, square.shape, 1)
    return jnp.sum(jnp.where(along == across, square, 0.0), axis=1, keepdims=True)


def per_head(values, heads):
    return values.reshape(heads, HEAD_DIM, values.shape[1])


def call(kernel, grid, in_specs, out_specs, out_shape, scratch=(), flops=0, prefetch=0, vmem=VMEM_BYTES):
    return pl.pallas_call(
        kernel,
        out_shape=out_shape,
        grid_spec=pltpu.PrefetchScalarGridSpec(
            num_scalar_prefetch=prefetch,
            grid=grid,
            in_specs=in_specs,
            out_specs=out_specs,
            scratch_shapes=list(scratch),
        ),
        compiler_params=pltpu.CompilerParams(
            vmem_limit_bytes=vmem, dimension_semantics=("arbitrary",) * len(grid)
        ),
        cost_estimate=pl.CostEstimate(flops=flops * COST_SCALE, bytes_accessed=4_000_000 * COST_SCALE, transcendentals=0),
    )


def whole(*shape):
    return pl.BlockSpec(shape, lambda i, *_: (0,) * len(shape))


def by_row(*shape):
    return pl.BlockSpec(shape, lambda i, *_: (i,) + (0,) * (len(shape) - 1))


ANY = pl.BlockSpec(memory_space=pl.ANY)


def decay_kernel(upper_ref, x_hbm, b_hbm, dt_hbm, alog_hbm, grown_ref, shrunk_ref, total_ref, gathered_ref,
                 payload_ref, mine_ref, x_ref, b_ref, dt_ref, alog_ref, rows_dt, sems):
    heads, length = rows_dt.shape
    group = 4 if heads % 4 == 0 else 1
    block = group * HEAD_DIM
    parts = heads // group
    pieces = [(dt_hbm, dt_ref), (alog_hbm, alog_ref), (b_hbm, b_ref)]
    for i in range(parts):
        here = pl.ds(i * block, block)
        pieces.append((x_hbm.at[here], x_ref.at[here]))
    copies = [pltpu.make_async_copy(src, dst, sems.at[i]) for i, (src, dst) in enumerate(pieces)]
    for copy in copies:
        copy.start()
    copies[0].wait()
    copies[1].wait()
    for h in range(heads):
        rows_dt[h : h + 1] = dt_ref[h]
    step_size = softplus(rows_dt[...])
    cumulative = running_sum(step_size * -jnp.exp(as_column(alog_ref[...])))
    grown = jnp.exp(cumulative)
    shrunk = step_size * jnp.exp(-cumulative)
    for h in range(heads):
        grown_ref[h] = grown[h : h + 1]
        shrunk_ref[h] = shrunk[h : h + 1]
    total = jnp.broadcast_to(cumulative[:, length - 1 :], total_ref.shape)
    total_ref[...] = total
    along = lax.broadcasted_iota(jnp.int32, total.shape, 0)
    across = lax.broadcasted_iota(jnp.int32, total.shape, 1)
    row = jnp.sum(jnp.where(along == across, total, 0.0), axis=0, keepdims=True)
    high, low = split(row)
    middle, low = split(row - high.astype(F32))
    rows = lax.broadcasted_iota(jnp.int32, payload_ref.shape[1:], 0)
    terms = jnp.where(rows == 0, high.astype(F32), jnp.where(rows == 1, middle.astype(F32), low.astype(F32)))
    payload_ref[heads] = jnp.where(rows < 3, terms, 0.0).astype(BF16)
    upper = upper_ref[0] == 1
    copies[2].wait()
    for i in range(parts):
        copies[3 + i].wait()
        x = per_head(x_ref[i * block : (i + 1) * block].astype(F32), group)
        high, low = split((x * shrunk_ref[i * group : (i + 1) * group]).reshape(block, length))
        gathered = dot(high, b_ref[...]) + dot(low, b_ref[...])
        gathered_ref[i * block : (i + 1) * block] = gathered
        for j in range(group):
            h = i * group + j
            local = gathered[j * HEAD_DIM : (j + 1) * HEAD_DIM] * jnp.exp(total[h : h + 1])
            first, second = local[: HEAD_DIM // 2], local[HEAD_DIM // 2 :]
            mine_ref[h] = jnp.where(upper, second, first)
            payload_ref[h] = jnp.where(upper, first, second).astype(BF16)


def inner_kernel(x_ref, b_ref, c_ref, shrunk_ref, skip_ref, after_ref, inner_ref, skips_ref, high_ref, low_ref):
    group = x_ref.shape[0] // HEAD_DIM
    half = x_ref.shape[1] // 2

    @pl.when(pl.program_id(0) == 0)
    def _():
        high_ref[...], low_ref[...] = split(causal_affinity(b_ref[...], c_ref[...]))
        skips = jnp.broadcast_to(as_column(skip_ref[...]), (skips_ref.shape[0], skips_ref.shape[2]))
        for h in range(skips_ref.shape[0]):
            skips_ref[h] = skips[h : h + 1]

    xs = split((per_head(x_ref[...].astype(F32), group) * shrunk_ref[...]).reshape(x_ref.shape))
    affinity = (high_ref, low_ref)
    early = (slice(None), slice(0, half))
    late = (slice(None), slice(half, None))
    corner = (slice(0, half), slice(0, half))
    inner_ref[:, :half] = dot_split(part(xs, early), part(affinity, corner))
    inner_ref[:, half:] = dot_split(xs, part(affinity, late))


def mixed_kernel(inner_ref, state_ref, c_ref, x_ref, grown_ref, skips_ref, after_ref, mixed_ref):
    group = x_ref.shape[0] // HEAD_DIM
    inner = per_head(inner_ref[...] + dot(state_ref[...], c_ref[...], NT), group)
    x = per_head(x_ref[...].astype(F32), group)
    mixed = grown_ref[...] * inner + skips_ref[...] * x
    mixed_ref[...] = mixed.reshape(x_ref.shape).astype(BF16)


def cotan_first_kernel(flag_ref, mine_ref, other_ref, g_ref, after_ref, out_ref, later_ref):
    @pl.when(flag_ref[0] == 1)
    def _():
        out_ref[...] = dot(mine_ref[...], g_ref[...])
        later_ref[...] = other_ref[...]

    @pl.when(flag_ref[0] == 0)
    def _():
        out_ref[...] = dot(other_ref[...], g_ref[...])
        later_ref[...] = mine_ref[...]


def cotan_kernel(weights_ref, g_ref, first_ref, c_ref, grown_ref, after_ref, cotan_ref, local_ref, sum_ref):
    sum_ref[...] = first_ref[...] + dot(weights_ref[...], g_ref[...])
    cotan = sum_ref[...].astype(BF16)
    cotan_ref[...] = cotan
    group = cotan.shape[0] // HEAD_DIM
    gs = (per_head(cotan.astype(F32), group) * grown_ref[...]).reshape(cotan.shape)
    high, low = split(gs)
    local_ref[...] = dot(high, c_ref[...]) + dot(low, c_ref[...])


def terms_kernel(pick_ref, g0_ref, g1_ref, m0_ref, m1_ref, after_ref, out_ref):
    high, _, low, columns, length = g0_ref.shape
    if columns % 16 == 0:
        flat = lambda ref: ref[...].reshape(high * low * columns, length)
        product = dot(flat(g0_ref), m0_ref[...], NT) + dot(flat(g1_ref), m1_ref[...], NT)
        out_ref[...] = product.reshape(out_ref.shape).astype(out_ref.dtype)
    else:
        for i in range(high):
            for j in range(low):
                product = dot(g0_ref[i, 0, j], m0_ref[...], NT) + dot(g1_ref[i, 0, j], m1_ref[...], NT)
                out_ref[i * low + j] = product.astype(out_ref.dtype)


def halve_kernel(pick_ref, sums_ref, kept_ref, sent_ref):
    mine = pick_ref[0]
    sent_ref[...] = sums_ref[1 - mine].astype(BF16)
    kept_ref[...] = sums_ref[mine]


def back_kernel(x_ref, cotan_ref, inner_ref, state_ref, b_ref, c_ref, grown_ref, shrunk_ref, after_ref,
                outer_ref, from_y_ref, grad_b_ref, grad_c_ref, high_ref, low_ref, across_ref):
    step = pl.program_id(0)
    group = x_ref.shape[0] // HEAD_DIM
    half = x_ref.shape[1] // 2

    @pl.when(step == 0)
    def _():
        high_ref[...], low_ref[...] = split(causal_affinity(b_ref[...], c_ref[...]))
        across_ref[...] = jnp.zeros_like(across_ref)
        grad_c_ref[...] = jnp.zeros_like(grad_c_ref)

    x = per_head(x_ref[...].astype(F32), group)
    xs = split((x * shrunk_ref[...]).reshape(x_ref.shape))
    gs_full = (per_head(cotan_ref[...].astype(F32), group) * grown_ref[...]).reshape(x_ref.shape)
    gs = split(gs_full)
    affinity = (high_ref, low_ref)
    late = (slice(None), slice(half, None))
    early = (slice(None), slice(0, half))
    top = (slice(0, half), slice(None))
    corner = (slice(half, None), slice(half, None))
    outer_ref[:, :half] = dot_split(gs, part(affinity, top), NT)
    outer_ref[:, half:] = dot_split(part(gs, late), part(affinity, corner), NT)
    across_ref[:half] += dot_split(part(xs, early), gs, TN)
    across_ref[half:, half:] += dot_split(part(xs, late), part(gs, late), TN)
    state = state_ref[...]
    grad_c_ref[...] += dot(gs[0], state, TN) + dot(gs[1], state, TN)
    inner = inner_ref[...] + dot(state, c_ref[...], NT)
    from_y_ref[...] = jnp.sum(per_head(gs_full * inner, group), axis=1, keepdims=True)

    @pl.when(step == pl.num_programs(0) - 1)
    def _():
        across = across_ref[...]
        source = lax.broadcasted_iota(jnp.int32, across.shape, 0)
        later = lax.broadcasted_iota(jnp.int32, across.shape, 1)
        high, low = split(jnp.where(source <= later, across, 0.0))
        grad_b_ref[...] = dot(high, c_ref[...]) + dot(low, c_ref[...])
        grad_c_ref[...] += dot(high, b_ref[...], TN) + dot(low, b_ref[...], TN)


def last_kernel(x_ref, cotan_ref, outer_ref, ends_ref, gathered_ref, state_ref, shrunk_ref, skips_ref,
                b_ref, dt_ref, alog_ref, from_y_ref, grad_b_ref, grad_c_ref, after_a_ref, after_b_ref,
                grad_inputs_ref, grad_dt_ref, small_ref, both_ref,
                from_x_s, from_end_s, from_skip_s, rows_x, rows_y, rows_skip, rows_end, rows_dt):
    step = pl.program_id(0)
    group = x_ref.shape[0] // HEAD_DIM
    heads, length = rows_x.shape
    n_state = b_ref.shape[1]
    ends = ends_ref[...]
    outer = per_head(outer_ref[...] + dot(ends, b_ref[...], NT), group)
    x = per_head(x_ref[...].astype(F32), group)
    cotan = per_head(cotan_ref[...].astype(F32), group)
    xs = x * shrunk_ref[...]
    grad_inputs = shrunk_ref[...] * outer + skips_ref[...] * cotan
    grad_inputs_ref[...] = grad_inputs.reshape(x_ref.shape).astype(BF16)
    here = pl.ds(step * group, group)
    from_x_s[here] = jnp.sum(xs * outer, axis=1, keepdims=True)
    from_skip_s[here] = jnp.sum(x * cotan, axis=1, keepdims=True)
    moved = ends.astype(F32) * (gathered_ref[...] + state_ref[...].astype(F32))
    from_end_s[here] = jnp.sum(per_head(moved, group), axis=1, keepdims=True)
    high, low = split(xs.reshape(x_ref.shape))

    @pl.when(step == 0)
    def _():
        both_ref[:, :n_state] = grad_b_ref[...]
        both_ref[:, n_state:] = grad_c_ref[...]

    both_ref[:, :n_state] += dot(high, ends, TN) + dot(low, ends, TN)

    @pl.when(step == pl.num_programs(0) - 1)
    def _():
        for h in range(heads):
            rows_x[h : h + 1] = from_x_s[h]
            rows_y[h : h + 1] = from_y_ref[h]
            rows_skip[h : h + 1] = from_skip_s[h]
            rows_end[h : h + 1] = from_end_s[h]
            rows_dt[h : h + 1] = dt_ref[h]
        from_x = rows_x[...]
        from_end = jnp.sum(rows_end[...], axis=1, keepdims=True)
        flow = running_sum(rows_y[...] - from_x, reverse=True) + from_end
        dt = rows_dt[...]
        step_size = softplus(dt)
        rate = -jnp.exp(as_column(alog_ref[...]))
        grad_dt = (from_x / step_size + flow * rate) / (1.0 + jnp.exp(-dt))
        for h in range(heads):
            grad_dt_ref[h] = grad_dt[h : h + 1]
        alog = jnp.sum(flow * step_size * rate, axis=1, keepdims=True)
        skip = jnp.sum(rows_skip[...], axis=1, keepdims=True)
        small_ref[0] = jnp.broadcast_to(alog, small_ref.shape[1:])
        small_ref[1] = jnp.broadcast_to(skip, small_ref.shape[1:])


def swap(value, axis, size, bit):
    return lax.ppermute(value, axis, [(i, i ^ bit) for i in range(size)])


def shifted(value, axis, size, step):
    pairs = [(i, i + step) for i in range(size) if 0 <= i + step < size]
    return lax.ppermute(value, axis, pairs)


def pack(state, total):
    heads, rows, lanes = state.shape
    high = lax.reduce_precision(total, 8, 7)
    middle = lax.reduce_precision(total - high, 8, 7)
    low = total - high - middle
    terms = jnp.stack([high, middle, low]).astype(BF16)
    extra = jnp.pad(terms, ((0, rows - 3), (0, lanes - heads)))
    return jnp.concatenate([state.astype(BF16), extra[None]], axis=0)


def unpack(payload):
    heads = payload.shape[0] - 1
    terms = payload[heads, :3, :heads].astype(F32)
    return payload[:heads].astype(F32), terms[0] + terms[1] + terms[2]


def decay(total):
    return jnp.exp(total)[:, None, None]


def halves_of(local, total):
    heads, width, lanes = local.shape
    upper = lax.rem(lax.axis_index("seq"), 2) == 1
    halves = local.reshape(heads, 2, width // 2, lanes)
    mine = jnp.where(upper, halves[:, 1], halves[:, 0])
    theirs = jnp.where(upper, halves[:, 0], halves[:, 1])
    return pack(theirs, total), mine


def pair_scan(payload, mine, total, n_seq, reverse, beside):
    heads, half_width, lanes = mine.shape
    upper = lax.rem(lax.axis_index("seq"), 2) == 1
    late = jnp.logical_not(upper) if reverse else upper
    works, taken = [], []

    def traveling(payload, got):
        if len(taken) in beside:
            work = beside[len(taken)](payload)
            got, work = lax.optimization_barrier((got, work))
            works.append(work)
        taken.append(payload)
        return got

    other, other_total = unpack(traveling(payload, swap(payload, "seq", n_seq, 1)))
    first = jnp.where(late, other, mine)
    second = jnp.where(late, mine, other)
    first_total = jnp.where(late, other_total, total)
    second_total = jnp.where(late, total, other_total)
    span = decay(second_total) * first + second
    span_total = first_total + second_total
    before, before_total = jnp.zeros_like(span), jnp.zeros_like(span_total)
    step = 2
    while step < n_seq:
        payload = pack(span, span_total)
        moved = shifted(payload, "seq", n_seq, -step if reverse else step)
        earlier, earlier_total = unpack(traveling(payload, moved))
        before = decay(before_total) * earlier + before
        span = decay(span_total) * earlier + span
        before_total = before_total + earlier_total
        span_total = span_total + earlier_total
        step *= 2
    for_first = before
    for_second = decay(first_total) * before + first
    if reverse:
        for_first = decay(first_total) * for_first
        for_second = decay(second_total) * for_second
    keep = jnp.where(late, for_second, for_first).astype(BF16)
    give = jnp.where(late, for_first, for_second).astype(BF16)
    got = swap(give, "seq", n_seq, 1)
    low = jnp.where(upper, got, keep)
    high = jnp.where(upper, keep, got)
    result = jnp.concatenate([low[:, None], high[:, None]], axis=1).reshape(heads * 2 * half_width, lanes)
    return works, result, give


def per_device(mesh, head_inputs, b_proj, c_proj, dt_raw, a_log, d_skip, w_out, out_grad):
    n_seq, n_dp, n_tensor = mesh.shape["seq"], mesh.shape["dp"], mesh.shape["tensor"]
    x, b, c, dt, g = head_inputs[0], b_proj[0], c_proj[0], dt_raw[0], out_grad[0]
    heads, length = dt.shape
    channels = heads * HEAD_DIM
    n_state = b.shape[1]
    features = g.shape[0] * n_tensor
    out_columns = features // (n_seq * n_dp)
    my_dp, my_tensor, my_seq = (lax.axis_index(a) for a in ("dp", "tensor", "seq"))
    group = 4 if heads % 4 == 0 else 1
    block = group * HEAD_DIM
    grid = (heads // group,)
    alog2, skip2, dt3 = a_log[None], d_skip[None], dt[:, None]

    if n_tensor == 2:
        g_first, half_index = g, my_tensor
        g_second = swap(g, "tensor", 2, 1)
    else:
        g_all = lax.all_gather(g, "tensor", axis=0, tiled=True)
        g_first, g_second, half_index = g_all[: features // 2], g_all[features // 2 :], 0

    long = jax.ShapeDtypeStruct((heads, 1, length), F32)
    upper = lax.rem(my_seq, 2).astype(jnp.int32).reshape(1)
    half_state = (HEAD_DIM // 2, n_state)
    grown, shrunk, totals, gathered, payload, mine = call(
        decay_kernel,
        (1,),
        [ANY] * 4,
        [whole(heads, 1, length)] * 2
        + [whole(heads, 128), whole(channels, n_state), whole(heads + 1, *half_state), whole(heads, *half_state)],
        [long] * 2
        + [jax.ShapeDtypeStruct((heads, 128), F32), jax.ShapeDtypeStruct((channels, n_state), F32)]
        + [jax.ShapeDtypeStruct((heads + 1, *half_state), BF16), jax.ShapeDtypeStruct((heads, *half_state), F32)],
        [
            pltpu.VMEM((channels, length), BF16),
            pltpu.VMEM((length, n_state), BF16),
            pltpu.VMEM((heads, 1, length), F32),
            pltpu.VMEM((1, heads), F32),
            pltpu.VMEM((heads, length), F32),
            pltpu.SemaphoreType.DMA((3 + heads // group,)),
        ],
        flops=4 * channels * length * n_state,
        vmem=FIRST_VMEM_BYTES,
        prefetch=1,
    )(upper, x, b, dt3, alog2)
    total = totals[:, 0]

    inners = lambda after: call(
        inner_kernel,
        grid,
        [by_row(block, length), whole(length, n_state), whole(length, n_state), by_row(group, 1, length), whole(1, heads), ANY],
        [by_row(block, length), whole(heads, 1, length)],
        [jax.ShapeDtypeStruct((channels, length), F32), long],
        [pltpu.VMEM((length, length), BF16)] * 2,
        flops=5 * channels * length * length,
    )(x, b, c, shrunk, skip2, after)

    w_other = swap(w_out, "dp", 2, 1)
    flag = (my_dp == half_index).astype(jnp.int32).reshape(1)
    half_features = features // 2
    wide_group = heads // 2 if heads % 2 == 0 else 1
    wide_block = wide_group * HEAD_DIM
    wide_grid = (heads // wide_group,)

    first = lambda after: call(
        cotan_first_kernel,
        wide_grid,
        [by_row(wide_block, half_features)] * 2 + [whole(half_features, length), ANY],
        [by_row(wide_block, length), by_row(wide_block, half_features)],
        [jax.ShapeDtypeStruct((channels, length), F32), jax.ShapeDtypeStruct((channels, half_features), BF16)],
        flops=2 * channels * half_features * length,
        prefetch=1,
    )(flag, w_out, w_other, g_first, after)
    cotans = lambda g_second, first, later, after: call(
        cotan_kernel,
        wide_grid,
        [by_row(wide_block, half_features)]
        + [whole(half_features, length), by_row(wide_block, length), whole(length, n_state), by_row(wide_group, 1, length), ANY],
        [by_row(wide_block, length), by_row(wide_block, n_state)],
        [jax.ShapeDtypeStruct((channels, length), BF16), jax.ShapeDtypeStruct((channels, n_state), F32)],
        [pltpu.VMEM((wide_block, length), F32)],
        flops=2 * channels * length * (half_features + 2 * n_state),
    )(later, g_second, first, c, grown, after)

    beside = {1: first}
    ((first_sum, later),), state_in, give = pair_scan(payload, mine, total, n_seq, False, beside)

    inner, skips = inners(give)

    def mix(after):
        return call(
            mixed_kernel,
            grid,
            [by_row(block, length), by_row(block, n_state), whole(length, n_state), by_row(block, length)]
            + [by_row(group, 1, length)] * 2
            + [ANY],
            by_row(block, length),
            jax.ShapeDtypeStruct((channels, length), BF16),
            flops=2 * channels * length * n_state,
        )(inner, state_in, c, x, grown, skips, after)

    n_bits = n_seq.bit_length() - 1
    unit = channels // 5 if channels % 640 == 0 else channels // 2
    sizes = (3 * unit, 2 * unit) if channels % 640 == 0 else (unit, unit)

    def my_bit(bit):
        value = jnp.bitwise_and(my_seq >> bit, 1)
        return value ^ half_index if bit == n_bits - 1 else value

    def terms(mixed, mixed_other, stream, bit, value, dtype, after):
        low = 1 << bit
        high = n_seq // (2 * low)
        offset = sizes[0] // unit if stream else 0
        rows = pl.BlockSpec((unit, length), lambda i, pick: (offset + i, 0))
        columns = pl.BlockSpec(
            (high, 1, low, out_columns, length), lambda i, pick: (0, pick[0], 0, 0, 0)
        )
        split_blocks = lambda blocks: blocks.reshape(high, 2, low, out_columns, length)
        return call(
            terms_kernel,
            (sizes[stream] // unit,),
            [columns, columns, rows, rows, ANY],
            pl.BlockSpec((n_seq // 2, out_columns, unit), lambda i, pick: (0, 0, i)),
            jax.ShapeDtypeStruct((n_seq // 2, out_columns, sizes[stream]), dtype),
            flops=n_seq * out_columns * sizes[stream] * 2 * length,
            prefetch=1,
        )(
            value.astype(jnp.int32).reshape(1),
            split_blocks(g_mine), split_blocks(g_other), mixed, mixed_other, after,
        )

    orders = [list(range(n_bits)), [1, 0] + list(range(2, n_bits))]
    held = {}

    mixed = mix(give)
    held["mixed"] = mixed, swap(mixed, "dp", 2, 1)
    if n_tensor == 2:
        g_second, _ = lax.optimization_barrier((g_second, mixed))
    firsts = g_first.reshape(n_seq // 2, n_dp, out_columns, length)
    seconds = g_second.reshape(n_seq // 2, n_dp, out_columns, length)

    def chosen(place):
        pick = lambda blocks: lax.dynamic_index_in_dim(blocks, place, 1, keepdims=False)
        return jnp.concatenate([pick(firsts), pick(seconds)])

    g_mine = chosen(my_dp)
    g_other = swap(chosen(1 - my_dp), "dp", 2, 1)
    y_cotan, local_cotan = cotans(g_second, first_sum, later, mixed)

    def keeping(s, after):
        return terms(*held["mixed"], s, orders[s][0], my_bit(orders[s][0]), F32, after)

    def sending(s, after):
        send = terms(*held["mixed"], s, orders[s][0], 1 - my_bit(orders[s][0]), BF16, after)
        held[s] = swap(send, "seq", n_seq, 1 << orders[s][0])
        return send

    def sending_a(after):
        held["send"] = sending(0, after)
        return held["send"], keeping(0, held["send"])

    def sending_b(after):
        return sending(1, after)

    def behind(after):
        return [keeping(s, after) for s in (1,)], back(after), (held[0], held[1])

    long = jax.ShapeDtypeStruct((heads, 1, length), F32)
    wide = jax.ShapeDtypeStruct((length, n_state), F32)
    back = lambda after: call(
        back_kernel,
        grid,
        [by_row(block, length)] * 3
        + [by_row(block, n_state), whole(length, n_state), whole(length, n_state)]
        + [by_row(group, 1, length)] * 2
        + [ANY],
        [by_row(block, length), by_row(group, 1, length), whole(length, n_state), whole(length, n_state)],
        [jax.ShapeDtypeStruct((channels, length), F32), long, wide, wide],
        [pltpu.VMEM((length, length), BF16)] * 2 + [pltpu.VMEM((length, length), F32)],
        flops=10 * channels * length * length,
    )(x, y_cotan, inner, state_in, b, c, grown, shrunk, after)
    works, cotan_end, _ = pair_scan(
        *halves_of(local_cotan.reshape(heads, HEAD_DIM, n_state), total), total, n_seq, True,
        {0: sending_a, 1: sending_b, 2: behind},
    )
    (_, keep_a), _, ((keep_b,), (outer, from_y, grad_b, grad_c), gots) = works
    keeps = keep_a, keep_b

    def halve(sums, left):
        axis = sorted(left, reverse=True).index(left[0])
        pick = lambda value: lax.dynamic_index_in_dim(sums, value, axis, keepdims=False)
        return pick(my_bit(left[0])), pick(1 - my_bit(left[0])).astype(BF16)

    streams = []
    for s in (0, 1):
        sums = keeps[s] + gots[s].astype(F32)
        sums = sums.reshape((2,) * (n_bits - 1) + (out_columns, sizes[s]))
        streams.append(halve(sums, orders[s][1:]))
    grad_inputs, grad_dt, small, both = call(
        last_kernel,
        grid,
        [by_row(block, length)] * 3
        + [by_row(block, n_state)] * 3
        + [by_row(group, 1, length)] * 2
        + [whole(length, n_state), whole(heads, 1, length), whole(1, heads), whole(heads, 1, length)]
        + [whole(length, n_state)] * 2
        + [ANY] * 2,
        [
            by_row(block, length),
            whole(heads, 1, length),
            whole(2, heads, 128),
            whole(length, 2 * n_state),
        ],
        [
            jax.ShapeDtypeStruct((channels, length), BF16),
            long,
            jax.ShapeDtypeStruct((2, heads, 128), F32),
            jax.ShapeDtypeStruct((length, 2 * n_state), F32),
        ],
        [
            pltpu.VMEM((heads, 1, length), F32),
            pltpu.VMEM((heads, 1, n_state), F32),
            pltpu.VMEM((heads, 1, length), F32),
            pltpu.VMEM((heads, length), F32),
            pltpu.VMEM((heads, length), F32),
            pltpu.VMEM((heads, length), F32),
            pltpu.VMEM((heads, n_state), F32),
            pltpu.VMEM((heads, length), F32),
        ],
        flops=6 * channels * length * n_state,
    )(
        x, y_cotan, outer, cotan_end, gathered, state_in, shrunk, skips,
        b, dt3, alog2, from_y, grad_b, grad_c, streams[0][1], streams[1][1],
    )
    if n_tensor == 2:
        both_other = swap(both, "tensor", 2, 1)
    small = small + swap(small, "dp", 2, 1)
    for done in range(1, n_bits):
        gots = [swap(streams[s][1], "seq", n_seq, 1 << orders[s][done]) for s in (0, 1)]
        if done == 1:
            gots, both, small = lax.optimization_barrier((gots, both, small))
        if done + 1 == n_bits:
            small = lax.all_to_all(jnp.broadcast_to(small, (n_seq,) + small.shape), "seq", 0, 0)
            both = (both + both_other if n_tensor == 2 else lax.psum(both, "tensor")).astype(BF16)
            grad_b, grad_c = both[:, :n_state], both[:, n_state:]
            gots, grad_b, grad_c = lax.optimization_barrier((gots, grad_b, grad_c))
        pairs = [streams[s][0] + gots[s].astype(F32) for s in (0, 1)]
        if done + 1 < n_bits:
            streams = [halve(pairs[s], orders[s][done + 1 :]) for s in (0, 1)]
            if done + 2 == n_bits:
                value = my_bit(n_bits - 1).astype(jnp.int32).reshape(1)
                streams = [
                    call(
                        halve_kernel,
                        (1,),
                        [whole(2, out_columns, sizes[s])],
                        [whole(out_columns, sizes[s])] * 2,
                        [jax.ShapeDtypeStruct((out_columns, sizes[s]), kind) for kind in (F32, BF16)],
                        prefetch=1,
                    )(value, pairs[s].reshape(2, out_columns, sizes[s]))
                    for s in (0, 1)
                ]
            if done + 2 == n_bits:
                small, _ = lax.optimization_barrier((small, [stream[1] for stream in streams]))
    small = jnp.sum(small[:, :, :, 0], axis=0)
    grad_w = jnp.concatenate(pairs, axis=1).T.astype(BF16)
    return (
        mixed[None],
        grad_inputs[None],
        grad_b[None],
        grad_c[None],
        grad_dt[:, 0][None],
        small[0],
        small[1],
        grad_w,
    )


def solution(mesh):
    in_specs = (
        P("dp", "tensor", "seq"),
        P("dp", "seq", None),
        P("dp", "seq", None),
        P("dp", "tensor", "seq"),
        P("tensor"),
        P("tensor"),
        P("tensor", "dp"),
        P("dp", "tensor", "seq"),
    )
    out_specs = (
        P("dp", "tensor", "seq"),
        P("dp", "tensor", "seq"),
        P("dp", "seq", None),
        P("dp", "seq", None),
        P("dp", "tensor", "seq"),
        P("tensor"),
        P("tensor"),
        P("tensor", ("seq", "dp")),
    )
    return jax.shard_map(
        functools.partial(per_device, mesh),
        mesh=mesh,
        in_specs=in_specs,
        out_specs=out_specs,
        check_vma=False,
    )
```
